32 devices in a mesh: gx: 4 (over y, core), gy: 4 (over z), gz: 2 (over x).
Axes of the slice: x: 2, y: 2, z: 4, core: 2. Of those that a mesh axis runs over, the one named last changes fastest.
Arguments:
- particles: float32 [26, 16384], P(None, ('gx', 'gy', 'gz')), may hold values from -4 to 4, as said below
- block_ids: int32 [16384], P(('gx', 'gy', 'gz')), may hold values from 0 to 7
- node_offsets: int32 [16384], P(('gx', 'gy', 'gz')), may hold values from 0 to 511
- live_count: int32 [32], P(('gx', 'gy', 'gz')), may hold values from 64 to 512, as said below
- migrations: int32 [6, 256], P(None, ('gx', 'gy', 'gz')), may hold values from 0 to 511, as said below
Outputs:
- moved_records: float32 [26, 16384], P(None, ('gx', 'gy', 'gz'))
The draws below stay inside these ranges and needn't reach their ends.
Inputs may be any that keep to these rules, and one draw needn't show every extreme that they name: `live_count`: slots below a domain's count are live; some domain is full and some holds exactly 64. `migrations`: the 48 entries of one domain are distinct slots, each live in that domain. `particles`: entries of F lie within 0.15 of the identity's; positions within a cell between -0.5 and 0.5; masses between 0.5 and 2; plastic ratios between 0.9 and 1.1.
All inputs are finite; a program needn't handle non-finite values.
Results may differ from the reference program's by a relative error of at most 0.0003.
Values sent between devices are 32-bit elements; how exact they have to be, the bound alone decides.
A program may use at most 64 MiB of HBM per device.

```python
import math
import jax
import jax.numpy as jnp
import numpy as np
from jax import lax

BLK = 2
P_DEV = 512
CAP = 8
PARTICLES = 16384
N_GX = 4
N_GY = 4
N_GZ = 2
DEVICES = 32


def migration_plan(key):
    key_count, key_jitter, key_full, key_score = jax.random.split(jax.random.fold_in(key, 11), 4)
    levels = jax.random.randint(key_count, (DEVICES,), 0, 4)
    jitter = jax.random.randint(key_jitter, (DEVICES,), 0, P_DEV // 16 + 1)
    counts = jnp.minimum(P_DEV // jnp.left_shift(jnp.int32(1), levels) + jitter, P_DEV)
    fullest = jax.random.randint(key_full, (), 0, DEVICES)
    device_index = jnp.arange(DEVICES, dtype=jnp.int32)
    counts = jnp.where(device_index == fullest, P_DEV, counts)
    counts = jnp.where(device_index == (fullest + 1) % DEVICES, P_DEV // 8, counts).astype(jnp.int32)
    slot_index = jnp.arange(P_DEV, dtype=jnp.int32)
    scores = jax.random.randint(key_score, (DEVICES, P_DEV), 0, 1 << 14) * P_DEV + slot_index[None, :] + 1
    scores = jnp.where(slot_index[None, :] < counts[:, None], scores, scores + (1 << 30))
    forced = (device_index[:, None] == fullest) & ((slot_index[None, :] == 0) | (slot_index[None, :] == P_DEV - 1))
    scores = jnp.where(forced, 0, scores)
    ranking = jnp.argsort(scores, axis=1, stable=True)[:, :6 * CAP].astype(jnp.int32)
    plan_table = ranking.reshape(DEVICES, 6, CAP).transpose(1, 0, 2).reshape(6, DEVICES * CAP)
    return (counts, plan_table)


def draw_live_count(key, part):
    return migration_plan(key)[0]


def draw_migrations(key, part):
    return migration_plan(key)[1]


def draw_particles(key, part):
    subkeys = jax.random.split(jax.random.fold_in(key, 5), 6)
    velocity = jnp.clip(jax.random.normal(subkeys[0], (3, PARTICLES)), -4.0, 4.0)
    affine = jnp.clip(0.6 * jax.random.normal(subkeys[1], (9, PARTICLES)), -3.0, 3.0)
    deform = jnp.eye(3, dtype=jnp.float32).reshape(9, 1) + jax.random.uniform(subkeys[2], (9, PARTICLES), minval=-0.15, maxval=0.15)
    fraction = jax.random.uniform(subkeys[3], (3, PARTICLES), minval=-0.5, maxval=0.5)
    particle_mass = jnp.exp(jax.random.uniform(subkeys[4], (1, PARTICLES), minval=math.log(0.5), maxval=math.log(2.0)))
    plastic = jax.random.uniform(subkeys[5], (1, PARTICLES), minval=0.9, maxval=1.1)
    return jnp.concatenate([velocity, affine, deform, fraction, particle_mass, plastic]).astype(jnp.float32)


def plant(drawn, rng, smallest, top_value):
    index_at = [jax.random.randint(jax.random.fold_in(rng, axis), (), 0, length) for axis, length in enumerate(drawn.shape)]
    longest = drawn.shape.index(max(drawn.shape))
    next_to = index_at[:longest] + [(index_at[longest] + 1) % drawn.shape[longest]] + index_at[longest + 1:]
    return drawn.at[tuple(index_at)].set(smallest).at[tuple(next_to)].set(top_value)


def cumulative_ranks(number_of, skew):
    weights = [(1 << 20) // math.isqrt(rank ** skew) + 1 for rank in range(1, number_of + 1)]
    spread = 1 + sum(weights) // (1 << 30)
    return np.cumsum(np.array([max(1, weight // spread) for weight in weights]))


def ranked_ids(rng, extent, count, lean):
    table = cumulative_ranks(count, lean)
    lot = jax.random.randint(jax.random.fold_in(rng, 1), extent, 0, int(table[count - 1]))
    standing = jnp.searchsorted(jnp.asarray(table, jnp.int32), lot, side="right")
    return jax.random.permutation(jax.random.fold_in(rng, 2), count)[standing].astype(jnp.int32)


def setup_inputs(seed: int = 0) -> dict:
    key_list = jax.random.split(jax.random.key(seed), 6)
    particles = draw_particles(jax.random.fold_in(key_list[5], 71), 0)
    block_ids = plant(ranked_ids(key_list[1], (PARTICLES,), BLK ** 3, 2), jax.random.fold_in(key_list[1], 3), 0, (BLK ** 3) - 1).astype(jnp.int32)
    node_offsets = plant(jax.random.randint(key_list[2], (PARTICLES,), 0, 512), jax.random.fold_in(key_list[2], 1), 0, 511).astype(jnp.int32)
    live_count = draw_live_count(jax.random.fold_in(key_list[5], 71), 0)
    migrations = draw_migrations(jax.random.fold_in(key_list[5], 71), 0)
    return dict(particles=particles, block_ids=block_ids, node_offsets=node_offsets, live_count=live_count, migrations=migrations)


time_step = 0.05
stress_gain = 0.2
shear_zero = 5.0
bulk_zero = 5.0
harden_rate = 10.0
mass_floor = 0.1
gravity = 9.8


def matrix_product(left_side, right_side):
    rows_out = []
    for row_id in range(3):
        entries = []
        for col_id in range(3):
            entries.append(left_side[row_id, 0] * right_side[0, col_id] + left_side[row_id, 1] * right_side[1, col_id] + left_side[row_id, 2] * right_side[2, col_id])
        rows_out.append(jnp.stack(entries))
    return jnp.stack(rows_out)


def matrix_vector(matrix, vector):
    return jnp.stack([matrix[row_id, 0] * vector[0] + matrix[row_id, 1] * vector[1] + matrix[row_id, 2] * vector[2] for row_id in range(3)])


def matrix_transpose(matrix):
    return jnp.transpose(matrix, (1, 0, 2))


def determinant(matrix):
    return (matrix[0, 0] * (matrix[1, 1] * matrix[2, 2] - matrix[1, 2] * matrix[2, 1])
            - matrix[0, 1] * (matrix[1, 0] * matrix[2, 2] - matrix[1, 2] * matrix[2, 0])
            + matrix[0, 2] * (matrix[1, 0] * matrix[2, 1] - matrix[1, 1] * matrix[2, 0]))


def kirchhoff(deform, plastic):
    identity = jnp.eye(3, dtype=deform.dtype)[:, :, None]
    rotation = deform
    for iteration in range(5):
        rotation = 0.5 * matrix_product(rotation, 3.0 * identity - matrix_product(matrix_transpose(rotation), rotation))
    volume = determinant(deform)
    harden = jnp.exp(harden_rate * (1.0 - plastic))
    shear_mod = shear_zero * harden
    bulk_mod = bulk_zero * harden
    return 2.0 * shear_mod * matrix_product(deform - rotation, matrix_transpose(deform)) + (bulk_mod * (volume - 1.0) * volume) * identity


def spline_weights(fraction):
    return jnp.stack([0.5 * (0.5 - fraction) ** 2, 0.75 - fraction * fraction, 0.5 * (0.5 + fraction) ** 2])


def anchor_nodes(block_ids, node_offsets, blocks):
    corner = jnp.stack([block_ids // (blocks * blocks), (block_ids // blocks) % blocks, block_ids % blocks])
    inside = jnp.stack([node_offsets // 64, (node_offsets // 8) % 8, node_offsets % 8])
    return 8 * corner + inside + 8


def stencil_point(fraction, anchor, weights_axis, padded, stencil_id):
    delta_node = (stencil_id // 9 - 1, (stencil_id // 3) % 3 - 1, stencil_id % 3 - 1)
    weight = weights_axis[delta_node[0] + 1, 0] * weights_axis[delta_node[1] + 1, 1] * weights_axis[delta_node[2] + 1, 2]
    displace = jnp.stack([delta_node[axis_id] - fraction[axis_id] for axis_id in range(3)])
    node_pos = [anchor[axis_id] + delta_node[axis_id] for axis_id in range(3)]
    block_flat = ((node_pos[0] // 8) * padded + node_pos[1] // 8) * padded + node_pos[2] // 8
    flat_index = block_flat * 512 + (node_pos[0] % 8) * 64 + (node_pos[1] % 8) * 8 + node_pos[2] % 8
    return flat_index, weight, displace


def scatter_grid(particles, block_ids, node_offsets, living, blocks):
    padded = blocks + 2
    fraction = particles[21:24]
    affine = particles[3:12].reshape(3, 3, -1)
    deform = particles[12:21].reshape(3, 3, -1)
    particle_mass = particles[24] * living
    coupling = (particles[24] * affine - stress_gain * kirchhoff(deform, particles[25])) * living
    momentum = particle_mass * particles[0:3]
    anchor = anchor_nodes(block_ids, node_offsets, blocks)
    weights_axis = spline_weights(fraction)
    grid_sums = jnp.zeros((4, padded * padded * padded * 512), particles.dtype)
    for stencil_id in range(27):
        flat_index, weight, displace = stencil_point(fraction, anchor, weights_axis, padded, stencil_id)
        pushed = weight * (momentum + matrix_vector(coupling, displace))
        values = jnp.concatenate([(weight * particle_mass)[None], pushed])
        grid_sums = grid_sums.at[:, flat_index].add(values)
    return grid_sums.reshape(4, padded, padded, padded, 512)


def grid_update(totals):
    velocity = totals[1:4] / jnp.maximum(totals[0:1], mass_floor)
    return velocity.at[2].add(-time_step * gravity)


def gather_grid(particles, block_ids, node_offsets, living, blocks, velocity_grid):
    padded = blocks + 2
    fraction = particles[21:24]
    deform = particles[12:21].reshape(3, 3, -1)
    anchor = anchor_nodes(block_ids, node_offsets, blocks)
    weights_axis = spline_weights(fraction)
    flattened = velocity_grid.reshape(3, -1)
    new_velocity = jnp.zeros_like(fraction)
    new_affine = jnp.zeros_like(deform)
    for stencil_id in range(27):
        flat_index, weight, displace = stencil_point(fraction, anchor, weights_axis, padded, stencil_id)
        sampled = weight * flattened[:, flat_index]
        new_velocity = new_velocity + sampled
        new_affine = new_affine + 4.0 * sampled[:, None, :] * displace[None, :, :]
    new_deform = deform + time_step * matrix_product(new_affine, deform)
    new_fraction = fraction + time_step * new_velocity
    record_rows = jnp.concatenate([new_velocity, new_affine.reshape(9, -1), new_deform.reshape(9, -1), new_fraction, particles[24:26]])
    return record_rows * living


def fold_axis(grid_sums, domain_axis, block_axis, blocks):
    lower_side = lax.slice_in_dim(grid_sums, 0, 1, axis=block_axis)
    upper_side = lax.slice_in_dim(grid_sums, blocks + 1, blocks + 2, axis=block_axis)
    centre = lax.slice_in_dim(grid_sums, 1, blocks + 1, axis=block_axis)
    first_block = lax.slice_in_dim(centre, 0, 1, axis=block_axis) + jnp.roll(upper_side, 1, axis=domain_axis)
    last_block = lax.slice_in_dim(centre, blocks - 1, blocks, axis=block_axis) + jnp.roll(lower_side, -1, axis=domain_axis)
    middle = lax.slice_in_dim(centre, 1, blocks - 1, axis=block_axis)
    return jnp.concatenate([first_block, middle, last_block], axis=block_axis)


def pad_axis(velocity_field, domain_axis, block_axis, blocks):
    lower_pad = jnp.roll(lax.slice_in_dim(velocity_field, blocks - 1, blocks, axis=block_axis), 1, axis=domain_axis)
    upper_pad = jnp.roll(lax.slice_in_dim(velocity_field, 0, 1, axis=block_axis), -1, axis=domain_axis)
    return jnp.concatenate([lower_pad, velocity_field, upper_pad], axis=block_axis)


def reference(particles, block_ids, node_offsets, live_count, migrations):
    domains = N_GX * N_GY * N_GZ
    padded = BLK + 2
    per_record = particles.reshape(26, domains, P_DEV).transpose(1, 0, 2)
    per_block = block_ids.reshape(domains, P_DEV)
    per_offset = node_offsets.reshape(domains, P_DEV)
    slot_index = jnp.arange(P_DEV, dtype=jnp.int32)
    living = (slot_index[None, :] < live_count[:, None]).astype(particles.dtype)
    grids = jax.vmap(lambda record_rows, chosen, placed, alive_rows: scatter_grid(record_rows, chosen, placed, alive_rows, BLK))(per_record, per_block, per_offset, living)
    grids = grids.reshape(N_GX, N_GY, N_GZ, 4, padded, padded, padded, 512)
    totals = fold_axis(fold_axis(fold_axis(grids, 0, 4, BLK), 1, 5, BLK), 2, 6, BLK)
    owned_velocity = jax.vmap(grid_update)(totals.reshape(domains, 4, BLK, BLK, BLK, 512))
    owned_velocity = owned_velocity.reshape(N_GX, N_GY, N_GZ, 3, BLK, BLK, BLK, 512)
    padded_velocity = pad_axis(pad_axis(pad_axis(owned_velocity, 0, 4, BLK), 1, 5, BLK), 2, 6, BLK)
    padded_velocity = padded_velocity.reshape(domains, 3, padded, padded, padded, 512)
    updated = jax.vmap(lambda record_rows, chosen, placed, alive_rows, velocity_grid: gather_grid(record_rows, chosen, placed, alive_rows, BLK, velocity_grid))(per_record, per_block, per_offset, living, padded_velocity)
    plan_table = migrations.reshape(6, domains, CAP).transpose(1, 0, 2).reshape(domains, 6 * CAP)
    outgoing = jax.vmap(lambda record_rows, chosen: record_rows[:, chosen])(updated, plan_table)
    outgoing = outgoing.reshape(N_GX, N_GY, N_GZ, 26, 6, CAP)
    arrivals = []
    for direction_id in range(6):
        direction = 1 if direction_id % 2 == 0 else -1
        arrivals.append(jnp.roll(outgoing[:, :, :, :, direction_id, :], direction, axis=direction_id // 2))
    arrived = jnp.stack(arrivals, axis=4).reshape(domains, 26, 6 * CAP)
    moved = jax.vmap(lambda record_rows, chosen, incoming: record_rows.at[:, chosen].set(incoming))(updated, plan_table, arrived)
    return moved.transpose(1, 0, 2).reshape(26, domains * P_DEV)
```

```python
import functools

import jax
import jax.numpy as jnp
from jax import lax
from jax.experimental import pallas as pl
from jax.experimental.pallas import tpu as pltpu
from jax.sharding import PartitionSpec as P

BLK = 2
AXES = ("gx", "gy", "gz")
SPAN = 8 * BLK + 2
STRIDE = 24
ROWS = 4 * SPAN
LANES = 512
USED = STRIDE * SPAN
EDGE = 2 * STRIDE
FACES = 6

time_step = 0.05
stress_gain = 0.2
shear_zero = 5.0
bulk_zero = 5.0
harden_rate = 10.0
mass_floor = 0.1
gravity = 9.8

f32 = jnp.float32
bf16 = jnp.bfloat16
MESH = pl.DeviceIdType.MESH


def iota(shape, dim):
    return lax.broadcasted_iota(jnp.int32, shape, dim)


def split(value):
    high = value.astype(bf16)
    return high, (value - high.astype(f32)).astype(bf16)


def stacked(value):
    high = value.astype(bf16).astype(f32)
    return jnp.concatenate([high, value - high], axis=0).astype(bf16)


def dot_nt(left, right):
    return lax.dot_general(left, right, (((1,), (1,)), ((), ())), preferred_element_type=f32)


def dot_nn(left, right):
    return lax.dot_general(left, right, (((1,), (0,)), ((), ())), preferred_element_type=f32)


def contract(dot, left, right_high, right_low):
    rows = left.shape[0]
    both = dot(stacked(left), right_high)
    return both[:rows] + both[rows:] + dot(left.astype(bf16), right_low)


def spline(place, anchor, fraction):
    apart = (place - anchor) - fraction
    size = jnp.abs(apart)
    outer = jnp.maximum(1.5 - size, 0.0)
    inner = jnp.maximum(0.5 - size, 0.0)
    weight = 0.5 * outer * outer - 1.5 * inner * inner
    return weight, weight * apart


def axis_tables(anchor, fraction):
    count = fraction.shape[1]
    line = iota((STRIDE, count), 0).astype(f32)
    line_x = jnp.right_shift(iota((ROWS, count), 0), 2).astype(f32)
    return (
        spline(line_x, anchor[0:1], fraction[0:1]),
        spline(line, anchor[1:2], fraction[1:2]),
        spline(line, anchor[2:3], fraction[2:3]),
    )


def store_pair(high_ref, low_ref, row, column, outer_line, inner_line, picks):
    count = inner_line.shape[1]
    pair = jnp.concatenate([outer_line[p : p + 1] * inner_line for p in picks], axis=0)
    high, low = split(pair)
    high_ref[row : row + EDGE, column : column + count] = high
    low_ref[row : row + EDGE, column : column + count] = low


def fill_tables(high_ref, low_ref, tables):
    _, (weight_y, shift_y), (weight_z, shift_z) = tables
    count = weight_y.shape[1]
    for part, (outer, inner) in enumerate(
        ((weight_y, weight_z), (shift_y, weight_z), (weight_y, shift_z))
    ):
        for pair in range(SPAN // 2):
            store_pair(
                high_ref, low_ref, EDGE * pair, part * count, outer, inner, (2 * pair, 2 * pair + 1)
            )
    for ref in (high_ref, low_ref):
        ref[USED:LANES, :] = jnp.zeros((LANES - USED, 3 * count), bf16)


def fill_face(high_ref, low_ref, tables):
    _, (weight_y, shift_y), (weight_z, shift_z) = tables
    count = weight_y.shape[1]
    for part, (outer, inner) in enumerate(
        ((weight_z, weight_y), (weight_z, shift_y), (shift_z, weight_y))
    ):
        store_pair(high_ref, low_ref, 0, part * count, outer, inner, (0, 1))
        store_pair(high_ref, low_ref, EDGE, part * count, outer, inner, (SPAN - 2, SPAN - 1))
    for ref in (high_ref, low_ref):
        ref[2 * EDGE : 128, :] = jnp.zeros((128 - 2 * EDGE, 3 * count), bf16)


def product(left, right):
    return [
        [
            left[i][0] * right[0][j] + left[i][1] * right[1][j] + left[i][2] * right[2][j]
            for j in range(3)
        ]
        for i in range(3)
    ]


def transposed(matrix):
    return [[matrix[j][i] for j in range(3)] for i in range(3)]


def pack(row):
    count = row.shape[1]
    return jnp.concatenate([row[:, s : s + 128] for s in range(0, count, 128)], axis=0)


def unpack(block):
    return jnp.concatenate([block[s : s + 1] for s in range(block.shape[0])], axis=1)


def stress(deform, plastic):
    rotation = deform
    for _ in range(5):
        inner = product(transposed(rotation), rotation)
        inner = [[(3.0 - inner[i][j]) if i == j else -inner[i][j] for j in range(3)] for i in range(3)]
        rotation = product(rotation, inner)
        rotation = [[0.5 * entry for entry in line] for line in rotation]
    f = deform
    volume = (
        f[0][0] * (f[1][1] * f[2][2] - f[1][2] * f[2][1])
        - f[0][1] * (f[1][0] * f[2][2] - f[1][2] * f[2][0])
        + f[0][2] * (f[1][0] * f[2][1] - f[1][1] * f[2][0])
    )
    harden = jnp.exp(harden_rate * (1.0 - plastic))
    shear = 2.0 * shear_zero * harden
    bulk = bulk_zero * harden * (volume - 1.0) * volume
    apart = [[f[i][j] - rotation[i][j] for j in range(3)] for i in range(3)]
    tau = product(apart, transposed(f))
    return [
        [shear * tau[i][j] + bulk if i == j else shear * tau[i][j] for j in range(3)]
        for i in range(3)
    ]


def read_back(out_ref, record, anchor, living, tables, high_ref, low_ref, velocity):
    count = record.shape[1]
    (weight_x, shift_x), _, _ = tables
    reads = contract(dot_nn, velocity, high_ref[...], low_ref[...])

    def fold(value):
        total = value[0:8]
        for row in range(8, ROWS, 8):
            total = total + value[row : row + 8]
        return total[0:4] + total[4:8]

    first = reads[:, 0:count]
    speed = fold(weight_x * first) * living
    along = [
        4.0 * living * fold(shift_x * first),
        4.0 * living * fold(weight_x * reads[:, count : 2 * count]),
        4.0 * living * fold(weight_x * reads[:, 2 * count : 3 * count]),
    ]
    out_ref[0:3, :] = speed[1:4]
    deform = [record[12 + 3 * k : 15 + 3 * k] for k in range(3)]
    for i in range(3):
        push = jnp.zeros((3, count), f32)
        for j in range(3):
            entry = along[j][1 + i : 2 + i]
            out_ref[3 + 3 * i + j : 4 + 3 * i + j, :] = entry
            push = push + entry * deform[j]
        out_ref[12 + 3 * i : 15 + 3 * i, :] = deform[i] * living + time_step * push
    out_ref[21:24, :] = record[21:24] * living + time_step * speed[1:4]
    out_ref[24:26, :] = record[24:26] * living
    out_ref[26:32, :] = jnp.zeros((6, count), f32)


def kernel(
    sizes,
    live_ref,
    record_ref,
    block_ref,
    offset_ref,
    plan_ref,
    out_ref,
    high_ref,
    low_ref,
    face_high,
    face_low,
    some_high,
    some_low,
    grid_ref,
    z_send,
    z_recv,
    x_recv,
    y_recv,
    c_recv,
    leave_ref,
    come_ref,
    new_ref,
    z_sems,
    xy_sems,
    m_sems,
):
    me = [lax.axis_index(name) for name in AXES]

    def at(*step):
        return tuple(
            lax.rem(me[a] + step[a] + sizes[a], sizes[a]) if step[a] else me[a] for a in range(3)
        )

    pair_z = sizes[2] == 2
    z_steps = ((0, 0, 1),) if pair_z else ((0, 0, 1), (0, 0, -1))
    xy_steps = tuple((i, j, 0) for i in (1, 0, -1) for j in (1, 0, -1) if i or j)
    barrier = pltpu.get_barrier_semaphore()
    for step in z_steps + xy_steps:
        pl.semaphore_signal(barrier, inc=1, device_id=at(*step), device_id_type=MESH)

    count = record_ref.shape[1]
    record = record_ref[...]
    fraction = record[21:24]
    blocks = block_ref[...]
    offsets = offset_ref[...]
    anchor = (
        jnp.concatenate(
            [
                8 * jnp.right_shift(blocks, 2) + jnp.right_shift(offsets, 6),
                8 * (jnp.right_shift(blocks, 1) & 1) + (jnp.right_shift(offsets, 3) & 7),
                8 * (blocks & 1) + (offsets & 7),
            ],
            axis=0,
        )
        + 1
    ).astype(f32)
    living = jnp.where(iota((1, count), 1) < live_ref[0], 1.0, 0.0).astype(f32)

    tables = axis_tables(anchor, fraction)
    fill_face(face_high, face_low, tables)

    plastic = pack(record[25:26])
    deform = [[pack(record[12 + 3 * i + j : 13 + 3 * i + j]) for j in range(3)] for i in range(3)]
    tau = stress(deform, plastic)
    mass = record[24:25]
    held = mass * living
    coupling = [
        [
            (mass * record[3 + 3 * i + j : 4 + 3 * i + j] - stress_gain * unpack(tau[i][j])) * living
            for j in range(3)
        ]
        for i in range(3)
    ]
    none = jnp.zeros((1, count), f32)
    base = jnp.concatenate([held, held * record[0:3]] * 2, axis=0)
    pushes = [
        jnp.concatenate([none, coupling[0][j], coupling[1][j], coupling[2][j]] * 2, axis=0)
        for j in range(3)
    ]
    weight_x, shift_x = tables[0]
    tiles = range(0, ROWS, 8)
    first = [base * weight_x[r : r + 8] + pushes[0] * shift_x[r : r + 8] for r in tiles]
    second = [pushes[1] * weight_x[r : r + 8] for r in tiles]
    third = [pushes[2] * weight_x[r : r + 8] for r in tiles]
    left = jnp.concatenate([jnp.concatenate(part, axis=0) for part in (first, second, third)], axis=1)

    z_send[...] = contract(dot_nt, left, face_high[...], face_low[...])
    pl.semaphore_wait(barrier, len(z_steps) + len(xy_steps))

    def send(source, target, sems, slot, step):
        copy = pltpu.make_async_remote_copy(
            src_ref=source,
            dst_ref=target,
            send_sem=sems.at[0, slot],
            recv_sem=sems.at[1, slot],
            device_id=at(*step),
            device_id_type=MESH,
        )
        copy.start()
        return copy

    z_copies = [
        send(z_send, z_recv.at[slot], z_sems, slot, step) for slot, step in enumerate(z_steps)
    ]

    fill_tables(high_ref, low_ref, tables)
    partial = contract(dot_nt, left, high_ref[...], low_ref[...])

    lane = iota((128, LANES), 1)
    row = iota((128, LANES), 0)
    lane_y = jnp.right_shift(lane * 2731, 16)
    row_k = jnp.right_shift(row * 2731, 16)
    goal_z = jnp.where(row_k < 2, row_k + (SPAN - 2), row_k - 2)
    spread = jnp.where(
        (row - STRIDE * row_k == lane_y)
        & (lane - STRIDE * lane_y == goal_z)
        & (row_k < 4)
        & (lane_y < SPAN),
        1.0,
        0.0,
    ).astype(bf16)
    for copy in z_copies:
        copy.wait()
    if pair_z:
        shared = z_recv[0]
    else:
        shared = jnp.where(iota((ROWS, 128), 1) < EDGE, z_recv[1], z_recv[0])
    spread_sum = dot_nn(stacked(shared), spread)
    grid_ref[...] = partial + spread_sum[:ROWS] + spread_sum[ROWS:]

    rows_of = {1: pl.ds(ROWS - 8, 8), -1: pl.ds(0, 8), 0: pl.ds(0, ROWS)}
    lanes_of = {1: pl.ds(LANES - 128, 128), -1: pl.ds(0, 128), 0: pl.ds(0, LANES)}
    xy_copies = []
    landing = {}
    for slot, (i, j, _) in enumerate(xy_steps):
        if i and j:
            target = c_recv.at[(0 if i > 0 else 2) + (0 if j > 0 else 1)]
        elif i:
            target = x_recv.at[0 if i > 0 else 1]
        else:
            target = y_recv.at[0 if j > 0 else 1]
        landing[i, j] = target
        xy_copies.append(send(grid_ref.at[rows_of[i], lanes_of[j]], target, xy_sems, slot, (i, j, 0)))

    plan = plan_ref[...].astype(f32)
    cap = plan.shape[1]
    leaving = FACES * cap
    wide = jnp.concatenate(
        [jnp.broadcast_to(plan[q : q + 1], (cap, cap)) for q in range(FACES)], axis=0
    )
    diagonal = (iota((leaving, cap), 0) & (cap - 1)) == iota((leaving, cap), 1)
    chosen = jnp.sum(jnp.where(diagonal, wide, 0.0), axis=1, keepdims=True)
    picked = jnp.where(iota((leaving, count), 1).astype(f32) == chosen, 1.0, 0.0).astype(f32)
    taken = jnp.sum(picked, axis=0, keepdims=True)
    picker = jnp.concatenate([picked, jnp.zeros((128 - leaving, count), f32)], axis=0).astype(bf16)
    full = jnp.concatenate([record, anchor, living, jnp.zeros((2, count), f32)], axis=0)

    def thirds(value):
        high = value.astype(bf16).astype(f32)
        rest = value - high
        middle = rest.astype(bf16).astype(f32)
        return jnp.concatenate([high, middle, rest - middle], axis=0).astype(bf16)

    def pick(dot, value):
        got = dot(thirds(value), picker)
        return got[0:32] + got[32:64] + got[64:96]

    some = pick(dot_nt, full)
    some_tables = axis_tables(some[26:29], some[21:24])
    fill_tables(some_high, some_low, some_tables)

    for copy in xy_copies:
        copy.wait()
    near = iota((ROWS, 128), 1) < EDGE
    near8 = iota((8, 128), 1) < EDGE
    partial = grid_ref[...]
    low_side = y_recv[0]
    high_side = jnp.where(near, y_recv[1], 0.0)
    middle = jnp.zeros((8, LANES - 256), f32)
    low_rows = x_recv[0] + jnp.concatenate(
        [c_recv[0], middle, jnp.where(near8, c_recv[1], 0.0)], axis=1
    )
    high_rows = x_recv[1] + jnp.concatenate(
        [c_recv[2], middle, jnp.where(near8, c_recv[3], 0.0)], axis=1
    )
    totals = jnp.concatenate(
        [
            partial[:, 0:128] + low_side,
            partial[:, 128 : LANES - 128],
            partial[:, LANES - 128 :] + high_side,
        ],
        axis=1,
    )
    totals = jnp.concatenate(
        [totals[0:8] + low_rows, totals[8 : ROWS - 8], totals[ROWS - 8 :] + high_rows], axis=0
    )
    channel = iota((ROWS, LANES), 0) & 3
    mass_of = jnp.where(
        channel == 1,
        pltpu.roll(totals, 1, 0),
        jnp.where(channel == 2, pltpu.roll(totals, 2, 0), pltpu.roll(totals, 3, 0)),
    )
    velocity = totals / jnp.maximum(mass_of, mass_floor)
    velocity = jnp.where(channel == 3, velocity - time_step * gravity, velocity)
    velocity = jnp.where(channel == 0, 0.0, velocity)

    read_back(
        leave_ref, some, some[26:29], some[29:30], some_tables, some_high, some_low, velocity
    )
    m_steps = ((1, 0, 0), (-1, 0, 0), (0, 1, 0), (0, -1, 0)) + z_steps
    m_copies = [
        send(leave_ref, come_ref.at[slot], m_sems, slot, step) for slot, step in enumerate(m_steps)
    ]
    read_back(new_ref, record, anchor, living, tables, high_ref, low_ref, velocity)
    for copy in m_copies:
        copy.wait()
    face = jnp.right_shift(iota((32, 128), 1), cap.bit_length() - 1)
    come = come_ref[0]
    for q in range(1, FACES):
        come = jnp.where(face == q, come_ref[min(q, len(m_steps) - 1)], come)
    placed = pick(dot_nn, come)
    out_ref[...] = jnp.where(taken > 0.0, placed, new_ref[...])[0:26]


def body(sizes, particles, block_ids, node_offsets, live_count, migrations):
    count = particles.shape[1]
    vmem = pl.BlockSpec(memory_space=pltpu.VMEM)
    return pl.pallas_call(
        functools.partial(kernel, sizes),
        out_shape=jax.ShapeDtypeStruct(particles.shape, f32),
        in_specs=[pl.BlockSpec(memory_space=pltpu.SMEM)] + [vmem] * 4,
        out_specs=vmem,
        scratch_shapes=[
            pltpu.VMEM((LANES, 3 * count), bf16),
            pltpu.VMEM((LANES, 3 * count), bf16),
            pltpu.VMEM((128, 3 * count), bf16),
            pltpu.VMEM((128, 3 * count), bf16),
            pltpu.VMEM((LANES, 3 * 128), bf16),
            pltpu.VMEM((LANES, 3 * 128), bf16),
            pltpu.VMEM((ROWS, LANES), f32),
            pltpu.VMEM((ROWS, 128), f32),
            pltpu.VMEM((2, ROWS, 128), f32),
            pltpu.VMEM((2, 8, LANES), f32),
            pltpu.VMEM((2, ROWS, 128), f32),
            pltpu.VMEM((4, 8, 128), f32),
            pltpu.VMEM((32, 128), f32),
            pltpu.VMEM((FACES, 32, 128), f32),
            pltpu.VMEM((32, count), f32),
            pltpu.SemaphoreType.DMA((2, 2)),
            pltpu.SemaphoreType.DMA((2, 8)),
            pltpu.SemaphoreType.DMA((2, 6)),
        ],
        compiler_params=pltpu.CompilerParams(
            collective_id=0, has_side_effects=True, vmem_limit_bytes=32 * 1024 * 1024
        ),
        name="substep",
    )(
        live_count,
        particles,
        block_ids.reshape(1, count),
        node_offsets.reshape(1, count),
        migrations,
    )


def solution(mesh):
    sizes = tuple(mesh.shape[name] for name in AXES)
    return jax.shard_map(
        functools.partial(body, sizes),
        mesh=mesh,
        in_specs=(
            P(None, AXES),
            P(AXES),
            P(AXES),
            P(AXES),
            P(None, AXES),
        ),
        out_specs=P(None, AXES),
        check_vma=False,
    )
```

```python
import functools

import jax
import jax.numpy as jnp
from jax import lax
from jax.experimental import pallas as pl
from jax.experimental.pallas import tpu as pltpu
from jax.sharding import PartitionSpec as P

BLK = 2
AXES = ("gx", "gy", "gz")
SPAN = 8 * BLK + 2
STRIDE = 24
ROWS = 4 * SPAN
LANES = 512
USED = STRIDE * SPAN
EDGE = 2 * STRIDE
CENTRE = 0.5 * (SPAN - 1)
FACES = 6

time_step = 0.05
stress_gain = 0.2
shear_zero = 5.0
bulk_zero = 5.0
harden_rate = 10.0
mass_floor = 0.1
gravity = 9.8

f32 = jnp.float32
bf16 = jnp.bfloat16
MESH = pl.DeviceIdType.MESH


def iota(shape, dim):
    return lax.broadcasted_iota(jnp.int32, shape, dim)


def split(value):
    high = value.astype(bf16)
    return high, (value - high.astype(f32)).astype(bf16)


def stacked(value):
    high = value.astype(bf16).astype(f32)
    return jnp.concatenate([high, value - high], axis=0).astype(bf16)


def dot_nt(left, right):
    return lax.dot_general(left, right, (((1,), (1,)), ((), ())), preferred_element_type=f32)


def dot_nn(left, right):
    return lax.dot_general(left, right, (((1,), (0,)), ((), ())), preferred_element_type=f32)


def contract(dot, left, right_high, right_low):
    rows = left.shape[0]
    both = dot(stacked(left), right_high)
    return both[:rows] + both[rows:] + dot(left.astype(bf16), right_low)


def spline(place, anchor, fraction):
    apart = (place - anchor) - fraction
    size = jnp.abs(apart)
    outer = jnp.maximum(1.5 - size, 0.0)
    inner = jnp.maximum(0.5 - size, 0.0)
    weight = 0.5 * outer * outer - 1.5 * inner * inner
    return weight, weight * apart


def axis_tables(anchor, fraction):
    count = fraction.shape[1]
    line = iota((STRIDE, count), 0).astype(f32)
    line_x = jnp.right_shift(iota((ROWS, count), 0), 2).astype(f32)
    return (
        spline(line_x, anchor[0:1], fraction[0:1]),
        spline(line, anchor[1:2], fraction[1:2]),
        spline(line, anchor[2:3], fraction[2:3]),
    )


def store_pair(high_ref, low_ref, row, outer_line, inner_line, picks):
    pair = jnp.concatenate([outer_line[p : p + 1] * inner_line for p in picks], axis=0)
    high, low = split(pair)
    high_ref[row : row + EDGE, :] = high
    low_ref[row : row + EDGE, :] = low


def fill_tables(high_ref, low_ref, tables):
    _, (weight_y, _), (weight_z, _) = tables
    count = weight_y.shape[1]
    for pair in range(SPAN // 2):
        store_pair(high_ref, low_ref, EDGE * pair, weight_y, weight_z, (2 * pair, 2 * pair + 1))
    for ref in (high_ref, low_ref):
        ref[USED:LANES, :] = jnp.zeros((LANES - USED, count), bf16)


def fill_face(high_ref, low_ref, tables):
    _, (weight_y, _), (weight_z, _) = tables
    count = weight_y.shape[1]
    store_pair(high_ref, low_ref, 0, weight_z, weight_y, (0, 1))
    store_pair(high_ref, low_ref, EDGE, weight_z, weight_y, (SPAN - 2, SPAN - 1))
    for ref in (high_ref, low_ref):
        ref[2 * EDGE : 128, :] = jnp.zeros((128 - 2 * EDGE, count), bf16)


def lane_places(lanes):
    lane = iota((1, lanes), 1)
    line = jnp.right_shift(lane * 2731, 16)
    return line.astype(f32) - CENTRE, (lane - STRIDE * line).astype(f32) - CENTRE


def combine(parts, place_y, place_z):
    return parts[:ROWS] + place_y * parts[ROWS : 2 * ROWS] + place_z * parts[2 * ROWS :]


def product(left, right):
    return [
        [
            left[i][0] * right[0][j] + left[i][1] * right[1][j] + left[i][2] * right[2][j]
            for j in range(3)
        ]
        for i in range(3)
    ]


def transposed(matrix):
    return [[matrix[j][i] for j in range(3)] for i in range(3)]


def pack(row):
    count = row.shape[1]
    return jnp.concatenate([row[:, s : s + 128] for s in range(0, count, 128)], axis=0)


def unpack(block):
    return jnp.concatenate([block[s : s + 1] for s in range(block.shape[0])], axis=1)


def stress(deform, plastic):
    rotation = deform
    for _ in range(5):
        inner = product(transposed(rotation), rotation)
        inner = [[(3.0 - inner[i][j]) if i == j else -inner[i][j] for j in range(3)] for i in range(3)]
        rotation = product(rotation, inner)
        rotation = [[0.5 * entry for entry in line] for line in rotation]
    f = deform
    volume = (
        f[0][0] * (f[1][1] * f[2][2] - f[1][2] * f[2][1])
        - f[0][1] * (f[1][0] * f[2][2] - f[1][2] * f[2][0])
        + f[0][2] * (f[1][0] * f[2][1] - f[1][1] * f[2][0])
    )
    harden = jnp.exp(harden_rate * (1.0 - plastic))
    shear = 2.0 * shear_zero * harden
    bulk = bulk_zero * harden * (volume - 1.0) * volume
    apart = [[f[i][j] - rotation[i][j] for j in range(3)] for i in range(3)]
    tau = product(apart, transposed(f))
    return [
        [shear * tau[i][j] + bulk if i == j else shear * tau[i][j] for j in range(3)]
        for i in range(3)
    ]


def read_back(out_ref, record, anchor, living, tables, high_ref, low_ref, velocity):
    count = record.shape[1]
    (weight_x, shift_x), _, _ = tables
    reads = contract(dot_nn, velocity, high_ref[...], low_ref[...])

    def fold(value):
        total = value[0:8]
        for row in range(8, ROWS, 8):
            total = total + value[row : row + 8]
        return total[0:4] + total[4:8]

    first = reads[:ROWS]
    speed = fold(weight_x * first) * living
    place = anchor + record[21:24] - CENTRE
    along = [
        4.0 * living * fold(shift_x * first),
        4.0 * (living * fold(weight_x * reads[ROWS : 2 * ROWS]) - place[1:2] * speed),
        4.0 * (living * fold(weight_x * reads[2 * ROWS :]) - place[2:3] * speed),
    ]
    out_ref[0:3, :] = speed[1:4]
    deform = [record[12 + 3 * k : 15 + 3 * k] for k in range(3)]
    for i in range(3):
        push = jnp.zeros((3, count), f32)
        for j in range(3):
            entry = along[j][1 + i : 2 + i]
            out_ref[3 + 3 * i + j : 4 + 3 * i + j, :] = entry
            push = push + entry * deform[j]
        out_ref[12 + 3 * i : 15 + 3 * i, :] = deform[i] * living + time_step * push
    out_ref[21:24, :] = record[21:24] * living + time_step * speed[1:4]
    out_ref[24:26, :] = record[24:26] * living
    out_ref[26:32, :] = jnp.zeros((6, count), f32)


def kernel(
    sizes,
    live_hbm,
    record_hbm,
    block_hbm,
    offset_hbm,
    plan_hbm,
    out_ref,
    live_ref,
    record_ref,
    block_ref,
    offset_ref,
    plan_ref,
    in_sems,
    high_ref,
    low_ref,
    face_high,
    face_low,
    some_high,
    some_low,
    grid_ref,
    z_send,
    z_recv,
    x_recv,
    y_recv,
    c_recv,
    leave_ref,
    come_ref,
    new_ref,
    z_sems,
    xy_sems,
    m_sems,
):
    operands = (
        (record_hbm, record_ref),
        (block_hbm, block_ref),
        (offset_hbm, offset_ref),
        (live_hbm, live_ref),
        (plan_hbm, plan_ref),
    )
    in_copies = [
        pltpu.make_async_copy(source, target, in_sems.at[slot])
        for slot, (source, target) in enumerate(operands)
    ]
    for copy in in_copies:
        copy.start()
    me = [lax.axis_index(name) for name in AXES]

    def at(*step):
        return tuple(
            lax.rem(me[a] + step[a] + sizes[a], sizes[a]) if step[a] else me[a] for a in range(3)
        )

    pair_z = sizes[2] == 2
    z_steps = ((0, 0, 1),) if pair_z else ((0, 0, 1), (0, 0, -1))
    xy_steps = tuple((i, j, 0) for i in (1, 0, -1) for j in (1, 0, -1) if i or j)
    barrier = pltpu.get_barrier_semaphore()
    for step in z_steps + xy_steps:
        pl.semaphore_signal(barrier, inc=1, device_id=at(*step), device_id_type=MESH)

    for copy in in_copies:
        copy.wait()
    count = record_ref.shape[1]
    record = record_ref[...]
    fraction = record[21:24]
    blocks = block_ref[...]
    offsets = offset_ref[...]
    anchor = (
        jnp.concatenate(
            [
                8 * jnp.right_shift(blocks, 2) + jnp.right_shift(offsets, 6),
                8 * (jnp.right_shift(blocks, 1) & 1) + (jnp.right_shift(offsets, 3) & 7),
                8 * (blocks & 1) + (offsets & 7),
            ],
            axis=0,
        )
        + 1
    ).astype(f32)
    living = jnp.where(iota((1, count), 1) < live_ref[0], 1.0, 0.0).astype(f32)

    tables = axis_tables(anchor, fraction)
    fill_face(face_high, face_low, tables)

    plastic = pack(record[25:26])
    deform = [[pack(record[12 + 3 * i + j : 13 + 3 * i + j]) for j in range(3)] for i in range(3)]
    tau = stress(deform, plastic)
    mass = record[24:25]
    held = mass * living
    coupling = [
        [
            (mass * record[3 + 3 * i + j : 4 + 3 * i + j] - stress_gain * unpack(tau[i][j])) * living
            for j in range(3)
        ]
        for i in range(3)
    ]
    none = jnp.zeros((1, count), f32)
    places = anchor + fraction - CENTRE
    momentum = [
        held * record[i : i + 1] - coupling[i][1] * places[1:2] - coupling[i][2] * places[2:3]
        for i in range(3)
    ]
    base = jnp.concatenate([held] + momentum + [held] + momentum, axis=0)
    pushes = [
        jnp.concatenate([none, coupling[0][j], coupling[1][j], coupling[2][j]] * 2, axis=0)
        for j in range(3)
    ]
    weight_x, shift_x = tables[0]
    tiles = range(0, ROWS, 8)
    left = jnp.concatenate(
        [base * weight_x[r : r + 8] + pushes[0] * shift_x[r : r + 8] for r in tiles]
        + [pushes[1] * weight_x[r : r + 8] for r in tiles]
        + [pushes[2] * weight_x[r : r + 8] for r in tiles],
        axis=0,
    )

    face_lane = iota((1, 128), 1)
    face_k = jnp.right_shift(face_lane * 2731, 16)
    face_y = (face_lane - STRIDE * face_k).astype(f32) - CENTRE
    face_z = jnp.where(face_k < 2, face_k, face_k + (SPAN - 4)).astype(f32) - CENTRE
    z_send[...] = combine(contract(dot_nt, left, face_high[...], face_low[...]), face_y, face_z)
    pl.semaphore_wait(barrier, len(z_steps) + len(xy_steps))

    def send(source, target, sems, slot, step):
        copy = pltpu.make_async_remote_copy(
            src_ref=source,
            dst_ref=target,
            send_sem=sems.at[0, slot],
            recv_sem=sems.at[1, slot],
            device_id=at(*step),
            device_id_type=MESH,
        )
        copy.start()
        return copy

    z_copies = [
        send(z_send, z_recv.at[slot], z_sems, slot, step) for slot, step in enumerate(z_steps)
    ]

    fill_tables(high_ref, low_ref, tables)
    lane_y, lane_z = lane_places(LANES)
    partial = combine(contract(dot_nt, left, high_ref[...], low_ref[...]), lane_y, lane_z)

    lane = iota((128, LANES), 1)
    row = iota((128, LANES), 0)
    line = jnp.right_shift(lane * 2731, 16)
    row_k = jnp.right_shift(row * 2731, 16)
    goal_z = jnp.where(row_k < 2, row_k + (SPAN - 2), row_k - 2)
    spread = jnp.where(
        (row - STRIDE * row_k == line)
        & (lane - STRIDE * line == goal_z)
        & (row_k < 4)
        & (line < SPAN),
        1.0,
        0.0,
    ).astype(bf16)
    for copy in z_copies:
        copy.wait()
    if pair_z:
        shared = z_recv[0]
    else:
        shared = jnp.where(iota((ROWS, 128), 1) < EDGE, z_recv[1], z_recv[0])
    spread_sum = dot_nn(stacked(shared), spread)
    grid_ref[...] = partial + spread_sum[:ROWS] + spread_sum[ROWS:]

    rows_of = {1: pl.ds(ROWS - 8, 8), -1: pl.ds(0, 8), 0: pl.ds(0, ROWS)}
    lanes_of = {1: pl.ds(LANES - 128, 128), -1: pl.ds(0, 128), 0: pl.ds(0, LANES)}
    xy_copies = []
    landing = {}
    for slot, (i, j, _) in enumerate(xy_steps):
        if i and j:
            target = c_recv.at[(0 if i > 0 else 2) + (0 if j > 0 else 1)]
        elif i:
            target = x_recv.at[0 if i > 0 else 1]
        else:
            target = y_recv.at[0 if j > 0 else 1]
        landing[i, j] = target
        xy_copies.append(send(grid_ref.at[rows_of[i], lanes_of[j]], target, xy_sems, slot, (i, j, 0)))

    plan = plan_ref[...].astype(f32)
    cap = plan.shape[1]
    leaving = FACES * cap
    wide = jnp.concatenate(
        [jnp.broadcast_to(plan[q : q + 1], (cap, cap)) for q in range(FACES)], axis=0
    )
    diagonal = (iota((leaving, cap), 0) & (cap - 1)) == iota((leaving, cap), 1)
    chosen = jnp.sum(jnp.where(diagonal, wide, 0.0), axis=1, keepdims=True)
    picked = jnp.where(iota((leaving, count), 1).astype(f32) == chosen, 1.0, 0.0).astype(f32)
    taken = jnp.sum(picked, axis=0, keepdims=True)
    picker = jnp.concatenate([picked, jnp.zeros((128 - leaving, count), f32)], axis=0).astype(bf16)
    full = jnp.concatenate([record, anchor, living, jnp.zeros((2, count), f32)], axis=0)

    def thirds(value):
        high = value.astype(bf16).astype(f32)
        rest = value - high
        middle = rest.astype(bf16).astype(f32)
        return jnp.concatenate([high, middle, rest - middle], axis=0).astype(bf16)

    def pick(dot, value):
        got = dot(thirds(value), picker)
        return got[0:32] + got[32:64] + got[64:96]

    some = pick(dot_nt, full)
    some_tables = axis_tables(some[26:29], some[21:24])
    fill_tables(some_high, some_low, some_tables)

    for copy in xy_copies:
        copy.wait()
    near = iota((ROWS, 128), 1) < EDGE
    near8 = iota((8, 128), 1) < EDGE
    partial = grid_ref[...]
    low_side = y_recv[0]
    high_side = jnp.where(near, y_recv[1], 0.0)
    middle = jnp.zeros((8, LANES - 256), f32)
    low_rows = x_recv[0] + jnp.concatenate(
        [c_recv[0], middle, jnp.where(near8, c_recv[1], 0.0)], axis=1
    )
    high_rows = x_recv[1] + jnp.concatenate(
        [c_recv[2], middle, jnp.where(near8, c_recv[3], 0.0)], axis=1
    )
    totals = jnp.concatenate(
        [
            partial[:, 0:128] + low_side,
            partial[:, 128 : LANES - 128],
            partial[:, LANES - 128 :] + high_side,
        ],
        axis=1,
    )
    totals = jnp.concatenate(
        [totals[0:8] + low_rows, totals[8 : ROWS - 8], totals[ROWS - 8 :] + high_rows], axis=0
    )
    channel = iota((ROWS, LANES), 0) & 3
    mass_of = jnp.where(
        channel == 1,
        pltpu.roll(totals, 1, 0),
        jnp.where(channel == 2, pltpu.roll(totals, 2, 0), pltpu.roll(totals, 3, 0)),
    )
    velocity = totals / jnp.maximum(mass_of, mass_floor)
    velocity = jnp.where(channel == 3, velocity - time_step * gravity, velocity)
    velocity = jnp.where(channel == 0, 0.0, velocity)
    velocity = jnp.concatenate([velocity, velocity * lane_y, velocity * lane_z], axis=0)

    read_back(
        leave_ref, some, some[26:29], some[29:30], some_tables, some_high, some_low, velocity
    )
    m_steps = ((1, 0, 0), (-1, 0, 0), (0, 1, 0), (0, -1, 0)) + z_steps
    m_copies = [
        send(leave_ref, come_ref.at[slot], m_sems, slot, step) for slot, step in enumerate(m_steps)
    ]
    read_back(new_ref, record, anchor, living, tables, high_ref, low_ref, velocity)
    for copy in m_copies:
        copy.wait()
    face = jnp.right_shift(iota((32, 128), 1), cap.bit_length() - 1)
    come = come_ref[0]
    for q in range(1, FACES):
        come = jnp.where(face == q, come_ref[min(q, len(m_steps) - 1)], come)
    placed = pick(dot_nn, come)
    out_ref[...] = jnp.where(taken > 0.0, placed, new_ref[...])[0:26]


def body(sizes, particles, block_ids, node_offsets, live_count, migrations):
    count = particles.shape[1]
    vmem = pl.BlockSpec(memory_space=pltpu.VMEM)
    return pl.pallas_call(
        functools.partial(kernel, sizes),
        out_shape=jax.ShapeDtypeStruct(particles.shape, f32),
        in_specs=[pl.BlockSpec(memory_space=pltpu.HBM)] * 5,
        out_specs=vmem,
        scratch_shapes=[
            pltpu.SMEM((1,), jnp.int32),
            pltpu.VMEM(particles.shape, f32),
            pltpu.VMEM((1, count), jnp.int32),
            pltpu.VMEM((1, count), jnp.int32),
            pltpu.VMEM(migrations.shape, jnp.int32),
            pltpu.SemaphoreType.DMA((5,)),
            pltpu.VMEM((LANES, count), bf16),
            pltpu.VMEM((LANES, count), bf16),
            pltpu.VMEM((128, count), bf16),
            pltpu.VMEM((128, count), bf16),
            pltpu.VMEM((LANES, 128), bf16),
            pltpu.VMEM((LANES, 128), bf16),
            pltpu.VMEM((ROWS, LANES), f32),
            pltpu.VMEM((ROWS, 128), f32),
            pltpu.VMEM((2, ROWS, 128), f32),
            pltpu.VMEM((2, 8, LANES), f32),
            pltpu.VMEM((2, ROWS, 128), f32),
            pltpu.VMEM((4, 8, 128), f32),
            pltpu.VMEM((32, 128), f32),
            pltpu.VMEM((FACES, 32, 128), f32),
            pltpu.VMEM((32, count), f32),
            pltpu.SemaphoreType.DMA((2, 2)),
            pltpu.SemaphoreType.DMA((2, 8)),
            pltpu.SemaphoreType.DMA((2, 6)),
        ],
        compiler_params=pltpu.CompilerParams(
            collective_id=0, has_side_effects=True, vmem_limit_bytes=60 * 1024 * 1024
        ),
        name="substep",
    )(
        live_count,
        particles,
        block_ids.reshape(1, count),
        node_offsets.reshape(1, count),
        migrations,
    )


def solution(mesh):
    sizes = tuple(mesh.shape[name] for name in AXES)
    return jax.shard_map(
        functools.partial(body, sizes),
        mesh=mesh,
        in_specs=(
            P(None, AXES),
            P(AXES),
            P(AXES),
            P(AXES),
            P(None, AXES),
        ),
        out_specs=P(None, AXES),
        check_vma=False,
    )
```

```python
import functools

import jax
import jax.numpy as jnp
from jax import lax
from jax.experimental import pallas as pl
from jax.experimental.pallas import tpu as pltpu
from jax.sharding import PartitionSpec as P

BLK = 2
AXES = ("gx", "gy", "gz")
SPAN = 8 * BLK + 2
STRIDE = 24
ROWS = 4 * SPAN
LANES = 512
USED = STRIDE * SPAN
EDGE = 2 * STRIDE
FOLD = 40
CENTRE = 0.5 * (SPAN - 1)
FACES = 6

time_step = 0.05
stress_gain = 0.2
shear_zero = 5.0
bulk_zero = 5.0
harden_rate = 10.0
mass_floor = 0.1
gravity = 9.8

f32 = jnp.float32
bf16 = jnp.bfloat16
MESH = pl.DeviceIdType.MESH


def iota(shape, dim):
    return lax.broadcasted_iota(jnp.int32, shape, dim)


def split(value):
    high = value.astype(bf16)
    return high, (value - high.astype(f32)).astype(bf16)


def stacked(value):
    high = value.astype(bf16).astype(f32)
    return jnp.concatenate([high, value - high], axis=0).astype(bf16)


def dot_nt(left, right):
    return lax.dot_general(left, right, (((1,), (1,)), ((), ())), preferred_element_type=f32)


def dot_nn(left, right):
    return lax.dot_general(left, right, (((1,), (0,)), ((), ())), preferred_element_type=f32)


def contract(dot, left, right_high, right_low):
    rows = left.shape[0]
    both = dot(stacked(left), right_high)
    return both[:rows] + both[rows:] + dot(left.astype(bf16), right_low)


def spline(place, anchor, fraction):
    apart = (place - anchor) - fraction
    size = jnp.abs(apart)
    outer = jnp.maximum(1.5 - size, 0.0)
    inner = jnp.maximum(0.5 - size, 0.0)
    weight = 0.5 * outer * outer - 1.5 * inner * inner
    return weight, weight * apart


def axis_tables(anchor, fraction):
    count = fraction.shape[1]
    line = iota((STRIDE, count), 0).astype(f32)
    line_x = jnp.right_shift(iota((ROWS, count), 0), 2).astype(f32)
    return (
        spline(line_x, anchor[0:1], fraction[0:1]),
        spline(line, anchor[1:2], fraction[1:2]),
        spline(line, anchor[2:3], fraction[2:3]),
    )


def store_pair(high_ref, low_ref, row, outer_line, inner_line, picks):
    pair = jnp.concatenate([outer_line[p : p + 1] * inner_line for p in picks], axis=0)
    high, low = split(pair)
    high_ref[row : row + EDGE, :] = high
    low_ref[row : row + EDGE, :] = low


def fill_tables(high_ref, low_ref, tables):
    _, (weight_y, _), (weight_z, _) = tables
    count = weight_y.shape[1]
    for pair in range(SPAN // 2):
        store_pair(high_ref, low_ref, EDGE * pair, weight_y, weight_z, (2 * pair, 2 * pair + 1))
    for ref in (high_ref, low_ref):
        ref[USED:LANES, :] = jnp.zeros((LANES - USED, count), bf16)


def fill_face(high_ref, low_ref, tables):
    _, (weight_y, _), (weight_z, _) = tables
    count = weight_y.shape[1]
    store_pair(high_ref, low_ref, 0, weight_z, weight_y, (0, 1))
    store_pair(high_ref, low_ref, EDGE, weight_z, weight_y, (SPAN - 2, SPAN - 1))
    for ref in (high_ref, low_ref):
        ref[2 * EDGE : 128, :] = jnp.zeros((128 - 2 * EDGE, count), bf16)


def lane_places(lanes):
    lane = iota((1, lanes), 1)
    line = jnp.right_shift(lane * 2731, 16)
    return line.astype(f32) - CENTRE, (lane - STRIDE * line).astype(f32) - CENTRE


def combine(parts, place_y, place_z):
    return parts[:ROWS] + place_y * parts[ROWS : 2 * ROWS] + place_z * parts[2 * ROWS :]


def product(left, right):
    return [
        [
            left[i][0] * right[0][j] + left[i][1] * right[1][j] + left[i][2] * right[2][j]
            for j in range(3)
        ]
        for i in range(3)
    ]


def transposed(matrix):
    return [[matrix[j][i] for j in range(3)] for i in range(3)]


def pack(row):
    count = row.shape[1]
    return jnp.concatenate([row[:, s : s + 128] for s in range(0, count, 128)], axis=0)


def unpack(block):
    return jnp.concatenate([block[s : s + 1] for s in range(block.shape[0])], axis=1)


def stress(deform, plastic):
    rotation = deform
    for _ in range(5):
        inner = product(transposed(rotation), rotation)
        inner = [[(3.0 - inner[i][j]) if i == j else -inner[i][j] for j in range(3)] for i in range(3)]
        rotation = product(rotation, inner)
        rotation = [[0.5 * entry for entry in line] for line in rotation]
    f = deform
    volume = (
        f[0][0] * (f[1][1] * f[2][2] - f[1][2] * f[2][1])
        - f[0][1] * (f[1][0] * f[2][2] - f[1][2] * f[2][0])
        + f[0][2] * (f[1][0] * f[2][1] - f[1][1] * f[2][0])
    )
    harden = jnp.exp(harden_rate * (1.0 - plastic))
    shear = 2.0 * shear_zero * harden
    bulk = bulk_zero * harden * (volume - 1.0) * volume
    apart = [[f[i][j] - rotation[i][j] for j in range(3)] for i in range(3)]
    tau = product(apart, transposed(f))
    return [
        [shear * tau[i][j] + bulk if i == j else shear * tau[i][j] for j in range(3)]
        for i in range(3)
    ]


def read_back(out_ref, record, anchor, living, tables, high_ref, low_ref, velocity):
    count = record.shape[1]
    (weight_x, shift_x), _, _ = tables
    reads = contract(dot_nn, velocity, high_ref[...], low_ref[...])

    def fold(value):
        total = value[0:8]
        for row in range(8, ROWS, 8):
            total = total + value[row : row + 8]
        return total[0:4] + total[4:8]

    first = reads[:ROWS]
    speed = fold(weight_x * first) * living
    place = anchor + record[21:24] - CENTRE
    along = [
        4.0 * living * fold(shift_x * first),
        4.0 * (living * fold(weight_x * reads[ROWS : 2 * ROWS]) - place[1:2] * speed),
        4.0 * (living * fold(weight_x * reads[2 * ROWS :]) - place[2:3] * speed),
    ]
    out_ref[0:3, :] = speed[1:4]
    deform = [record[12 + 3 * k : 15 + 3 * k] for k in range(3)]
    for i in range(3):
        push = jnp.zeros((3, count), f32)
        for j in range(3):
            entry = along[j][1 + i : 2 + i]
            out_ref[3 + 3 * i + j : 4 + 3 * i + j, :] = entry
            push = push + entry * deform[j]
        out_ref[12 + 3 * i : 15 + 3 * i, :] = deform[i] * living + time_step * push
    out_ref[21:24, :] = record[21:24] * living + time_step * speed[1:4]
    out_ref[24:26, :] = record[24:26] * living
    out_ref[26:32, :] = jnp.zeros((6, count), f32)


def pack_side(tile):
    rest = jnp.concatenate([tile[FOLD:], jnp.zeros((2 * FOLD - ROWS, 128), f32)], axis=0)
    return jnp.where(iota((FOLD, 128), 1) < 64, tile[:FOLD], pltpu.roll(rest, 64, 1))


def open_side(packed):
    rest = pltpu.roll(packed, 64, 1)[: ROWS - FOLD]
    full = jnp.concatenate([packed, rest], axis=0)
    return jnp.where(iota((ROWS, 128), 1) < EDGE, full, 0.0)


def turned(value):
    rows = jnp.zeros((128 - value.shape[0], 128), f32)
    return jnp.concatenate([value, rows], axis=0).T


def kernel(
    sizes,
    live_hbm,
    record_hbm,
    block_hbm,
    offset_hbm,
    plan_hbm,
    out_ref,
    live_ref,
    record_ref,
    block_ref,
    offset_ref,
    plan_ref,
    in_sems,
    high_ref,
    low_ref,
    face_high,
    face_low,
    some_high,
    some_low,
    grid_ref,
    z_send,
    z_recv,
    x_recv,
    y_send,
    y_recv,
    c_recv,
    leave_ref,
    m_send,
    come_ref,
    new_ref,
    z_sems,
    xy_sems,
    m_sems,
):
    operands = (
        (record_hbm, record_ref),
        (block_hbm, block_ref),
        (offset_hbm, offset_ref),
        (live_hbm, live_ref),
        (plan_hbm, plan_ref),
    )
    in_copies = [
        pltpu.make_async_copy(source, target, in_sems.at[slot])
        for slot, (source, target) in enumerate(operands)
    ]
    for copy in in_copies:
        copy.start()
    me = [lax.axis_index(name) for name in AXES]

    def at(*step):
        return tuple(
            lax.rem(me[a] + step[a] + sizes[a], sizes[a]) if step[a] else me[a] for a in range(3)
        )

    pair_z = sizes[2] == 2
    z_steps = ((0, 0, 1),) if pair_z else ((0, 0, 1), (0, 0, -1))
    xy_steps = tuple((i, j, 0) for i in (0, 1, -1) for j in (1, -1, 0) if i or j)
    barrier = pltpu.get_barrier_semaphore()
    for step in z_steps + xy_steps:
        pl.semaphore_signal(barrier, inc=1, device_id=at(*step), device_id_type=MESH)

    for copy in in_copies:
        copy.wait()
    count = record_ref.shape[1]
    record = record_ref[...]
    fraction = record[21:24]
    blocks = block_ref[...]
    offsets = offset_ref[...]
    anchor = (
        jnp.concatenate(
            [
                8 * jnp.right_shift(blocks, 2) + jnp.right_shift(offsets, 6),
                8 * (jnp.right_shift(blocks, 1) & 1) + (jnp.right_shift(offsets, 3) & 7),
                8 * (blocks & 1) + (offsets & 7),
            ],
            axis=0,
        )
        + 1
    ).astype(f32)
    living = jnp.where(iota((1, count), 1) < live_ref[0], 1.0, 0.0).astype(f32)

    tables = axis_tables(anchor, fraction)
    fill_face(face_high, face_low, tables)

    plastic = pack(record[25:26])
    deform = [[pack(record[12 + 3 * i + j : 13 + 3 * i + j]) for j in range(3)] for i in range(3)]
    tau = stress(deform, plastic)
    mass = record[24:25]
    held = mass * living
    coupling = [
        [
            (mass * record[3 + 3 * i + j : 4 + 3 * i + j] - stress_gain * unpack(tau[i][j])) * living
            for j in range(3)
        ]
        for i in range(3)
    ]
    none = jnp.zeros((1, count), f32)
    places = anchor + fraction - CENTRE
    momentum = [
        held * record[i : i + 1] - coupling[i][1] * places[1:2] - coupling[i][2] * places[2:3]
        for i in range(3)
    ]
    base = jnp.concatenate([held] + momentum + [held] + momentum, axis=0)
    pushes = [
        jnp.concatenate([none, coupling[0][j], coupling[1][j], coupling[2][j]] * 2, axis=0)
        for j in range(3)
    ]
    weight_x, shift_x = tables[0]
    tiles = range(0, ROWS, 8)
    left = jnp.concatenate(
        [base * weight_x[r : r + 8] + pushes[0] * shift_x[r : r + 8] for r in tiles]
        + [pushes[1] * weight_x[r : r + 8] for r in tiles]
        + [pushes[2] * weight_x[r : r + 8] for r in tiles],
        axis=0,
    )

    face_lane = iota((1, 128), 1)
    face_k = jnp.right_shift(face_lane * 2731, 16)
    face_y = (face_lane - STRIDE * face_k).astype(f32) - CENTRE
    face_z = jnp.where(face_k < 2, face_k, face_k + (SPAN - 4)).astype(f32) - CENTRE
    z_send[...] = combine(contract(dot_nt, left, face_high[...], face_low[...]), face_y, face_z)
    pl.semaphore_wait(barrier, len(z_steps) + len(xy_steps))

    def send(source, target, sems, slot, step):
        copy = pltpu.make_async_remote_copy(
            src_ref=source,
            dst_ref=target,
            send_sem=sems.at[0, slot],
            recv_sem=sems.at[1, slot],
            device_id=at(*step),
            device_id_type=MESH,
        )
        copy.start()
        return copy

    z_copies = [
        send(z_send, z_recv.at[slot], z_sems, slot, step) for slot, step in enumerate(z_steps)
    ]

    fill_tables(high_ref, low_ref, tables)
    lane_y, lane_z = lane_places(LANES)
    partial = combine(contract(dot_nt, left, high_ref[...], low_ref[...]), lane_y, lane_z)

    lane = iota((128, LANES), 1)
    row = iota((128, LANES), 0)
    line = jnp.right_shift(lane * 2731, 16)
    row_k = jnp.right_shift(row * 2731, 16)
    goal_z = jnp.where(row_k < 2, row_k + (SPAN - 2), row_k - 2)
    spread = jnp.where(
        (row - STRIDE * row_k == line)
        & (lane - STRIDE * line == goal_z)
        & (row_k < 4)
        & (line < SPAN),
        1.0,
        0.0,
    ).astype(bf16)
    for copy in z_copies:
        copy.wait()
    if pair_z:
        shared = z_recv[0]
    else:
        shared = jnp.where(iota((ROWS, 128), 1) < EDGE, z_recv[1], z_recv[0])
    spread_sum = dot_nn(stacked(shared), spread)
    partial = partial + spread_sum[:ROWS] + spread_sum[ROWS:]
    grid_ref[...] = partial
    y_send[0] = pack_side(partial[:, LANES - 128 :])
    y_send[1] = pack_side(partial[:, 0:128])

    rows_of = {1: pl.ds(ROWS - 8, 8), -1: pl.ds(0, 8)}
    lanes_of = {1: pl.ds(LANES - 128, 128), -1: pl.ds(0, 128)}
    xy_copies = []
    for slot, (i, j, _) in enumerate(xy_steps):
        if i and j:
            source = grid_ref.at[rows_of[i], lanes_of[j]]
            target = c_recv.at[(0 if i > 0 else 2) + (0 if j > 0 else 1)]
        elif i:
            source = grid_ref.at[rows_of[i], :]
            target = x_recv.at[0 if i > 0 else 1]
        else:
            source = y_send.at[0 if j > 0 else 1]
            target = y_recv.at[0 if j > 0 else 1]
        xy_copies.append(send(source, target, xy_sems, slot, (i, j, 0)))

    plan = plan_ref[...].astype(f32)
    cap = plan.shape[1]
    leaving = FACES * cap
    wide = jnp.concatenate(
        [jnp.broadcast_to(plan[q : q + 1], (cap, cap)) for q in range(FACES)], axis=0
    )
    diagonal = (iota((leaving, cap), 0) & (cap - 1)) == iota((leaving, cap), 1)
    chosen = jnp.sum(jnp.where(diagonal, wide, 0.0), axis=1, keepdims=True)
    picked = jnp.where(iota((leaving, count), 1).astype(f32) == chosen, 1.0, 0.0).astype(f32)
    taken = jnp.sum(picked, axis=0, keepdims=True)
    picker = jnp.concatenate([picked, jnp.zeros((128 - leaving, count), f32)], axis=0).astype(bf16)
    full = jnp.concatenate([record, anchor, living, jnp.zeros((2, count), f32)], axis=0)

    def thirds(value):
        high = value.astype(bf16).astype(f32)
        rest = value - high
        middle = rest.astype(bf16).astype(f32)
        return jnp.concatenate([high, middle, rest - middle], axis=0).astype(bf16)

    def pick(dot, value):
        got = dot(thirds(value), picker)
        return got[0:32] + got[32:64] + got[64:96]

    some = pick(dot_nt, full)
    some_tables = axis_tables(some[26:29], some[21:24])
    fill_tables(some_high, some_low, some_tables)

    for copy in xy_copies:
        copy.wait()
    near8 = iota((8, 128), 1) < EDGE
    partial = grid_ref[...]
    low_side = open_side(y_recv[0])
    high_side = open_side(y_recv[1])
    middle = jnp.zeros((8, LANES - 256), f32)
    low_rows = x_recv[0] + jnp.concatenate(
        [c_recv[0], middle, jnp.where(near8, c_recv[1], 0.0)], axis=1
    )
    high_rows = x_recv[1] + jnp.concatenate(
        [c_recv[2], middle, jnp.where(near8, c_recv[3], 0.0)], axis=1
    )
    totals = jnp.concatenate(
        [
            partial[:, 0:128] + low_side,
            partial[:, 128 : LANES - 128],
            partial[:, LANES - 128 :] + high_side,
        ],
        axis=1,
    )
    totals = jnp.concatenate(
        [totals[0:8] + low_rows, totals[8 : ROWS - 8], totals[ROWS - 8 :] + high_rows], axis=0
    )
    channel = iota((ROWS, LANES), 0) & 3
    mass_of = jnp.where(
        channel == 1,
        pltpu.roll(totals, 1, 0),
        jnp.where(channel == 2, pltpu.roll(totals, 2, 0), pltpu.roll(totals, 3, 0)),
    )
    velocity = totals / jnp.maximum(mass_of, mass_floor)
    velocity = jnp.where(channel == 3, velocity - time_step * gravity, velocity)
    velocity = jnp.where(channel == 0, 0.0, velocity)
    velocity = jnp.concatenate([velocity, velocity * lane_y, velocity * lane_z], axis=0)

    read_back(
        leave_ref, some, some[26:29], some[29:30], some_tables, some_high, some_low, velocity
    )
    m_send[...] = turned(leave_ref[...])[:leaving].reshape(FACES, cap, 128)
    m_steps = ((1, 0, 0), (-1, 0, 0), (0, 1, 0), (0, -1, 0), (0, 0, 1), (0, 0, -1))
    m_copies = [
        send(m_send.at[slot], come_ref.at[slot], m_sems, slot, step)
        for slot, step in enumerate(m_steps)
    ]
    read_back(new_ref, record, anchor, living, tables, high_ref, low_ref, velocity)
    for copy in m_copies:
        copy.wait()
    placed = pick(dot_nn, turned(come_ref[...].reshape(leaving, 128))[:32])
    out_ref[...] = jnp.where(taken > 0.0, placed, new_ref[...])[0:26]


def body(sizes, particles, block_ids, node_offsets, live_count, migrations):
    count = particles.shape[1]
    vmem = pl.BlockSpec(memory_space=pltpu.VMEM)
    return pl.pallas_call(
        functools.partial(kernel, sizes),
        out_shape=pltpu.VMEM(particles.shape, f32),
        in_specs=[pl.BlockSpec(memory_space=pltpu.HBM)] * 5,
        out_specs=vmem,
        scratch_shapes=[
            pltpu.SMEM((1,), jnp.int32),
            pltpu.VMEM(particles.shape, f32),
            pltpu.VMEM((1, count), jnp.int32),
            pltpu.VMEM((1, count), jnp.int32),
            pltpu.VMEM(migrations.shape, jnp.int32),
            pltpu.SemaphoreType.DMA((5,)),
            pltpu.VMEM((LANES, count), bf16),
            pltpu.VMEM((LANES, count), bf16),
            pltpu.VMEM((128, count), bf16),
            pltpu.VMEM((128, count), bf16),
            pltpu.VMEM((LANES, 128), bf16),
            pltpu.VMEM((LANES, 128), bf16),
            pltpu.VMEM((ROWS, LANES), f32),
            pltpu.VMEM((ROWS, 128), f32),
            pltpu.VMEM((2, ROWS, 128), f32),
            pltpu.VMEM((2, 8, LANES), f32),
            pltpu.VMEM((2, FOLD, 128), f32),
            pltpu.VMEM((2, FOLD, 128), f32),
            pltpu.VMEM((4, 8, 128), f32),
            pltpu.VMEM((32, 128), f32),
            pltpu.VMEM((FACES, migrations.shape[1], 128), f32),
            pltpu.VMEM((FACES, migrations.shape[1], 128), f32),
            pltpu.VMEM((32, count), f32),
            pltpu.SemaphoreType.DMA((2, 2)),
            pltpu.SemaphoreType.DMA((2, 8)),
            pltpu.SemaphoreType.DMA((2, 6)),
        ],
        compiler_params=pltpu.CompilerParams(
            collective_id=0, has_side_effects=True, vmem_limit_bytes=60 * 1024 * 1024
        ),
        name="substep",
    )(
        live_count,
        particles,
        block_ids.reshape(1, count),
        node_offsets.reshape(1, count),
        migrations,
    )


def solution(mesh):
    sizes = tuple(mesh.shape[name] for name in AXES)
    return jax.shard_map(
        functools.partial(body, sizes),
        mesh=mesh,
        in_specs=(
            P(None, AXES),
            P(AXES),
            P(AXES),
            P(AXES),
            P(None, AXES),
        ),
        out_specs=P(None, AXES),
        check_vma=False,
    )
```

```python
import functools

import jax
import jax.numpy as jnp
from jax import lax
from jax.experimental import pallas as pl
from jax.experimental.pallas import tpu as pltpu
from jax.sharding import PartitionSpec as P

BLK = 2
AXES = ("gx", "gy", "gz")
SPAN = 8 * BLK + 2
STRIDE = 24
ROWS = 4 * SPAN
LANES = 512
USED = STRIDE * SPAN
EDGE = 2 * STRIDE
FOLD = 40
CENTRE = 0.5 * (SPAN - 1)
FACES = 6

time_step = 0.05
stress_gain = 0.2
shear_zero = 5.0
bulk_zero = 5.0
harden_rate = 10.0
mass_floor = 0.1
gravity = 9.8

f32 = jnp.float32
bf16 = jnp.bfloat16
MESH = pl.DeviceIdType.MESH


def iota(shape, dim):
    return lax.broadcasted_iota(jnp.int32, shape, dim)


def split(value):
    high = value.astype(bf16)
    return high, (value - high.astype(f32)).astype(bf16)


def stacked(value):
    high = value.astype(bf16).astype(f32)
    return jnp.concatenate([high, value - high], axis=0).astype(bf16)


def dot_nt(left, right):
    return lax.dot_general(left, right, (((1,), (1,)), ((), ())), preferred_element_type=f32)


def dot_nn(left, right):
    return lax.dot_general(left, right, (((1,), (0,)), ((), ())), preferred_element_type=f32)


def contract(dot, left, right_high, right_low):
    rows = left.shape[0]
    both = dot(stacked(left), right_high)
    return both[:rows] + both[rows:] + dot(left.astype(bf16), right_low)


def spline(place, anchor, fraction):
    apart = (place - anchor) - fraction
    size = jnp.abs(apart)
    outer = jnp.maximum(1.5 - size, 0.0)
    inner = jnp.maximum(0.5 - size, 0.0)
    weight = 0.5 * outer * outer - 1.5 * inner * inner
    return weight, weight * apart


def axis_tables(anchor, fraction):
    count = fraction.shape[1]
    line = iota((STRIDE, count), 0).astype(f32)
    line_x = jnp.right_shift(iota((ROWS, count), 0), 2).astype(f32)
    return (
        spline(line_x, anchor[0:1], fraction[0:1]),
        spline(line, anchor[1:2], fraction[1:2]),
        spline(line, anchor[2:3], fraction[2:3]),
    )


def store_pair(high_ref, low_ref, row, outer_line, inner_line, picks):
    pair = jnp.concatenate([outer_line[p : p + 1] * inner_line for p in picks], axis=0)
    high, low = split(pair)
    high_ref[row : row + EDGE, :] = high
    low_ref[row : row + EDGE, :] = low


def fill_tables(high_ref, low_ref, tables):
    _, (weight_y, _), (weight_z, _) = tables
    count = weight_y.shape[1]
    for pair in range(SPAN // 2):
        store_pair(high_ref, low_ref, EDGE * pair, weight_y, weight_z, (2 * pair, 2 * pair + 1))
    for ref in (high_ref, low_ref):
        ref[USED:LANES, :] = jnp.zeros((LANES - USED, count), bf16)


def fill_masks(gather_ref, spread_ref):
    lane = iota((128, LANES), 1)
    row = iota((128, LANES), 0)
    line = jnp.right_shift(lane * 2731, 16)
    place = lane - STRIDE * line
    k = row & 3
    same = (jnp.right_shift(row, 2) == line) & (line < SPAN)
    near = jnp.where(k < 2, k, k + (SPAN - 4))
    far = jnp.where(k < 2, k + (SPAN - 2), k - 2)
    gather_ref[...] = jnp.where(same & (place == near), 1.0, 0.0).astype(bf16)
    spread_ref[...] = jnp.where(same & (place == far), 1.0, 0.0).astype(bf16)


def pack_edges(face):
    group = jnp.right_shift(iota((8, 128), 1), 3)
    tiles = []
    for start in (4 * (SPAN - 2), 0):
        tile = jnp.zeros((8, 128), f32)
        for g in range(ROWS // 8):
            rolled = pltpu.roll(face[8 * g : 8 * g + 8], (8 * g - start) % 128, 1)
            tile = jnp.where(group == g, rolled, tile)
        tiles.append(tile)
    return tiles


def lane_places(lanes):
    lane = iota((1, lanes), 1)
    line = jnp.right_shift(lane * 2731, 16)
    return line.astype(f32) - CENTRE, (lane - STRIDE * line).astype(f32) - CENTRE


def combine(parts, place_y, place_z):
    return parts[:ROWS] + place_y * parts[ROWS : 2 * ROWS] + place_z * parts[2 * ROWS :]


def product(left, right):
    return [
        [
            left[i][0] * right[0][j] + left[i][1] * right[1][j] + left[i][2] * right[2][j]
            for j in range(3)
        ]
        for i in range(3)
    ]


def transposed(matrix):
    return [[matrix[j][i] for j in range(3)] for i in range(3)]


def pack(row):
    count = row.shape[1]
    return jnp.concatenate([row[:, s : s + 128] for s in range(0, count, 128)], axis=0)


def unpack(block):
    return jnp.concatenate([block[s : s + 1] for s in range(block.shape[0])], axis=1)


def stress(deform, plastic):
    rotation = deform
    for _ in range(5):
        inner = product(transposed(rotation), rotation)
        inner = [[(3.0 - inner[i][j]) if i == j else -inner[i][j] for j in range(3)] for i in range(3)]
        rotation = product(rotation, inner)
        rotation = [[0.5 * entry for entry in line] for line in rotation]
    f = deform
    volume = (
        f[0][0] * (f[1][1] * f[2][2] - f[1][2] * f[2][1])
        - f[0][1] * (f[1][0] * f[2][2] - f[1][2] * f[2][0])
        + f[0][2] * (f[1][0] * f[2][1] - f[1][1] * f[2][0])
    )
    harden = jnp.exp(harden_rate * (1.0 - plastic))
    shear = 2.0 * shear_zero * harden
    bulk = bulk_zero * harden * (volume - 1.0) * volume
    apart = [[f[i][j] - rotation[i][j] for j in range(3)] for i in range(3)]
    tau = product(apart, transposed(f))
    return [
        [shear * tau[i][j] + bulk if i == j else shear * tau[i][j] for j in range(3)]
        for i in range(3)
    ]


def read_back(out_ref, record, anchor, living, tables, high_ref, low_ref, velocity):
    count = record.shape[1]
    (weight_x, shift_x), _, _ = tables
    reads = contract(dot_nn, velocity, high_ref[...], low_ref[...])

    def fold(value):
        total = value[0:8]
        for row in range(8, ROWS, 8):
            total = total + value[row : row + 8]
        return total[0:4] + total[4:8]

    first = reads[:ROWS]
    speed = fold(weight_x * first) * living
    place = anchor + record[21:24] - CENTRE
    along = [
        4.0 * living * fold(shift_x * first),
        4.0 * (living * fold(weight_x * reads[ROWS : 2 * ROWS]) - place[1:2] * speed),
        4.0 * (living * fold(weight_x * reads[2 * ROWS :]) - place[2:3] * speed),
    ]
    out_ref[0:3, :] = speed[1:4]
    deform = [record[12 + 3 * k : 15 + 3 * k] for k in range(3)]
    for i in range(3):
        push = jnp.zeros((3, count), f32)
        for j in range(3):
            entry = along[j][1 + i : 2 + i]
            out_ref[3 + 3 * i + j : 4 + 3 * i + j, :] = entry
            push = push + entry * deform[j]
        out_ref[12 + 3 * i : 15 + 3 * i, :] = deform[i] * living + time_step * push
    out_ref[21:24, :] = record[21:24] * living + time_step * speed[1:4]
    out_ref[24:26, :] = record[24:26] * living
    out_ref[26:32, :] = jnp.zeros((6, count), f32)


def pack_side(tile):
    rest = jnp.concatenate([tile[FOLD:], jnp.zeros((2 * FOLD - ROWS, 128), f32)], axis=0)
    return jnp.where(iota((FOLD, 128), 1) < 64, tile[:FOLD], pltpu.roll(rest, 64, 1))


def open_side(packed):
    rest = pltpu.roll(packed, 64, 1)[: ROWS - FOLD]
    full = jnp.concatenate([packed, rest], axis=0)
    return jnp.where(iota((ROWS, 128), 1) < EDGE, full, 0.0)


def turned(value):
    rows = jnp.zeros((128 - value.shape[0], 128), f32)
    return jnp.concatenate([value, rows], axis=0).T


def kernel(
    sizes,
    live_hbm,
    record_hbm,
    block_hbm,
    offset_hbm,
    plan_hbm,
    out_ref,
    live_ref,
    record_ref,
    block_ref,
    offset_ref,
    plan_ref,
    in_sems,
    high_ref,
    low_ref,
    gather_ref,
    spread_ref,
    some_high,
    some_low,
    grid_ref,
    z_send,
    z_recv,
    e_send,
    e_recv,
    x_recv,
    y_send,
    y_recv,
    c_recv,
    leave_ref,
    m_send,
    come_ref,
    new_ref,
    z_sems,
    xy_sems,
    m_sems,
):
    operands = (
        (record_hbm, record_ref),
        (block_hbm, block_ref),
        (offset_hbm, offset_ref),
        (live_hbm, live_ref),
        (plan_hbm, plan_ref),
    )
    in_copies = [
        pltpu.make_async_copy(source, target, in_sems.at[slot])
        for slot, (source, target) in enumerate(operands)
    ]
    for copy in in_copies:
        copy.start()
    me = [lax.axis_index(name) for name in AXES]

    def at(*step):
        return tuple(
            lax.rem(me[a] + step[a] + sizes[a], sizes[a]) if step[a] else me[a] for a in range(3)
        )

    pair_z = sizes[2] == 2
    z_steps = ((0, 0, 1),) if pair_z else ((0, 0, 1), (0, 0, -1))
    xy_steps = tuple((i, j, 0) for i in (0, 1, -1) for j in (1, -1, 0) if i or j)
    barrier = pltpu.get_barrier_semaphore()
    around = xy_steps + tuple((i, j, k) for _, _, k in z_steps for i, j, _ in ((0, 0, 0),) + xy_steps)
    for step in around:
        pl.semaphore_signal(barrier, inc=1, device_id=at(*step), device_id_type=MESH)

    fill_masks(gather_ref, spread_ref)
    for copy in in_copies:
        copy.wait()
    count = record_ref.shape[1]
    record = record_ref[...]
    fraction = record[21:24]
    blocks = block_ref[...]
    offsets = offset_ref[...]
    anchor = (
        jnp.concatenate(
            [
                8 * jnp.right_shift(blocks, 2) + jnp.right_shift(offsets, 6),
                8 * (jnp.right_shift(blocks, 1) & 1) + (jnp.right_shift(offsets, 3) & 7),
                8 * (blocks & 1) + (offsets & 7),
            ],
            axis=0,
        )
        + 1
    ).astype(f32)
    living = jnp.where(iota((1, count), 1) < live_ref[0], 1.0, 0.0).astype(f32)

    tables = axis_tables(anchor, fraction)
    fill_tables(high_ref, low_ref, tables)

    plastic = pack(record[25:26])
    deform = [[pack(record[12 + 3 * i + j : 13 + 3 * i + j]) for j in range(3)] for i in range(3)]
    tau = stress(deform, plastic)
    mass = record[24:25]
    held = mass * living
    coupling = [
        [
            (mass * record[3 + 3 * i + j : 4 + 3 * i + j] - stress_gain * unpack(tau[i][j])) * living
            for j in range(3)
        ]
        for i in range(3)
    ]
    none = jnp.zeros((1, count), f32)
    places = anchor + fraction - CENTRE
    momentum = [
        held * record[i : i + 1] - coupling[i][1] * places[1:2] - coupling[i][2] * places[2:3]
        for i in range(3)
    ]
    base = jnp.concatenate([held] + momentum + [held] + momentum, axis=0)
    pushes = [
        jnp.concatenate([none, coupling[0][j], coupling[1][j], coupling[2][j]] * 2, axis=0)
        for j in range(3)
    ]
    weight_x, shift_x = tables[0]
    tiles = range(0, ROWS, 8)
    left = jnp.concatenate(
        [base * weight_x[r : r + 8] + pushes[0] * shift_x[r : r + 8] for r in tiles]
        + [pushes[1] * weight_x[r : r + 8] for r in tiles]
        + [pushes[2] * weight_x[r : r + 8] for r in tiles],
        axis=0,
    )

    def send(source, target, sems, slot, step):
        copy = pltpu.make_async_remote_copy(
            src_ref=source,
            dst_ref=target,
            send_sem=sems.at[0, slot],
            recv_sem=sems.at[1, slot],
            device_id=at(*step),
            device_id_type=MESH,
        )
        copy.start()
        return copy

    lane_y, lane_z = lane_places(LANES)
    partial = combine(contract(dot_nt, left, high_ref[...], low_ref[...]), lane_y, lane_z)
    grid_ref[...] = partial
    y_send[0] = pack_side(partial[:, LANES - 128 :])
    y_send[1] = pack_side(partial[:, 0:128])
    pl.semaphore_wait(barrier, len(around))

    rows_of = {1: pl.ds(ROWS - 8, 8), -1: pl.ds(0, 8)}
    lanes_of = {1: pl.ds(LANES - 128, 128), -1: pl.ds(0, 128)}
    xy_copies = []
    for slot, (i, j, _) in enumerate(xy_steps):
        if i and j:
            source = grid_ref.at[rows_of[i], lanes_of[j]]
            target = c_recv.at[(0 if i > 0 else 2) + (0 if j > 0 else 1)]
        elif i:
            source = grid_ref.at[rows_of[i], :]
            target = x_recv.at[0 if i > 0 else 1]
        else:
            source = y_send.at[0 if j > 0 else 1]
            target = y_recv.at[0 if j > 0 else 1]
        xy_copies.append(send(source, target, xy_sems, slot, (i, j, 0)))

    face = dot_nt(stacked(partial), gather_ref[...])
    face = face[:ROWS] + face[ROWS:]
    z_send[...] = face
    e_send[0], e_send[1] = pack_edges(face)
    z_copies = []
    for slot, (_, _, k) in enumerate(z_steps):
        z_copies.append(send(z_send, z_recv.at[slot], z_sems, 9 * slot, (0, 0, k)))
        for number, (i, j, _) in enumerate(xy_steps):
            source = z_send.at[rows_of[i]] if i else e_send.at[0 if j > 0 else 1]
            target = e_recv.at[slot, number]
            z_copies.append(send(source, target, z_sems, 9 * slot + 1 + number, (i, j, k)))

    plan = plan_ref[...].astype(f32)
    cap = plan.shape[1]
    leaving = FACES * cap
    wide = jnp.concatenate(
        [jnp.broadcast_to(plan[q : q + 1], (cap, cap)) for q in range(FACES)], axis=0
    )
    diagonal = (iota((leaving, cap), 0) & (cap - 1)) == iota((leaving, cap), 1)
    chosen = jnp.sum(jnp.where(diagonal, wide, 0.0), axis=1, keepdims=True)
    picked = jnp.where(iota((leaving, count), 1).astype(f32) == chosen, 1.0, 0.0).astype(f32)
    taken = jnp.sum(picked, axis=0, keepdims=True)
    picker = jnp.concatenate([picked, jnp.zeros((128 - leaving, count), f32)], axis=0).astype(bf16)
    full = jnp.concatenate([record, anchor, living, jnp.zeros((2, count), f32)], axis=0)

    def thirds(value):
        high = value.astype(bf16).astype(f32)
        rest = value - high
        middle = rest.astype(bf16).astype(f32)
        return jnp.concatenate([high, middle, rest - middle], axis=0).astype(bf16)

    def pick(dot, value):
        got = dot(thirds(value), picker)
        return got[0:32] + got[32:64] + got[64:96]

    some = pick(dot_nt, full)
    some_tables = axis_tables(some[26:29], some[21:24])
    fill_tables(some_high, some_low, some_tables)

    for copy in z_copies:
        copy.wait()

    def from_z(ref, *index):
        if pair_z:
            return ref[(0,) + index]
        value = ref[(1,) + index]
        return jnp.where((iota(value.shape, 1) & 3) < 2, value, ref[(0,) + index])

    face_lane = iota((8, 128), 1)
    face_side = {1: face_lane < 8, -1: (face_lane >= 4 * (SPAN - 2)) & (face_lane < 4 * SPAN)}
    face_start = {1: 0, -1: 4 * (SPAN - 2)}
    edge = {(i, j): from_z(e_recv, number) for number, (i, j, _) in enumerate(xy_steps)}
    shared = from_z(z_recv)
    shared = [shared[8 * g : 8 * g + 8] for g in range(ROWS // 8)]
    for g in range(ROWS // 8):
        for j in (1, -1):
            rolled = pltpu.roll(edge[0, j], (face_start[j] - 8 * g) % 128, 1)
            shared[g] = jnp.where(face_side[j], shared[g] + rolled, shared[g])
    for i in (1, -1):
        g = 0 if i > 0 else ROWS // 8 - 1
        shared[g] = shared[g] + edge[i, 0]
        for j in (1, -1):
            rolled = pltpu.roll(edge[i, j], (face_start[j] - face_start[-j]) % 128, 1)
            shared[g] = jnp.where(face_side[j], shared[g] + rolled, shared[g])
    spread_sum = dot_nn(stacked(jnp.concatenate(shared, axis=0)), spread_ref[...])
    partial = grid_ref[...] + spread_sum[:ROWS] + spread_sum[ROWS:]

    for copy in xy_copies:
        copy.wait()
    near8 = iota((8, 128), 1) < EDGE
    low_side = open_side(y_recv[0])
    high_side = open_side(y_recv[1])
    middle = jnp.zeros((8, LANES - 256), f32)
    low_rows = x_recv[0] + jnp.concatenate(
        [c_recv[0], middle, jnp.where(near8, c_recv[1], 0.0)], axis=1
    )
    high_rows = x_recv[1] + jnp.concatenate(
        [c_recv[2], middle, jnp.where(near8, c_recv[3], 0.0)], axis=1
    )
    totals = jnp.concatenate(
        [
            partial[:, 0:128] + low_side,
            partial[:, 128 : LANES - 128],
            partial[:, LANES - 128 :] + high_side,
        ],
        axis=1,
    )
    totals = jnp.concatenate(
        [totals[0:8] + low_rows, totals[8 : ROWS - 8], totals[ROWS - 8 :] + high_rows], axis=0
    )
    channel = iota((ROWS, LANES), 0) & 3
    mass_of = jnp.where(
        channel == 1,
        pltpu.roll(totals, 1, 0),
        jnp.where(channel == 2, pltpu.roll(totals, 2, 0), pltpu.roll(totals, 3, 0)),
    )
    velocity = totals / jnp.maximum(mass_of, mass_floor)
    velocity = jnp.where(channel == 3, velocity - time_step * gravity, velocity)
    velocity = jnp.where(channel == 0, 0.0, velocity)
    velocity = jnp.concatenate([velocity, velocity * lane_y, velocity * lane_z], axis=0)

    read_back(
        leave_ref, some, some[26:29], some[29:30], some_tables, some_high, some_low, velocity
    )
    m_send[...] = turned(leave_ref[...])[:leaving].reshape(FACES, cap, 128)
    m_steps = ((1, 0, 0), (-1, 0, 0), (0, 1, 0), (0, -1, 0), (0, 0, 1), (0, 0, -1))
    m_copies = [
        send(m_send.at[slot], come_ref.at[slot], m_sems, slot, step)
        for slot, step in enumerate(m_steps)
    ]
    read_back(new_ref, record, anchor, living, tables, high_ref, low_ref, velocity)
    for copy in m_copies:
        copy.wait()
    placed = pick(dot_nn, turned(come_ref[...].reshape(leaving, 128))[:32])
    out_ref[...] = jnp.where(taken > 0.0, placed, new_ref[...])[0:26]


def body(sizes, particles, block_ids, node_offsets, live_count, migrations):
    count = particles.shape[1]
    vmem = pl.BlockSpec(memory_space=pltpu.VMEM)
    return pl.pallas_call(
        functools.partial(kernel, sizes),
        out_shape=pltpu.VMEM(particles.shape, f32),
        in_specs=[pl.BlockSpec(memory_space=pltpu.HBM)] * 5,
        out_specs=vmem,
        scratch_shapes=[
            pltpu.SMEM((1,), jnp.int32),
            pltpu.VMEM(particles.shape, f32),
            pltpu.VMEM((1, count), jnp.int32),
            pltpu.VMEM((1, count), jnp.int32),
            pltpu.VMEM(migrations.shape, jnp.int32),
            pltpu.SemaphoreType.DMA((5,)),
            pltpu.VMEM((LANES, count), bf16),
            pltpu.VMEM((LANES, count), bf16),
            pltpu.VMEM((128, LANES), bf16),
            pltpu.VMEM((128, LANES), bf16),
            pltpu.VMEM((LANES, 128), bf16),
            pltpu.VMEM((LANES, 128), bf16),
            pltpu.VMEM((ROWS, LANES), f32),
            pltpu.VMEM((ROWS, 128), f32),
            pltpu.VMEM((2, ROWS, 128), f32),
            pltpu.VMEM((2, 8, 128), f32),
            pltpu.VMEM((2, 8, 8, 128), f32),
            pltpu.VMEM((2, 8, LANES), f32),
            pltpu.VMEM((2, FOLD, 128), f32),
            pltpu.VMEM((2, FOLD, 128), f32),
            pltpu.VMEM((4, 8, 128), f32),
            pltpu.VMEM((32, 128), f32),
            pltpu.VMEM((FACES, migrations.shape[1], 128), f32),
            pltpu.VMEM((FACES, migrations.shape[1], 128), f32),
            pltpu.VMEM((32, count), f32),
            pltpu.SemaphoreType.DMA((2, 18)),
            pltpu.SemaphoreType.DMA((2, 8)),
            pltpu.SemaphoreType.DMA((2, 6)),
        ],
        compiler_params=pltpu.CompilerParams(
            collective_id=0, has_side_effects=True, vmem_limit_bytes=60 * 1024 * 1024
        ),
        name="substep",
    )(
        live_count,
        particles,
        block_ids.reshape(1, count),
        node_offsets.reshape(1, count),
        migrations,
    )


def solution(mesh):
    sizes = tuple(mesh.shape[name] for name in AXES)
    return jax.shard_map(
        functools.partial(body, sizes),
        mesh=mesh,
        in_specs=(
            P(None, AXES),
            P(AXES),
            P(AXES),
            P(AXES),
            P(None, AXES),
        ),
        out_specs=P(None, AXES),
        check_vma=False,
    )
```

```python
import functools

import jax
import jax.numpy as jnp
from jax import lax
from jax.experimental import pallas as pl
from jax.experimental.pallas import tpu as pltpu
from jax.sharding import PartitionSpec as P

BLK = 2
AXES = ("gx", "gy", "gz")
SPAN = 8 * BLK + 2
STRIDE = 24
ROWS = 4 * SPAN
LANES = 512
USED = STRIDE * SPAN
EDGE = 2 * STRIDE
SIDE = STRIDE + SPAN
THIRD = ROWS // 3
HEAD = 40
FACE_ROWS = HEAD + 8
CENTRE = 0.5 * (SPAN - 1)
FACES = 6

time_step = 0.05
stress_gain = 0.2
shear_zero = 5.0
bulk_zero = 5.0
harden_rate = 10.0
mass_floor = 0.1
gravity = 9.8

f32 = jnp.float32
bf16 = jnp.bfloat16
MESH = pl.DeviceIdType.MESH


def iota(shape, dim):
    return lax.broadcasted_iota(jnp.int32, shape, dim)


def split(value):
    high = value.astype(bf16)
    return high, (value - high.astype(f32)).astype(bf16)


def stacked(value):
    high = value.astype(bf16).astype(f32)
    return jnp.concatenate([high, value - high], axis=0).astype(bf16)


def dot_nt(left, right):
    return lax.dot_general(left, right, (((1,), (1,)), ((), ())), preferred_element_type=f32)


def dot_nn(left, right):
    return lax.dot_general(left, right, (((1,), (0,)), ((), ())), preferred_element_type=f32)


def contract(dot, left, right_high, right_low):
    rows = left.shape[0]
    both = dot(stacked(left), right_high)
    return both[:rows] + both[rows:] + dot(left.astype(bf16), right_low)


def spline(place, anchor, fraction):
    apart = (place - anchor) - fraction
    size = jnp.abs(apart)
    outer = jnp.maximum(1.5 - size, 0.0)
    inner = jnp.maximum(0.5 - size, 0.0)
    weight = 0.5 * outer * outer - 1.5 * inner * inner
    return weight, weight * apart


def axis_tables(anchor, fraction):
    count = fraction.shape[1]
    line = iota((STRIDE, count), 0).astype(f32)
    line_x = jnp.right_shift(iota((ROWS, count), 0), 2).astype(f32)
    return (
        spline(line_x, anchor[0:1], fraction[0:1]),
        spline(line, anchor[1:2], fraction[1:2]),
        spline(line, anchor[2:3], fraction[2:3]),
    )


def store_pair(high_ref, low_ref, row, outer_line, inner_line, picks):
    pair = jnp.concatenate([outer_line[p : p + 1] * inner_line for p in picks], axis=0)
    high, low = split(pair)
    high_ref[row : row + EDGE, :] = high
    low_ref[row : row + EDGE, :] = low


def fill_tables(high_ref, low_ref, tables):
    _, (weight_y, _), (weight_z, _) = tables
    count = weight_y.shape[1]
    for pair in range(SPAN // 2):
        store_pair(high_ref, low_ref, EDGE * pair, weight_y, weight_z, (2 * pair, 2 * pair + 1))
    for ref in (high_ref, low_ref):
        ref[USED:LANES, :] = jnp.zeros((LANES - USED, count), bf16)


def fill_masks(gather_ref, spread_ref):
    lane = iota((128, LANES), 1)
    row = iota((128, LANES), 0)
    line = jnp.right_shift(lane * 2731, 16)
    place = lane - STRIDE * line
    k = row & 3
    same = (jnp.right_shift(row, 2) == line) & (line < SPAN)
    near = jnp.where(k < 2, k, k + (SPAN - 4))
    far = jnp.where(k < 2, k + (SPAN - 2), k - 2)
    gather_ref[...] = jnp.where(same & (place == near), 1.0, 0.0).astype(bf16)
    spread_ref[...] = jnp.where(same & (place == far), 1.0, 0.0).astype(bf16)


def pack_edges(face):
    group = jnp.right_shift(iota((8, 128), 1), 3)
    tiles = []
    for start in (4 * (SPAN - 2), 0):
        tile = jnp.zeros((8, 128), f32)
        for g in range(ROWS // 8):
            rolled = pltpu.roll(face[8 * g : 8 * g + 8], (8 * g - start) % 128, 1)
            tile = jnp.where(group == g, rolled, tile)
        tiles.append(tile)
    return tiles


def lane_places(lanes):
    lane = iota((1, lanes), 1)
    line = jnp.right_shift(lane * 2731, 16)
    return line.astype(f32) - CENTRE, (lane - STRIDE * line).astype(f32) - CENTRE


def combine(parts, place_y, place_z):
    return parts[:ROWS] + place_y * parts[ROWS : 2 * ROWS] + place_z * parts[2 * ROWS :]


def product(left, right):
    return [
        [
            left[i][0] * right[0][j] + left[i][1] * right[1][j] + left[i][2] * right[2][j]
            for j in range(3)
        ]
        for i in range(3)
    ]


def transposed(matrix):
    return [[matrix[j][i] for j in range(3)] for i in range(3)]


def pack(row):
    count = row.shape[1]
    return jnp.concatenate([row[:, s : s + 128] for s in range(0, count, 128)], axis=0)


def unpack(block):
    return jnp.concatenate([block[s : s + 1] for s in range(block.shape[0])], axis=1)


def stress(deform, plastic):
    rotation = deform
    for _ in range(5):
        inner = product(transposed(rotation), rotation)
        inner = [[(3.0 - inner[i][j]) if i == j else -inner[i][j] for j in range(3)] for i in range(3)]
        rotation = product(rotation, inner)
        rotation = [[0.5 * entry for entry in line] for line in rotation]
    f = deform
    volume = (
        f[0][0] * (f[1][1] * f[2][2] - f[1][2] * f[2][1])
        - f[0][1] * (f[1][0] * f[2][2] - f[1][2] * f[2][0])
        + f[0][2] * (f[1][0] * f[2][1] - f[1][1] * f[2][0])
    )
    harden = jnp.exp(harden_rate * (1.0 - plastic))
    shear = 2.0 * shear_zero * harden
    bulk = bulk_zero * harden * (volume - 1.0) * volume
    apart = [[f[i][j] - rotation[i][j] for j in range(3)] for i in range(3)]
    tau = product(apart, transposed(f))
    return [
        [shear * tau[i][j] + bulk if i == j else shear * tau[i][j] for j in range(3)]
        for i in range(3)
    ]


def read_back(out_ref, record, anchor, living, tables, high_ref, low_ref, velocity):
    count = record.shape[1]
    (weight_x, shift_x), _, _ = tables
    reads = contract(dot_nn, velocity, high_ref[...], low_ref[...])

    def fold(value):
        total = value[0:8]
        for row in range(8, ROWS, 8):
            total = total + value[row : row + 8]
        return total[0:4] + total[4:8]

    first = reads[:ROWS]
    speed = fold(weight_x * first) * living
    place = anchor + record[21:24] - CENTRE
    along = [
        4.0 * living * fold(shift_x * first),
        4.0 * (living * fold(weight_x * reads[ROWS : 2 * ROWS]) - place[1:2] * speed),
        4.0 * (living * fold(weight_x * reads[2 * ROWS :]) - place[2:3] * speed),
    ]
    out_ref[0:3, :] = speed[1:4]
    deform = [record[12 + 3 * k : 15 + 3 * k] for k in range(3)]
    for i in range(3):
        push = jnp.zeros((3, count), f32)
        for j in range(3):
            entry = along[j][1 + i : 2 + i]
            out_ref[3 + 3 * i + j : 4 + 3 * i + j, :] = entry
            push = push + entry * deform[j]
        out_ref[12 + 3 * i : 15 + 3 * i, :] = deform[i] * living + time_step * push
    out_ref[21:24, :] = record[21:24] * living + time_step * speed[1:4]
    out_ref[24:26, :] = record[24:26] * living
    out_ref[26:32, :] = jnp.zeros((6, count), f32)


def pack_side(tile):
    lane = iota((THIRD, 128), 1)
    middle = pltpu.roll(tile[THIRD : 2 * THIRD], SIDE, 1)
    last = pltpu.roll(tile[2 * THIRD :], 2 * SIDE, 1)
    return jnp.where(lane < SIDE, tile[:THIRD], jnp.where(lane < 2 * SIDE, middle, last))


def open_side(packed):
    rolled = [packed] + [pltpu.roll(packed, 128 - g * SIDE, 1) for g in (1, 2)]
    return jnp.where(iota((ROWS, 128), 1) < SIDE, jnp.concatenate(rolled, axis=0), 0.0)


def pack_corner(tile):
    return jnp.where(iota((4, 128), 1) < 64, tile[0:4], pltpu.roll(tile[4:8], 64, 1))


def open_corner(packed):
    full = jnp.concatenate([packed, pltpu.roll(packed, 64, 1)], axis=0)
    return jnp.where(iota((8, 128), 1) < SIDE, full, 0.0)


def pack_face(face):
    rest = jnp.concatenate([face[HEAD:], jnp.zeros((2 * HEAD - ROWS, 128), f32)], axis=0)
    head = jnp.where(iota((HEAD, 128), 1) < 72, face[:HEAD], pltpu.roll(rest, 72, 1))
    group = jnp.right_shift(iota((8, 128), 1), 4)
    tail = jnp.zeros((8, 128), f32)
    for g in range((ROWS - HEAD) // 8):
        rolled = pltpu.roll(rest[8 * g : 8 * g + 8], (16 * g - 56) % 128, 1)
        tail = jnp.where(group == g, rolled, tail)
    return jnp.concatenate([head, tail], axis=0)


def open_face(packed):
    tiles = [packed[r : r + 8] for r in range(0, HEAD, 8)]
    tail = packed[HEAD:]
    lane = iota((8, 128), 1)
    for g in range((ROWS - HEAD) // 8):
        body_part = pltpu.roll(packed[8 * g : 8 * g + 8], 56, 1)
        tiles.append(jnp.where(lane < 56, body_part, pltpu.roll(tail, (56 - 16 * g) % 128, 1)))
    return tiles


def pack_line(tile, start):
    group = jnp.right_shift(iota((8, 128), 1), 3)
    row = iota((8, 128), 0)
    total = jnp.zeros((8, 128), f32)
    for r in range(8):
        rolled = pltpu.roll(tile, (8 * r - start) % 128, 1)
        total = jnp.where((group == r) & (row == r), rolled, total)
    return jnp.sum(total, axis=0, keepdims=True)


def open_line(packed, start):
    wide = jnp.broadcast_to(packed, (8, 128))
    row = iota((8, 128), 0)
    total = pltpu.roll(wide, start, 1) if start else wide
    for r in range(1, 8):
        total = jnp.where(row == r, pltpu.roll(wide, (start - 8 * r) % 128, 1), total)
    return total


def turned(value):
    rows = jnp.zeros((128 - value.shape[0], 128), f32)
    return jnp.concatenate([value, rows], axis=0).T


def kernel(
    sizes,
    live_hbm,
    record_hbm,
    block_hbm,
    offset_hbm,
    plan_hbm,
    out_ref,
    live_ref,
    record_ref,
    block_ref,
    offset_ref,
    plan_ref,
    in_sems,
    high_ref,
    low_ref,
    gather_ref,
    spread_ref,
    some_high,
    some_low,
    grid_ref,
    z_send,
    z_recv,
    e_send,
    e_recv,
    x_recv,
    y_send,
    y_recv,
    c_send,
    c_recv,
    l_send,
    l_recv,
    leave_ref,
    m_send,
    come_ref,
    new_ref,
    z_sems,
    xy_sems,
    m_sems,
):
    operands = (
        (record_hbm, record_ref),
        (block_hbm, block_ref),
        (offset_hbm, offset_ref),
        (live_hbm, live_ref),
        (plan_hbm, plan_ref),
    )
    in_copies = [
        pltpu.make_async_copy(source, target, in_sems.at[slot])
        for slot, (source, target) in enumerate(operands)
    ]
    for copy in in_copies:
        copy.start()
    me = [lax.axis_index(name) for name in AXES]

    def at(*step):
        return tuple(
            lax.rem(me[a] + step[a] + sizes[a], sizes[a]) if step[a] else me[a] for a in range(3)
        )

    pair_z = sizes[2] == 2
    z_steps = ((0, 0, 1),) if pair_z else ((0, 0, 1), (0, 0, -1))
    xy_steps = tuple((i, j, 0) for i in (0, 1, -1) for j in (1, -1, 0) if i or j)
    barrier = pltpu.get_barrier_semaphore()
    around = xy_steps + tuple((i, j, k) for _, _, k in z_steps for i, j, _ in ((0, 0, 0),) + xy_steps)
    for step in around:
        pl.semaphore_signal(barrier, inc=1, device_id=at(*step), device_id_type=MESH)

    fill_masks(gather_ref, spread_ref)
    for copy in in_copies:
        copy.wait()
    count = record_ref.shape[1]
    record = record_ref[...]
    fraction = record[21:24]
    blocks = block_ref[...]
    offsets = offset_ref[...]
    anchor = (
        jnp.concatenate(
            [
                8 * jnp.right_shift(blocks, 2) + jnp.right_shift(offsets, 6),
                8 * (jnp.right_shift(blocks, 1) & 1) + (jnp.right_shift(offsets, 3) & 7),
                8 * (blocks & 1) + (offsets & 7),
            ],
            axis=0,
        )
        + 1
    ).astype(f32)
    living = jnp.where(iota((1, count), 1) < live_ref[0], 1.0, 0.0).astype(f32)

    tables = axis_tables(anchor, fraction)
    fill_tables(high_ref, low_ref, tables)

    plastic = pack(record[25:26])
    deform = [[pack(record[12 + 3 * i + j : 13 + 3 * i + j]) for j in range(3)] for i in range(3)]
    tau = stress(deform, plastic)
    mass = record[24:25]
    held = mass * living
    coupling = [
        [
            (mass * record[3 + 3 * i + j : 4 + 3 * i + j] - stress_gain * unpack(tau[i][j])) * living
            for j in range(3)
        ]
        for i in range(3)
    ]
    none = jnp.zeros((1, count), f32)
    places = anchor + fraction - CENTRE
    momentum = [
        held * record[i : i + 1] - coupling[i][1] * places[1:2] - coupling[i][2] * places[2:3]
        for i in range(3)
    ]
    base = jnp.concatenate([held] + momentum + [held] + momentum, axis=0)
    pushes = [
        jnp.concatenate([none, coupling[0][j], coupling[1][j], coupling[2][j]] * 2, axis=0)
        for j in range(3)
    ]
    weight_x, shift_x = tables[0]
    tiles = range(0, ROWS, 8)
    left = jnp.concatenate(
        [base * weight_x[r : r + 8] + pushes[0] * shift_x[r : r + 8] for r in tiles]
        + [pushes[1] * weight_x[r : r + 8] for r in tiles]
        + [pushes[2] * weight_x[r : r + 8] for r in tiles],
        axis=0,
    )

    def send(source, target, sems, slot, step):
        copy = pltpu.make_async_remote_copy(
            src_ref=source,
            dst_ref=target,
            send_sem=sems.at[0, slot],
            recv_sem=sems.at[1, slot],
            device_id=at(*step),
            device_id_type=MESH,
        )
        copy.start()
        return copy

    lane_y, lane_z = lane_places(LANES)
    partial = combine(contract(dot_nt, left, high_ref[...], low_ref[...]), lane_y, lane_z)
    grid_ref[...] = partial
    y_send[0] = pack_side(partial[:, LANES - 128 :])
    y_send[1] = pack_side(partial[:, 0:128])
    pl.semaphore_wait(barrier, len(around))

    corners = ((1, 1), (1, -1), (-1, 1), (-1, -1))
    sides = ((0, 1), (0, -1), (1, 0), (-1, 0))
    last = {1: ROWS - 8, -1: 0}
    last_lane = {1: LANES - 128, -1: 0}
    last_face = {1: 4 * (SPAN - 2), -1: 0}
    for number, (i, j) in enumerate(corners):
        c_send[number] = pack_corner(
            partial[last[i] : last[i] + 8, last_lane[j] : last_lane[j] + 128]
        )
    xy_copies = []
    for slot, (i, j, _) in enumerate(xy_steps):
        if i and j:
            number = corners.index((i, j))
            source, target = c_send.at[number], c_recv.at[number]
        elif i:
            source = grid_ref.at[pl.ds(last[i], 8), :]
            target = x_recv.at[0 if i > 0 else 1]
        else:
            number = 0 if j > 0 else 1
            source, target = y_send.at[number], y_recv.at[number]
        xy_copies.append(send(source, target, xy_sems, slot, (i, j, 0)))

    face = dot_nt(stacked(partial), gather_ref[...])
    face = face[:ROWS] + face[ROWS:]
    z_send[...] = pack_face(face)
    z_copies = [
        send(z_send, z_recv.at[slot], z_sems, 9 * slot, (0, 0, k))
        for slot, (_, _, k) in enumerate(z_steps)
    ]
    e_send[0], e_send[1] = pack_edges(face)
    e_send[2] = face[last[1] : last[1] + 8]
    e_send[3] = face[last[-1] : last[-1] + 8]
    for slot, (_, _, k) in enumerate(z_steps):
        for number, (i, j) in enumerate(sides):
            target = e_recv.at[slot, number]
            z_copies.append(
                send(e_send.at[number], target, z_sems, 9 * slot + 1 + number, (i, j, k))
            )
    for number, (i, j) in enumerate(corners):
        l_send[number] = pack_line(face[last[i] : last[i] + 8], last_face[j])
    for slot, (_, _, k) in enumerate(z_steps):
        for number, (i, j) in enumerate(corners):
            target = l_recv.at[slot, number]
            z_copies.append(
                send(l_send.at[number], target, z_sems, 9 * slot + 5 + number, (i, j, k))
            )

    plan = plan_ref[...].astype(f32)
    cap = plan.shape[1]
    leaving = FACES * cap
    wide = jnp.concatenate(
        [jnp.broadcast_to(plan[q : q + 1], (cap, cap)) for q in range(FACES)], axis=0
    )
    diagonal = (iota((leaving, cap), 0) & (cap - 1)) == iota((leaving, cap), 1)
    chosen = jnp.sum(jnp.where(diagonal, wide, 0.0), axis=1, keepdims=True)
    picked = jnp.where(iota((leaving, count), 1).astype(f32) == chosen, 1.0, 0.0).astype(f32)
    taken = jnp.sum(picked, axis=0, keepdims=True)
    picker = jnp.concatenate([picked, jnp.zeros((128 - leaving, count), f32)], axis=0).astype(bf16)
    full = jnp.concatenate([record, anchor, living, jnp.zeros((2, count), f32)], axis=0)

    def thirds(value):
        high = value.astype(bf16).astype(f32)
        rest = value - high
        middle = rest.astype(bf16).astype(f32)
        return jnp.concatenate([high, middle, rest - middle], axis=0).astype(bf16)

    def pick(dot, value):
        got = dot(thirds(value), picker)
        return got[0:32] + got[32:64] + got[64:96]

    some = pick(dot_nt, full)
    some_tables = axis_tables(some[26:29], some[21:24])
    fill_tables(some_high, some_low, some_tables)

    for copy in z_copies:
        copy.wait()

    def from_z(ref, *index):
        if pair_z:
            return ref[(0,) + index]
        value = ref[(1,) + index]
        return jnp.where((iota(value.shape, 1) & 3) < 2, value, ref[(0,) + index])

    face_lane = iota((8, 128), 1)
    face_side = {1: face_lane < 8, -1: (face_lane >= 4 * (SPAN - 2)) & (face_lane < 4 * SPAN)}
    face_start = {1: 0, -1: 4 * (SPAN - 2)}
    edge = {step: from_z(e_recv, number) for number, step in enumerate(sides)}
    shared = open_face(from_z(z_recv))
    for g in range(ROWS // 8):
        for j in (1, -1):
            rolled = pltpu.roll(edge[0, j], (face_start[j] - 8 * g) % 128, 1)
            shared[g] = jnp.where(face_side[j], shared[g] + rolled, shared[g])
    for i in (1, -1):
        g = 0 if i > 0 else ROWS // 8 - 1
        shared[g] = shared[g] + edge[i, 0]
        for j in (1, -1):
            line = open_line(from_z(l_recv, corners.index((i, j))), face_start[j])
            shared[g] = jnp.where(face_side[j], shared[g] + line, shared[g])
    spread_sum = dot_nn(stacked(jnp.concatenate(shared, axis=0)), spread_ref[...])
    partial = grid_ref[...] + spread_sum[:ROWS] + spread_sum[ROWS:]

    for copy in xy_copies:
        copy.wait()
    low_side = open_side(y_recv[0])
    high_side = open_side(y_recv[1])
    middle = jnp.zeros((8, LANES - 256), f32)
    corner = [open_corner(c_recv[number]) for number in range(4)]
    low_rows = x_recv[0] + jnp.concatenate([corner[0], middle, corner[1]], axis=1)
    high_rows = x_recv[1] + jnp.concatenate([corner[2], middle, corner[3]], axis=1)
    totals = jnp.concatenate(
        [
            partial[:, 0:128] + low_side,
            partial[:, 128 : LANES - 128],
            partial[:, LANES - 128 :] + high_side,
        ],
        axis=1,
    )
    totals = jnp.concatenate(
        [totals[0:8] + low_rows, totals[8 : ROWS - 8], totals[ROWS - 8 :] + high_rows], axis=0
    )
    channel = iota((ROWS, LANES), 0) & 3
    mass_of = jnp.where(
        channel == 1,
        pltpu.roll(totals, 1, 0),
        jnp.where(channel == 2, pltpu.roll(totals, 2, 0), pltpu.roll(totals, 3, 0)),
    )
    velocity = totals / jnp.maximum(mass_of, mass_floor)
    velocity = jnp.where(channel == 3, velocity - time_step * gravity, velocity)
    velocity = jnp.where(channel == 0, 0.0, velocity)
    velocity = jnp.concatenate([velocity, velocity * lane_y, velocity * lane_z], axis=0)

    read_back(
        leave_ref, some, some[26:29], some[29:30], some_tables, some_high, some_low, velocity
    )
    m_send[...] = turned(leave_ref[...])[:leaving].reshape(FACES, cap, 128)
    m_steps = ((1, 0, 0), (-1, 0, 0), (0, 1, 0), (0, -1, 0), (0, 0, 1), (0, 0, -1))
    m_copies = [
        send(m_send.at[slot], come_ref.at[slot], m_sems, slot, step)
        for slot, step in enumerate(m_steps)
    ]
    read_back(new_ref, record, anchor, living, tables, high_ref, low_ref, velocity)
    for copy in m_copies:
        copy.wait()
    placed = pick(dot_nn, turned(come_ref[...].reshape(leaving, 128))[:32])
    out_ref[...] = jnp.where(taken > 0.0, placed, new_ref[...])[0:26]


def body(sizes, particles, block_ids, node_offsets, live_count, migrations):
    count = particles.shape[1]
    vmem = pl.BlockSpec(memory_space=pltpu.VMEM)
    return pl.pallas_call(
        functools.partial(kernel, sizes),
        out_shape=pltpu.VMEM(particles.shape, f32),
        in_specs=[pl.BlockSpec(memory_space=pltpu.HBM)] * 5,
        out_specs=vmem,
        scratch_shapes=[
            pltpu.SMEM((1,), jnp.int32),
            pltpu.VMEM(particles.shape, f32),
            pltpu.VMEM((1, count), jnp.int32),
            pltpu.VMEM((1, count), jnp.int32),
            pltpu.VMEM(migrations.shape, jnp.int32),
            pltpu.SemaphoreType.DMA((5,)),
            pltpu.VMEM((LANES, count), bf16),
            pltpu.VMEM((LANES, count), bf16),
            pltpu.VMEM((128, LANES), bf16),
            pltpu.VMEM((128, LANES), bf16),
            pltpu.VMEM((LANES, 128), bf16),
            pltpu.VMEM((LANES, 128), bf16),
            pltpu.VMEM((ROWS, LANES), f32),
            pltpu.VMEM((FACE_ROWS, 128), f32),
            pltpu.VMEM((2, FACE_ROWS, 128), f32),
            pltpu.VMEM((4, 8, 128), f32),
            pltpu.VMEM((2, 4, 8, 128), f32),
            pltpu.VMEM((2, 8, LANES), f32),
            pltpu.VMEM((2, THIRD, 128), f32),
            pltpu.VMEM((2, THIRD, 128), f32),
            pltpu.VMEM((4, 4, 128), f32),
            pltpu.VMEM((4, 4, 128), f32),
            pltpu.VMEM((4, 1, 128), f32),
            pltpu.VMEM((2, 4, 1, 128), f32),
            pltpu.VMEM((32, 128), f32),
            pltpu.VMEM((FACES, migrations.shape[1], 128), f32),
            pltpu.VMEM((FACES, migrations.shape[1], 128), f32),
            pltpu.VMEM((32, count), f32),
            pltpu.SemaphoreType.DMA((2, 18)),
            pltpu.SemaphoreType.DMA((2, 8)),
            pltpu.SemaphoreType.DMA((2, 6)),
        ],
        compiler_params=pltpu.CompilerParams(
            collective_id=0, has_side_effects=True, vmem_limit_bytes=60 * 1024 * 1024
        ),
        name="substep",
    )(
        live_count,
        particles,
        block_ids.reshape(1, count),
        node_offsets.reshape(1, count),
        migrations,
    )


def solution(mesh):
    sizes = tuple(mesh.shape[name] for name in AXES)
    return jax.shard_map(
        functools.partial(body, sizes),
        mesh=mesh,
        in_specs=(
            P(None, AXES),
            P(AXES),
            P(AXES),
            P(AXES),
            P(None, AXES),
        ),
        out_specs=P(None, AXES),
        check_vma=False,
    )
```

```python
import functools

import jax
import jax.numpy as jnp
from jax import lax
from jax.experimental import pallas as pl
from jax.experimental.pallas import tpu as pltpu
from jax.sharding import PartitionSpec as P

BLK = 2
AXES = ("gx", "gy", "gz")
SPAN = 8 * BLK + 2
STRIDE = 24
ROWS = 4 * SPAN
LANES = 512
USED = STRIDE * SPAN
EDGE = 2 * STRIDE
SIDE = STRIDE + SPAN
THIRD = ROWS // 3
HEAD = 40
FACE_ROWS = HEAD + 8
CENTRE = 0.5 * (SPAN - 1)
FACES = 6

time_step = 0.05
stress_gain = 0.2
shear_zero = 5.0
bulk_zero = 5.0
harden_rate = 10.0
mass_floor = 0.1
gravity = 9.8

f32 = jnp.float32
bf16 = jnp.bfloat16
MESH = pl.DeviceIdType.MESH


def iota(shape, dim):
    return lax.broadcasted_iota(jnp.int32, shape, dim)


def split(value):
    high = value.astype(bf16)
    return high, (value - high.astype(f32)).astype(bf16)


def stacked(value):
    high = value.astype(bf16).astype(f32)
    return jnp.concatenate([high, value - high], axis=0).astype(bf16)


def dot_nt(left, right):
    return lax.dot_general(left, right, (((1,), (1,)), ((), ())), preferred_element_type=f32)


def dot_nn(left, right):
    return lax.dot_general(left, right, (((1,), (0,)), ((), ())), preferred_element_type=f32)


def contract(dot, left, right_high, right_low):
    rows = left.shape[0]
    both = dot(stacked(left), right_high)
    return both[:rows] + both[rows:] + dot(left.astype(bf16), right_low)


def spline(place, anchor, fraction):
    apart = (place - anchor) - fraction
    size = jnp.abs(apart)
    outer = jnp.maximum(1.5 - size, 0.0)
    inner = jnp.maximum(0.5 - size, 0.0)
    weight = 0.5 * outer * outer - 1.5 * inner * inner
    return weight, weight * apart


def axis_tables(anchor, fraction):
    count = fraction.shape[1]
    line = iota((STRIDE, count), 0).astype(f32)
    line_x = jnp.right_shift(iota((ROWS, count), 0), 2).astype(f32)
    return (
        spline(line_x, anchor[0:1], fraction[0:1]),
        spline(line, anchor[1:2], fraction[1:2]),
        spline(line, anchor[2:3], fraction[2:3]),
    )


def store_pair(high_ref, low_ref, row, outer_line, inner_line, picks):
    pair = jnp.concatenate([outer_line[p : p + 1] * inner_line for p in picks], axis=0)
    high, low = split(pair)
    high_ref[row : row + EDGE, :] = high
    low_ref[row : row + EDGE, :] = low


def fill_tables(high_ref, low_ref, tables, pairs=range(SPAN // 2)):
    _, (weight_y, _), (weight_z, _) = tables
    count = weight_y.shape[1]
    for pair in pairs:
        store_pair(high_ref, low_ref, EDGE * pair, weight_y, weight_z, (2 * pair, 2 * pair + 1))
    if len(pairs) == SPAN // 2:
        for ref in (high_ref, low_ref):
            ref[USED:LANES, :] = jnp.zeros((LANES - USED, count), bf16)


def fill_masks(gather_ref, spread_ref, corner_ref):
    lane = iota((128, LANES), 1)
    row = iota((128, LANES), 0)
    line = jnp.right_shift(lane * 2731, 16)
    place = lane - STRIDE * line
    k = row & 3
    same = (jnp.right_shift(row, 2) == line) & (line < SPAN)
    near = jnp.where(k < 2, k, k + (SPAN - 4))
    far = jnp.where(k < 2, k + (SPAN - 2), k - 2)
    gather_ref[...] = jnp.where(same & (place == near), 1.0, 0.0).astype(bf16)
    corner_ref[...] = jnp.where(
        jnp.where(line < 2, line, line + (SPAN - 4)) == jnp.right_shift(row, 2),
        jnp.where((place == near) & (line < 4), 1.0, 0.0),
        0.0,
    )[:, :128].astype(bf16)
    spread_ref[...] = jnp.where(same & (place == far), 1.0, 0.0).astype(bf16)


def pack_edges(face):
    group = jnp.right_shift(iota((8, 128), 1), 3)
    tiles = []
    for start in (4 * (SPAN - 2), 0):
        tile = jnp.zeros((8, 128), f32)
        for g in range(ROWS // 8):
            rolled = pltpu.roll(face[8 * g : 8 * g + 8], (8 * g - start) % 128, 1)
            tile = jnp.where(group == g, rolled, tile)
        tiles.append(tile)
    return tiles


def lane_places(lanes):
    lane = iota((1, lanes), 1)
    line = jnp.right_shift(lane * 2731, 16)
    return line.astype(f32) - CENTRE, (lane - STRIDE * line).astype(f32) - CENTRE


def combine(parts, place_y, place_z):
    return parts[:ROWS] + place_y * parts[ROWS : 2 * ROWS] + place_z * parts[2 * ROWS :]


def product(left, right):
    return [
        [
            left[i][0] * right[0][j] + left[i][1] * right[1][j] + left[i][2] * right[2][j]
            for j in range(3)
        ]
        for i in range(3)
    ]


def transposed(matrix):
    return [[matrix[j][i] for j in range(3)] for i in range(3)]


def pack(row):
    count = row.shape[1]
    return jnp.concatenate([row[:, s : s + 128] for s in range(0, count, 128)], axis=0)


def unpack(block):
    return jnp.concatenate([block[s : s + 1] for s in range(block.shape[0])], axis=1)


def stress(deform, plastic):
    rotation = deform
    for _ in range(5):
        inner = product(transposed(rotation), rotation)
        inner = [[(3.0 - inner[i][j]) if i == j else -inner[i][j] for j in range(3)] for i in range(3)]
        rotation = product(rotation, inner)
        rotation = [[0.5 * entry for entry in line] for line in rotation]
    f = deform
    volume = (
        f[0][0] * (f[1][1] * f[2][2] - f[1][2] * f[2][1])
        - f[0][1] * (f[1][0] * f[2][2] - f[1][2] * f[2][0])
        + f[0][2] * (f[1][0] * f[2][1] - f[1][1] * f[2][0])
    )
    harden = jnp.exp(harden_rate * (1.0 - plastic))
    shear = 2.0 * shear_zero * harden
    bulk = bulk_zero * harden * (volume - 1.0) * volume
    apart = [[f[i][j] - rotation[i][j] for j in range(3)] for i in range(3)]
    tau = product(apart, transposed(f))
    return [
        [shear * tau[i][j] + bulk if i == j else shear * tau[i][j] for j in range(3)]
        for i in range(3)
    ]


def read_back(out_ref, record, anchor, living, tables, high_ref, low_ref, velocity):
    count = record.shape[1]
    (weight_x, shift_x), _, _ = tables
    reads = contract(dot_nn, velocity, high_ref[...], low_ref[...])

    def fold(value):
        total = value[0:8]
        for row in range(8, ROWS, 8):
            total = total + value[row : row + 8]
        return total[0:4] + total[4:8]

    first = reads[:ROWS]
    speed = fold(weight_x * first) * living
    place = anchor + record[21:24] - CENTRE
    along = [
        4.0 * living * fold(shift_x * first),
        4.0 * (living * fold(weight_x * reads[ROWS : 2 * ROWS]) - place[1:2] * speed),
        4.0 * (living * fold(weight_x * reads[2 * ROWS :]) - place[2:3] * speed),
    ]
    out_ref[0:3, :] = speed[1:4]
    deform = [record[12 + 3 * k : 15 + 3 * k] for k in range(3)]
    for i in range(3):
        push = jnp.zeros((3, count), f32)
        for j in range(3):
            entry = along[j][1 + i : 2 + i]
            out_ref[3 + 3 * i + j : 4 + 3 * i + j, :] = entry
            push = push + entry * deform[j]
        out_ref[12 + 3 * i : 15 + 3 * i, :] = deform[i] * living + time_step * push
    out_ref[21:24, :] = record[21:24] * living + time_step * speed[1:4]
    out_ref[24:26, :] = record[24:26] * living
    out_ref[26:32, :] = jnp.zeros((6, count), f32)


def pack_side(tile):
    lane = iota((THIRD, 128), 1)
    middle = pltpu.roll(tile[THIRD : 2 * THIRD], SIDE, 1)
    last = pltpu.roll(tile[2 * THIRD :], 2 * SIDE, 1)
    return jnp.where(lane < SIDE, tile[:THIRD], jnp.where(lane < 2 * SIDE, middle, last))


def open_side(packed):
    rolled = [packed] + [pltpu.roll(packed, 128 - g * SIDE, 1) for g in (1, 2)]
    return jnp.where(iota((ROWS, 128), 1) < SIDE, jnp.concatenate(rolled, axis=0), 0.0)


def pack_corner(tile):
    return jnp.where(iota((4, 128), 1) < 64, tile[0:4], pltpu.roll(tile[4:8], 64, 1))


def open_corner(packed):
    full = jnp.concatenate([packed, pltpu.roll(packed, 64, 1)], axis=0)
    return jnp.where(iota((8, 128), 1) < SIDE, full, 0.0)


def pack_face(face):
    rest = jnp.concatenate([face[HEAD:], jnp.zeros((2 * HEAD - ROWS, 128), f32)], axis=0)
    head = jnp.where(iota((HEAD, 128), 1) < 72, face[:HEAD], pltpu.roll(rest, 72, 1))
    group = jnp.right_shift(iota((8, 128), 1), 4)
    tail = jnp.zeros((8, 128), f32)
    for g in range((ROWS - HEAD) // 8):
        rolled = pltpu.roll(rest[8 * g : 8 * g + 8], (16 * g - 56) % 128, 1)
        tail = jnp.where(group == g, rolled, tail)
    return jnp.concatenate([head, tail], axis=0)


def open_face(packed):
    tiles = [packed[r : r + 8] for r in range(0, HEAD, 8)]
    tail = packed[HEAD:]
    lane = iota((8, 128), 1)
    for g in range((ROWS - HEAD) // 8):
        body_part = pltpu.roll(packed[8 * g : 8 * g + 8], 56, 1)
        tiles.append(jnp.where(lane < 56, body_part, pltpu.roll(tail, (56 - 16 * g) % 128, 1)))
    return tiles


def pack_line(tile, start):
    group = jnp.right_shift(iota((8, 128), 1), 3)
    row = iota((8, 128), 0)
    total = jnp.zeros((8, 128), f32)
    for r in range(8):
        rolled = pltpu.roll(tile, (8 * r - start) % 128, 1)
        total = jnp.where((group == r) & (row == r), rolled, total)
    return jnp.sum(total, axis=0, keepdims=True)


def open_line(packed, start):
    wide = jnp.broadcast_to(packed, (8, 128))
    row = iota((8, 128), 0)
    total = pltpu.roll(wide, start, 1) if start else wide
    for r in range(1, 8):
        total = jnp.where(row == r, pltpu.roll(wide, (start - 8 * r) % 128, 1), total)
    return total


def turned(value):
    rows = jnp.zeros((128 - value.shape[0], 128), f32)
    return jnp.concatenate([value, rows], axis=0).T


def kernel(
    sizes,
    live_hbm,
    record_hbm,
    block_hbm,
    offset_hbm,
    plan_hbm,
    out_ref,
    live_ref,
    record_ref,
    block_ref,
    offset_ref,
    plan_ref,
    in_sems,
    high_ref,
    low_ref,
    gather_ref,
    spread_ref,
    corner_ref,
    some_high,
    some_low,
    grid_ref,
    z_send,
    z_recv,
    e_send,
    e_recv,
    x_recv,
    y_send,
    y_recv,
    c_send,
    c_recv,
    l_send,
    l_recv,
    leave_ref,
    m_send,
    come_ref,
    new_ref,
    z_sems,
    xy_sems,
    m_sems,
):
    operands = (
        (record_hbm, record_ref),
        (block_hbm, block_ref),
        (offset_hbm, offset_ref),
        (live_hbm, live_ref),
        (plan_hbm, plan_ref),
    )
    in_copies = [
        pltpu.make_async_copy(source, target, in_sems.at[slot])
        for slot, (source, target) in enumerate(operands)
    ]
    for copy in in_copies:
        copy.start()
    me = [lax.axis_index(name) for name in AXES]

    def at(*step):
        return tuple(
            lax.rem(me[a] + step[a] + sizes[a], sizes[a]) if step[a] else me[a] for a in range(3)
        )

    pair_z = sizes[2] == 2
    z_steps = ((0, 0, 1),) if pair_z else ((0, 0, 1), (0, 0, -1))
    xy_steps = tuple((i, j, 0) for i in (0, 1, -1) for j in (1, -1, 0) if i or j)
    barrier = pltpu.get_barrier_semaphore()
    around = xy_steps + tuple((i, j, k) for _, _, k in z_steps for i, j, _ in ((0, 0, 0),) + xy_steps)
    for step in around:
        pl.semaphore_signal(barrier, inc=1, device_id=at(*step), device_id_type=MESH)

    fill_masks(gather_ref, spread_ref, corner_ref)
    for copy in in_copies:
        copy.wait()
    count = record_ref.shape[1]
    record = record_ref[...]
    fraction = record[21:24]
    blocks = block_ref[...]
    offsets = offset_ref[...]
    anchor = (
        jnp.concatenate(
            [
                8 * jnp.right_shift(blocks, 2) + jnp.right_shift(offsets, 6),
                8 * (jnp.right_shift(blocks, 1) & 1) + (jnp.right_shift(offsets, 3) & 7),
                8 * (blocks & 1) + (offsets & 7),
            ],
            axis=0,
        )
        + 1
    ).astype(f32)
    living = jnp.where(iota((1, count), 1) < live_ref[0], 1.0, 0.0).astype(f32)

    tables = axis_tables(anchor, fraction)
    fill_tables(high_ref, low_ref, tables, (0, SPAN // 2 - 1))

    plastic = pack(record[25:26])
    deform = [[pack(record[12 + 3 * i + j : 13 + 3 * i + j]) for j in range(3)] for i in range(3)]
    tau = stress(deform, plastic)
    mass = record[24:25]
    held = mass * living
    coupling = [
        [
            (mass * record[3 + 3 * i + j : 4 + 3 * i + j] - stress_gain * unpack(tau[i][j])) * living
            for j in range(3)
        ]
        for i in range(3)
    ]
    none = jnp.zeros((1, count), f32)
    places = anchor + fraction - CENTRE
    momentum = [
        held * record[i : i + 1] - coupling[i][1] * places[1:2] - coupling[i][2] * places[2:3]
        for i in range(3)
    ]
    base = jnp.concatenate([held] + momentum + [held] + momentum, axis=0)
    pushes = [
        jnp.concatenate([none, coupling[0][j], coupling[1][j], coupling[2][j]] * 2, axis=0)
        for j in range(3)
    ]
    weight_x, shift_x = tables[0]
    tiles = range(0, ROWS, 8)
    left = jnp.concatenate(
        [base * weight_x[r : r + 8] + pushes[0] * shift_x[r : r + 8] for r in tiles]
        + [pushes[1] * weight_x[r : r + 8] for r in tiles]
        + [pushes[2] * weight_x[r : r + 8] for r in tiles],
        axis=0,
    )

    def send(source, target, sems, slot, step):
        copy = pltpu.make_async_remote_copy(
            src_ref=source,
            dst_ref=target,
            send_sem=sems.at[0, slot],
            recv_sem=sems.at[1, slot],
            device_id=at(*step),
            device_id_type=MESH,
        )
        copy.start()
        return copy

    corners = ((1, 1), (1, -1), (-1, 1), (-1, -1))
    sides = ((0, 1), (0, -1), (1, 0), (-1, 0))
    last = {1: ROWS - 8, -1: 0}
    last_face = {1: 4 * (SPAN - 2), -1: 0}

    blank = jnp.zeros((128 - 2 * EDGE, count), bf16)
    edge_high, edge_low = [
        jnp.concatenate([ref[0:EDGE, :], ref[USED - EDGE : USED, :], blank], axis=0)
        for ref in (high_ref, low_ref)
    ]
    lane_y, lane_z = lane_places(128)
    lane_y = jnp.where(lane_y < 2 - CENTRE, lane_y, lane_y + (SPAN - 4))
    ends = combine(contract(dot_nt, left, edge_high, edge_low), lane_y, lane_z)
    ends = {-1: ends, 1: pltpu.roll(ends, 128 - EDGE, 1)}
    y_send[0] = pack_side(ends[1])
    y_send[1] = pack_side(ends[-1])
    for number, (i, j) in enumerate(corners):
        c_send[number] = pack_corner(ends[j][last[i] : last[i] + 8])
    pl.semaphore_wait(barrier, len(around))
    xy_copies = []
    for number, j in enumerate((1, -1)):
        xy_copies.append(send(y_send.at[number], y_recv.at[number], xy_sems, number, (0, j, 0)))
    for number, (i, j) in enumerate(corners):
        xy_copies.append(send(c_send.at[number], c_recv.at[number], xy_sems, 2 + number, (i, j, 0)))

    face = dot_nt(stacked(ends[-1]), corner_ref[...])
    face = face[:ROWS] + face[ROWS:]
    e_send[0], e_send[1] = pack_edges(face)
    for number, (i, j) in enumerate(corners):
        l_send[number] = pack_line(face[last[i] : last[i] + 8], last_face[j])
    z_copies = []

    def send_edges(numbers):
        for slot, (_, _, k) in enumerate(z_steps):
            for number in numbers:
                i, j = sides[number]
                target = e_recv.at[slot, number]
                z_copies.append(
                    send(e_send.at[number], target, z_sems, 9 * slot + 1 + number, (i, j, k))
                )

    send_edges((0, 1))
    for slot, (_, _, k) in enumerate(z_steps):
        for number, (i, j) in enumerate(corners):
            target = l_recv.at[slot, number]
            z_copies.append(
                send(l_send.at[number], target, z_sems, 9 * slot + 5 + number, (i, j, k))
            )

    fill_tables(high_ref, low_ref, tables, range(1, SPAN // 2 - 1))
    for ref in (high_ref, low_ref):
        ref[USED:LANES, :] = jnp.zeros((LANES - USED, count), bf16)
    lane_y, lane_z = lane_places(LANES)
    partial = combine(contract(dot_nt, left, high_ref[...], low_ref[...]), lane_y, lane_z)
    grid_ref[...] = partial
    for number, i in enumerate((1, -1)):
        source = grid_ref.at[pl.ds(last[i], 8), :]
        xy_copies.append(send(source, x_recv.at[number], xy_sems, 6 + number, (i, 0, 0)))
    face = dot_nt(stacked(partial), gather_ref[...])
    face = face[:ROWS] + face[ROWS:]
    z_send[...] = pack_face(face)
    for slot, (_, _, k) in enumerate(z_steps):
        z_copies.append(send(z_send, z_recv.at[slot], z_sems, 9 * slot, (0, 0, k)))
    e_send[2] = face[last[1] : last[1] + 8]
    e_send[3] = face[last[-1] : last[-1] + 8]
    send_edges((2, 3))

    plan = plan_ref[...].astype(f32)
    cap = plan.shape[1]
    leaving = FACES * cap
    wide = jnp.concatenate(
        [jnp.broadcast_to(plan[q : q + 1], (cap, cap)) for q in range(FACES)], axis=0
    )
    diagonal = (iota((leaving, cap), 0) & (cap - 1)) == iota((leaving, cap), 1)
    chosen = jnp.sum(jnp.where(diagonal, wide, 0.0), axis=1, keepdims=True)
    picked = jnp.where(iota((leaving, count), 1).astype(f32) == chosen, 1.0, 0.0).astype(f32)
    taken = jnp.sum(picked, axis=0, keepdims=True)
    picker = jnp.concatenate([picked, jnp.zeros((128 - leaving, count), f32)], axis=0).astype(bf16)
    full = jnp.concatenate([record, anchor, living, jnp.zeros((2, count), f32)], axis=0)

    def thirds(value):
        high = value.astype(bf16).astype(f32)
        rest = value - high
        middle = rest.astype(bf16).astype(f32)
        return jnp.concatenate([high, middle, rest - middle], axis=0).astype(bf16)

    def pick(dot, value):
        got = dot(thirds(value), picker)
        return got[0:32] + got[32:64] + got[64:96]

    some = pick(dot_nt, full)
    some_tables = axis_tables(some[26:29], some[21:24])
    fill_tables(some_high, some_low, some_tables)

    for copy in z_copies:
        copy.wait_recv()

    def from_z(ref, *index):
        if pair_z:
            return ref[(0,) + index]
        value = ref[(1,) + index]
        return jnp.where((iota(value.shape, 1) & 3) < 2, value, ref[(0,) + index])

    face_lane = iota((8, 128), 1)
    face_side = {1: face_lane < 8, -1: (face_lane >= 4 * (SPAN - 2)) & (face_lane < 4 * SPAN)}
    face_start = {1: 0, -1: 4 * (SPAN - 2)}
    edge = {step: from_z(e_recv, number) for number, step in enumerate(sides)}
    shared = open_face(from_z(z_recv))
    for g in range(ROWS // 8):
        for j in (1, -1):
            rolled = pltpu.roll(edge[0, j], (face_start[j] - 8 * g) % 128, 1)
            shared[g] = jnp.where(face_side[j], shared[g] + rolled, shared[g])
    for i in (1, -1):
        g = 0 if i > 0 else ROWS // 8 - 1
        shared[g] = shared[g] + edge[i, 0]
        for j in (1, -1):
            line = open_line(from_z(l_recv, corners.index((i, j))), face_start[j])
            shared[g] = jnp.where(face_side[j], shared[g] + line, shared[g])
    spread_sum = dot_nn(stacked(jnp.concatenate(shared, axis=0)), spread_ref[...])
    partial = grid_ref[...] + spread_sum[:ROWS] + spread_sum[ROWS:]

    for copy in xy_copies:
        copy.wait_recv()
    low_side = open_side(y_recv[0])
    high_side = open_side(y_recv[1])
    middle = jnp.zeros((8, LANES - 256), f32)
    corner = [open_corner(c_recv[number]) for number in range(4)]
    low_rows = x_recv[0] + jnp.concatenate([corner[0], middle, corner[1]], axis=1)
    high_rows = x_recv[1] + jnp.concatenate([corner[2], middle, corner[3]], axis=1)
    totals = jnp.concatenate(
        [
            partial[:, 0:128] + low_side,
            partial[:, 128 : LANES - 128],
            partial[:, LANES - 128 :] + high_side,
        ],
        axis=1,
    )
    totals = jnp.concatenate(
        [totals[0:8] + low_rows, totals[8 : ROWS - 8], totals[ROWS - 8 :] + high_rows], axis=0
    )
    channel = iota((ROWS, LANES), 0) & 3
    mass_of = jnp.where(
        channel == 1,
        pltpu.roll(totals, 1, 0),
        jnp.where(channel == 2, pltpu.roll(totals, 2, 0), pltpu.roll(totals, 3, 0)),
    )
    velocity = totals / jnp.maximum(mass_of, mass_floor)
    velocity = jnp.where(channel == 3, velocity - time_step * gravity, velocity)
    velocity = jnp.where(channel == 0, 0.0, velocity)
    velocity = jnp.concatenate([velocity, velocity * lane_y, velocity * lane_z], axis=0)

    read_back(
        leave_ref, some, some[26:29], some[29:30], some_tables, some_high, some_low, velocity
    )
    m_send[...] = turned(leave_ref[...])[:leaving].reshape(FACES, cap, 128)
    m_steps = ((1, 0, 0), (-1, 0, 0), (0, 1, 0), (0, -1, 0), (0, 0, 1), (0, 0, -1))
    m_copies = [
        send(m_send.at[slot], come_ref.at[slot], m_sems, slot, step)
        for slot, step in enumerate(m_steps)
    ]
    read_back(new_ref, record, anchor, living, tables, high_ref, low_ref, velocity)
    for copy in xy_copies + z_copies + m_copies:
        copy.wait_send()
    for copy in m_copies:
        copy.wait_recv()
    placed = pick(dot_nn, turned(come_ref[...].reshape(leaving, 128))[:32])
    out_ref[...] = jnp.where(taken > 0.0, placed, new_ref[...])[0:26]


def body(sizes, particles, block_ids, node_offsets, live_count, migrations):
    count = particles.shape[1]
    vmem = pl.BlockSpec(memory_space=pltpu.VMEM)
    return pl.pallas_call(
        functools.partial(kernel, sizes),
        out_shape=pltpu.VMEM(particles.shape, f32),
        in_specs=[pl.BlockSpec(memory_space=pltpu.HBM)] * 5,
        out_specs=vmem,
        scratch_shapes=[
            pltpu.SMEM((1,), jnp.int32),
            pltpu.VMEM(particles.shape, f32),
            pltpu.VMEM((1, count), jnp.int32),
            pltpu.VMEM((1, count), jnp.int32),
            pltpu.VMEM(migrations.shape, jnp.int32),
            pltpu.SemaphoreType.DMA((5,)),
            pltpu.VMEM((LANES, count), bf16),
            pltpu.VMEM((LANES, count), bf16),
            pltpu.VMEM((128, LANES), bf16),
            pltpu.VMEM((128, LANES), bf16),
            pltpu.VMEM((128, 128), bf16),
            pltpu.VMEM((LANES, 128), bf16),
            pltpu.VMEM((LANES, 128), bf16),
            pltpu.VMEM((ROWS, LANES), f32),
            pltpu.VMEM((FACE_ROWS, 128), f32),
            pltpu.VMEM((2, FACE_ROWS, 128), f32),
            pltpu.VMEM((4, 8, 128), f32),
            pltpu.VMEM((2, 4, 8, 128), f32),
            pltpu.VMEM((2, 8, LANES), f32),
            pltpu.VMEM((2, THIRD, 128), f32),
            pltpu.VMEM((2, THIRD, 128), f32),
            pltpu.VMEM((4, 4, 128), f32),
            pltpu.VMEM((4, 4, 128), f32),
            pltpu.VMEM((4, 1, 128), f32),
            pltpu.VMEM((2, 4, 1, 128), f32),
            pltpu.VMEM((32, 128), f32),
            pltpu.VMEM((FACES, migrations.shape[1], 128), f32),
            pltpu.VMEM((FACES, migrations.shape[1], 128), f32),
            pltpu.VMEM((32, count), f32),
            pltpu.SemaphoreType.DMA((2, 18)),
            pltpu.SemaphoreType.DMA((2, 8)),
            pltpu.SemaphoreType.DMA((2, 6)),
        ],
        compiler_params=pltpu.CompilerParams(
            collective_id=0, has_side_effects=True, vmem_limit_bytes=60 * 1024 * 1024
        ),
        name="substep",
    )(
        live_count,
        particles,
        block_ids.reshape(1, count),
        node_offsets.reshape(1, count),
        migrations,
    )


def solution(mesh):
    sizes = tuple(mesh.shape[name] for name in AXES)
    return jax.shard_map(
        functools.partial(body, sizes),
        mesh=mesh,
        in_specs=(
            P(None, AXES),
            P(AXES),
            P(AXES),
            P(AXES),
            P(None, AXES),
        ),
        out_specs=P(None, AXES),
        check_vma=False,
    )
```

```python
import functools

import jax
import jax.numpy as jnp
from jax import lax
from jax.experimental import pallas as pl
from jax.experimental.pallas import tpu as pltpu
from jax.sharding import PartitionSpec as P

BLK = 2
AXES = ("gx", "gy", "gz")
SPAN = 8 * BLK + 2
STRIDE = 24
ROWS = 4 * SPAN
LANES = 512
USED = STRIDE * SPAN
EDGE = 2 * STRIDE
SIDE = STRIDE + SPAN
THIRD = ROWS // 3
HEAD = 40
FACE_ROWS = HEAD + 8
CENTRE = 0.5 * (SPAN - 1)
FACES = 6

time_step = 0.05
stress_gain = 0.2
shear_zero = 5.0
bulk_zero = 5.0
harden_rate = 10.0
mass_floor = 0.1
gravity = 9.8

f32 = jnp.float32
bf16 = jnp.bfloat16
MESH = pl.DeviceIdType.MESH


def iota(shape, dim):
    return lax.broadcasted_iota(jnp.int32, shape, dim)


def split(value):
    high = value.astype(bf16)
    return high, (value - high.astype(f32)).astype(bf16)


def stacked(value):
    high = value.astype(bf16).astype(f32)
    return jnp.concatenate([high, value - high], axis=0).astype(bf16)


def dot_nt(left, right):
    return lax.dot_general(left, right, (((1,), (1,)), ((), ())), preferred_element_type=f32)


def dot_nn(left, right):
    return lax.dot_general(left, right, (((1,), (0,)), ((), ())), preferred_element_type=f32)


def contract(dot, left, right_high, right_low):
    rows = left.shape[0]
    both = dot(stacked(left), right_high)
    return both[:rows] + both[rows:] + dot(left.astype(bf16), right_low)


def spline(place, anchor, fraction):
    apart = (place - anchor) - fraction
    size = jnp.abs(apart)
    outer = jnp.maximum(1.5 - size, 0.0)
    inner = jnp.maximum(0.5 - size, 0.0)
    weight = 0.5 * outer * outer - 1.5 * inner * inner
    return weight, weight * apart


def axis_tables(anchor, fraction):
    count = fraction.shape[1]
    line = iota((STRIDE, count), 0).astype(f32)
    line_x = jnp.right_shift(iota((ROWS, count), 0), 2).astype(f32)
    return (
        spline(line_x, anchor[0:1], fraction[0:1]),
        spline(line, anchor[1:2], fraction[1:2]),
        spline(line, anchor[2:3], fraction[2:3]),
    )


def store_pair(high_ref, low_ref, row, outer_line, inner_line, picks):
    pair = jnp.concatenate([outer_line[p : p + 1] * inner_line for p in picks], axis=0)
    high, low = split(pair)
    high_ref[row : row + EDGE, :] = high
    low_ref[row : row + EDGE, :] = low


def fill_tables(high_ref, low_ref, tables, pairs=range(SPAN // 2)):
    _, (weight_y, _), (weight_z, _) = tables
    count = weight_y.shape[1]
    for pair in pairs:
        store_pair(high_ref, low_ref, EDGE * pair, weight_y, weight_z, (2 * pair, 2 * pair + 1))
    if len(pairs) == SPAN // 2:
        for ref in (high_ref, low_ref):
            ref[USED:LANES, :] = jnp.zeros((LANES - USED, count), bf16)


def fill_masks(gather_ref, spread_ref, corner_ref):
    lane = iota((128, LANES), 1)
    row = iota((128, LANES), 0)
    line = jnp.right_shift(lane * 2731, 16)
    place = lane - STRIDE * line
    k = row & 3
    same = (jnp.right_shift(row, 2) == line) & (line < SPAN)
    near = jnp.where(k < 2, k, k + (SPAN - 4))
    far = jnp.where(k < 2, k + (SPAN - 2), k - 2)
    gather_ref[...] = jnp.where(same & (place == near), 1.0, 0.0).astype(bf16)
    corner_ref[...] = jnp.where(
        jnp.where(line < 2, line, line + (SPAN - 4)) == jnp.right_shift(row, 2),
        jnp.where((place == near) & (line < 4), 1.0, 0.0),
        0.0,
    )[:, :128].astype(bf16)
    spread_ref[...] = jnp.where(same & (place == far), 1.0, 0.0).astype(bf16)


def pack_edges(face):
    group = jnp.right_shift(iota((8, 128), 1), 3)
    tiles = []
    for start in (4 * (SPAN - 2), 0):
        tile = jnp.zeros((8, 128), f32)
        for g in range(ROWS // 8):
            rolled = pltpu.roll(face[8 * g : 8 * g + 8], (8 * g - start) % 128, 1)
            tile = jnp.where(group == g, rolled, tile)
        tiles.append(tile)
    return tiles


def lane_places(lanes):
    lane = iota((1, lanes), 1)
    line = jnp.right_shift(lane * 2731, 16)
    return line.astype(f32) - CENTRE, (lane - STRIDE * line).astype(f32) - CENTRE


def combine(parts, place_y, place_z):
    return parts[:ROWS] + place_y * parts[ROWS : 2 * ROWS] + place_z * parts[2 * ROWS :]


def product(left, right):
    return [
        [
            left[i][0] * right[0][j] + left[i][1] * right[1][j] + left[i][2] * right[2][j]
            for j in range(3)
        ]
        for i in range(3)
    ]


def transposed(matrix):
    return [[matrix[j][i] for j in range(3)] for i in range(3)]


def pack(row):
    count = row.shape[1]
    return jnp.concatenate([row[:, s : s + 128] for s in range(0, count, 128)], axis=0)


def unpack(block):
    return jnp.concatenate([block[s : s + 1] for s in range(block.shape[0])], axis=1)


def stress(deform, plastic):
    rotation = deform
    for _ in range(5):
        inner = product(transposed(rotation), rotation)
        inner = [[(3.0 - inner[i][j]) if i == j else -inner[i][j] for j in range(3)] for i in range(3)]
        rotation = product(rotation, inner)
        rotation = [[0.5 * entry for entry in line] for line in rotation]
    f = deform
    volume = (
        f[0][0] * (f[1][1] * f[2][2] - f[1][2] * f[2][1])
        - f[0][1] * (f[1][0] * f[2][2] - f[1][2] * f[2][0])
        + f[0][2] * (f[1][0] * f[2][1] - f[1][1] * f[2][0])
    )
    harden = jnp.exp(harden_rate * (1.0 - plastic))
    shear = 2.0 * shear_zero * harden
    bulk = bulk_zero * harden * (volume - 1.0) * volume
    apart = [[f[i][j] - rotation[i][j] for j in range(3)] for i in range(3)]
    tau = product(apart, transposed(f))
    return [
        [shear * tau[i][j] + bulk if i == j else shear * tau[i][j] for j in range(3)]
        for i in range(3)
    ]


def read_back(out_ref, record, anchor, living, tables, high_ref, low_ref, velocity):
    count = record.shape[1]
    (weight_x, shift_x), _, _ = tables
    reads = contract(dot_nn, velocity, high_ref[...], low_ref[...])

    def fold(value):
        total = value[0:8]
        for row in range(8, ROWS, 8):
            total = total + value[row : row + 8]
        return total[0:4] + total[4:8]

    first = reads[:ROWS]
    speed = fold(weight_x * first) * living
    place = anchor + record[21:24] - CENTRE
    along = [
        4.0 * living * fold(shift_x * first),
        4.0 * (living * fold(weight_x * reads[ROWS : 2 * ROWS]) - place[1:2] * speed),
        4.0 * (living * fold(weight_x * reads[2 * ROWS :]) - place[2:3] * speed),
    ]
    out_ref[0:3, :] = speed[1:4]
    deform = [record[12 + 3 * k : 15 + 3 * k] for k in range(3)]
    for i in range(3):
        push = jnp.zeros((3, count), f32)
        for j in range(3):
            entry = along[j][1 + i : 2 + i]
            out_ref[3 + 3 * i + j : 4 + 3 * i + j, :] = entry
            push = push + entry * deform[j]
        out_ref[12 + 3 * i : 15 + 3 * i, :] = deform[i] * living + time_step * push
    out_ref[21:24, :] = record[21:24] * living + time_step * speed[1:4]
    out_ref[24:26, :] = record[24:26] * living
    out_ref[26:32, :] = jnp.zeros((6, count), f32)


def pack_side(tile):
    lane = iota((THIRD, 128), 1)
    middle = pltpu.roll(tile[THIRD : 2 * THIRD], SIDE, 1)
    last = pltpu.roll(tile[2 * THIRD :], 2 * SIDE, 1)
    return jnp.where(lane < SIDE, tile[:THIRD], jnp.where(lane < 2 * SIDE, middle, last))


def open_side(packed):
    rolled = [packed] + [pltpu.roll(packed, 128 - g * SIDE, 1) for g in (1, 2)]
    return jnp.where(iota((ROWS, 128), 1) < SIDE, jnp.concatenate(rolled, axis=0), 0.0)


def pack_corner(tile):
    return jnp.where(iota((4, 128), 1) < 64, tile[0:4], pltpu.roll(tile[4:8], 64, 1))


def open_corner(packed):
    full = jnp.concatenate([packed, pltpu.roll(packed, 64, 1)], axis=0)
    return jnp.where(iota((8, 128), 1) < SIDE, full, 0.0)


def pack_face(face):
    rest = jnp.concatenate([face[HEAD:], jnp.zeros((2 * HEAD - ROWS, 128), f32)], axis=0)
    head = jnp.where(iota((HEAD, 128), 1) < 72, face[:HEAD], pltpu.roll(rest, 72, 1))
    group = jnp.right_shift(iota((8, 128), 1), 4)
    tail = jnp.zeros((8, 128), f32)
    for g in range((ROWS - HEAD) // 8):
        rolled = pltpu.roll(rest[8 * g : 8 * g + 8], (16 * g - 56) % 128, 1)
        tail = jnp.where(group == g, rolled, tail)
    return jnp.concatenate([head, tail], axis=0)


def open_face(packed):
    tiles = [packed[r : r + 8] for r in range(0, HEAD, 8)]
    tail = packed[HEAD:]
    lane = iota((8, 128), 1)
    for g in range((ROWS - HEAD) // 8):
        body_part = pltpu.roll(packed[8 * g : 8 * g + 8], 56, 1)
        tiles.append(jnp.where(lane < 56, body_part, pltpu.roll(tail, (56 - 16 * g) % 128, 1)))
    return tiles


def pack_line(tile, start):
    group = jnp.right_shift(iota((8, 128), 1), 3)
    row = iota((8, 128), 0)
    total = jnp.zeros((8, 128), f32)
    for r in range(8):
        rolled = pltpu.roll(tile, (8 * r - start) % 128, 1)
        total = jnp.where((group == r) & (row == r), rolled, total)
    return jnp.sum(total, axis=0, keepdims=True)


def open_line(packed, start):
    wide = jnp.broadcast_to(packed, (8, 128))
    row = iota((8, 128), 0)
    total = pltpu.roll(wide, start, 1) if start else wide
    for r in range(1, 8):
        total = jnp.where(row == r, pltpu.roll(wide, (start - 8 * r) % 128, 1), total)
    return total


def turned(value):
    rows = jnp.zeros((128 - value.shape[0], 128), f32)
    return jnp.concatenate([value, rows], axis=0).T


def kernel(
    sizes,
    live_hbm,
    record_hbm,
    block_hbm,
    offset_hbm,
    plan_hbm,
    out_ref,
    live_ref,
    record_ref,
    block_ref,
    offset_ref,
    plan_ref,
    in_sems,
    high_ref,
    low_ref,
    gather_ref,
    spread_ref,
    corner_ref,
    some_high,
    some_low,
    grid_ref,
    z_send,
    z_recv,
    e_send,
    e_recv,
    x_recv,
    y_send,
    y_recv,
    c_send,
    c_recv,
    l_send,
    l_recv,
    leave_ref,
    m_send,
    come_ref,
    new_ref,
    z_sems,
    xy_sems,
    m_sems,
):
    operands = (
        (record_hbm, record_ref),
        (block_hbm, block_ref),
        (offset_hbm, offset_ref),
        (live_hbm, live_ref),
        (plan_hbm, plan_ref),
    )
    in_copies = [
        pltpu.make_async_copy(source, target, in_sems.at[slot])
        for slot, (source, target) in enumerate(operands)
    ]
    for copy in in_copies:
        copy.start()
    me = [lax.axis_index(name) for name in AXES]

    def at(*step):
        return tuple(
            lax.rem(me[a] + step[a] + sizes[a], sizes[a]) if step[a] else me[a] for a in range(3)
        )

    pair_z = sizes[2] == 2
    z_steps = ((0, 0, 1),) if pair_z else ((0, 0, 1), (0, 0, -1))
    xy_steps = tuple((i, j, 0) for i in (0, 1, -1) for j in (1, -1, 0) if i or j)
    barrier = pltpu.get_barrier_semaphore()
    around = xy_steps + tuple((i, j, k) for _, _, k in z_steps for i, j, _ in ((0, 0, 0),) + xy_steps)
    for step in around:
        pl.semaphore_signal(barrier, inc=1, device_id=at(*step), device_id_type=MESH)

    fill_masks(gather_ref, spread_ref, corner_ref)
    for copy in in_copies:
        copy.wait()
    count = record_ref.shape[1]
    record = record_ref[...]
    fraction = record[21:24]
    blocks = block_ref[...]
    offsets = offset_ref[...]
    anchor = (
        jnp.concatenate(
            [
                8 * jnp.right_shift(blocks, 2) + jnp.right_shift(offsets, 6),
                8 * (jnp.right_shift(blocks, 1) & 1) + (jnp.right_shift(offsets, 3) & 7),
                8 * (blocks & 1) + (offsets & 7),
            ],
            axis=0,
        )
        + 1
    ).astype(f32)
    living = jnp.where(iota((1, count), 1) < live_ref[0], 1.0, 0.0).astype(f32)

    tables = axis_tables(anchor, fraction)
    early = (0, 1, 2, SPAN // 2 - 1)
    fill_tables(high_ref, low_ref, tables, early)
    for ref in (high_ref, low_ref):
        ref[USED:LANES, :] = jnp.zeros((LANES - USED, count), bf16)

    plastic = pack(record[25:26])
    deform = [[pack(record[12 + 3 * i + j : 13 + 3 * i + j]) for j in range(3)] for i in range(3)]
    tau = stress(deform, plastic)
    mass = record[24:25]
    held = mass * living
    coupling = [
        [
            (mass * record[3 + 3 * i + j : 4 + 3 * i + j] - stress_gain * unpack(tau[i][j])) * living
            for j in range(3)
        ]
        for i in range(3)
    ]
    none = jnp.zeros((1, count), f32)
    places = anchor + fraction - CENTRE
    momentum = [
        held * record[i : i + 1] - coupling[i][1] * places[1:2] - coupling[i][2] * places[2:3]
        for i in range(3)
    ]
    base = jnp.concatenate([held] + momentum + [held] + momentum, axis=0)
    pushes = [
        jnp.concatenate([none, coupling[0][j], coupling[1][j], coupling[2][j]] * 2, axis=0)
        for j in range(3)
    ]
    weight_x, shift_x = tables[0]
    tiles = range(0, ROWS, 8)
    left = jnp.concatenate(
        [base * weight_x[r : r + 8] + pushes[0] * shift_x[r : r + 8] for r in tiles]
        + [pushes[1] * weight_x[r : r + 8] for r in tiles]
        + [pushes[2] * weight_x[r : r + 8] for r in tiles],
        axis=0,
    )

    def send(source, target, sems, slot, step):
        copy = pltpu.make_async_remote_copy(
            src_ref=source,
            dst_ref=target,
            send_sem=sems.at[0, slot],
            recv_sem=sems.at[1, slot],
            device_id=at(*step),
            device_id_type=MESH,
        )
        copy.start()
        return copy

    corners = ((1, 1), (1, -1), (-1, 1), (-1, -1))
    sides = ((0, 1), (0, -1), (1, 0), (-1, 0))
    last = {1: ROWS - 8, -1: 0}
    last_face = {1: 4 * (SPAN - 2), -1: 0}

    lane_y, lane_z = lane_places(LANES)
    cut = LANES - 128

    def outside(value, axis):
        low, high = lax.slice_in_dim(value, 0, 128, axis=axis), lax.slice_in_dim(value, cut, LANES, axis=axis)
        return jnp.concatenate([low, high], axis=axis)

    ends = combine(
        contract(
            dot_nt,
            left,
            *[jnp.concatenate([ref[0:128, :], ref[cut:, :]], axis=0) for ref in (high_ref, low_ref)],
        ),
        outside(lane_y, 1),
        outside(lane_z, 1),
    )
    ends = {-1: ends[:, :128], 1: ends[:, 128:]}
    y_send[0] = pack_side(ends[1])
    y_send[1] = pack_side(ends[-1])
    for number, (i, j) in enumerate(corners):
        c_send[number] = pack_corner(ends[j][last[i] : last[i] + 8])
    pl.semaphore_wait(barrier, len(around))
    xy_copies = []
    for number, j in enumerate((1, -1)):
        xy_copies.append(send(y_send.at[number], y_recv.at[number], xy_sems, number, (0, j, 0)))
    for number, (i, j) in enumerate(corners):
        xy_copies.append(send(c_send.at[number], c_recv.at[number], xy_sems, 2 + number, (i, j, 0)))

    both = jnp.where(iota((ROWS, 128), 1) < EDGE, ends[-1], pltpu.roll(ends[1], EDGE, 1))
    face = dot_nt(stacked(both), corner_ref[...])
    face = face[:ROWS] + face[ROWS:]
    e_send[0], e_send[1] = pack_edges(face)
    for number, (i, j) in enumerate(corners):
        l_send[number] = pack_line(face[last[i] : last[i] + 8], last_face[j])
    z_copies = []

    def send_edges(numbers):
        for slot, (_, _, k) in enumerate(z_steps):
            for number in numbers:
                i, j = sides[number]
                target = e_recv.at[slot, number]
                z_copies.append(
                    send(e_send.at[number], target, z_sems, 9 * slot + 1 + number, (i, j, k))
                )

    send_edges((0, 1))
    for slot, (_, _, k) in enumerate(z_steps):
        for number, (i, j) in enumerate(corners):
            target = l_recv.at[slot, number]
            z_copies.append(
                send(l_send.at[number], target, z_sems, 9 * slot + 5 + number, (i, j, k))
            )

    fill_tables(high_ref, low_ref, tables, range(3, SPAN // 2 - 1))
    inside = combine(
        contract(dot_nt, left, high_ref[128:cut, :], low_ref[128:cut, :]),
        lane_y[:, 128:cut],
        lane_z[:, 128:cut],
    )
    partial = jnp.concatenate([ends[-1], inside, ends[1]], axis=1)
    grid_ref[...] = partial
    for number, i in enumerate((1, -1)):
        source = grid_ref.at[pl.ds(last[i], 8), :]
        xy_copies.append(send(source, x_recv.at[number], xy_sems, 6 + number, (i, 0, 0)))
    face = dot_nt(stacked(partial), gather_ref[...])
    face = face[:ROWS] + face[ROWS:]
    z_send[...] = pack_face(face)
    for slot, (_, _, k) in enumerate(z_steps):
        z_copies.append(send(z_send, z_recv.at[slot], z_sems, 9 * slot, (0, 0, k)))
    e_send[2] = face[last[1] : last[1] + 8]
    e_send[3] = face[last[-1] : last[-1] + 8]
    send_edges((2, 3))

    plan = plan_ref[...].astype(f32)
    cap = plan.shape[1]
    leaving = FACES * cap
    wide = jnp.concatenate(
        [jnp.broadcast_to(plan[q : q + 1], (cap, cap)) for q in range(FACES)], axis=0
    )
    diagonal = (iota((leaving, cap), 0) & (cap - 1)) == iota((leaving, cap), 1)
    chosen = jnp.sum(jnp.where(diagonal, wide, 0.0), axis=1, keepdims=True)
    picked = jnp.where(iota((leaving, count), 1).astype(f32) == chosen, 1.0, 0.0).astype(f32)
    taken = jnp.sum(picked, axis=0, keepdims=True)
    picker = jnp.concatenate([picked, jnp.zeros((128 - leaving, count), f32)], axis=0).astype(bf16)
    full = jnp.concatenate([record, anchor, living, jnp.zeros((2, count), f32)], axis=0)

    def thirds(value):
        high = value.astype(bf16).astype(f32)
        rest = value - high
        middle = rest.astype(bf16).astype(f32)
        return jnp.concatenate([high, middle, rest - middle], axis=0).astype(bf16)

    def pick(dot, value):
        got = dot(thirds(value), picker)
        return got[0:32] + got[32:64] + got[64:96]

    some = pick(dot_nt, full)
    some_tables = axis_tables(some[26:29], some[21:24])
    fill_tables(some_high, some_low, some_tables)

    for copy in xy_copies:
        copy.wait_recv()
    partial = grid_ref[...]
    low_side = open_side(y_recv[0])
    high_side = open_side(y_recv[1])
    middle = jnp.zeros((8, LANES - 256), f32)
    corner = [open_corner(c_recv[number]) for number in range(4)]
    low_rows = x_recv[0] + jnp.concatenate([corner[0], middle, corner[1]], axis=1)
    high_rows = x_recv[1] + jnp.concatenate([corner[2], middle, corner[3]], axis=1)
    totals = jnp.concatenate(
        [
            partial[:, 0:128] + low_side,
            partial[:, 128 : LANES - 128],
            partial[:, LANES - 128 :] + high_side,
        ],
        axis=1,
    )
    totals = jnp.concatenate(
        [totals[0:8] + low_rows, totals[8 : ROWS - 8], totals[ROWS - 8 :] + high_rows], axis=0
    )
    for copy in z_copies:
        copy.wait_recv()

    def from_z(ref, *index):
        if pair_z:
            return ref[(0,) + index]
        value = ref[(1,) + index]
        return jnp.where((iota(value.shape, 1) & 3) < 2, value, ref[(0,) + index])

    face_lane = iota((8, 128), 1)
    face_side = {1: face_lane < 8, -1: (face_lane >= 4 * (SPAN - 2)) & (face_lane < 4 * SPAN)}
    face_start = {1: 0, -1: 4 * (SPAN - 2)}
    edge = {step: from_z(e_recv, number) for number, step in enumerate(sides)}
    shared = open_face(from_z(z_recv))
    for g in range(ROWS // 8):
        for j in (1, -1):
            rolled = pltpu.roll(edge[0, j], (face_start[j] - 8 * g) % 128, 1)
            shared[g] = jnp.where(face_side[j], shared[g] + rolled, shared[g])
    for i in (1, -1):
        g = 0 if i > 0 else ROWS // 8 - 1
        shared[g] = shared[g] + edge[i, 0]
        for j in (1, -1):
            line = open_line(from_z(l_recv, corners.index((i, j))), face_start[j])
            shared[g] = jnp.where(face_side[j], shared[g] + line, shared[g])
    spread_sum = dot_nn(stacked(jnp.concatenate(shared, axis=0)), spread_ref[...])
    totals = totals + spread_sum[:ROWS] + spread_sum[ROWS:]

    channel = iota((ROWS, LANES), 0) & 3
    mass_of = jnp.where(
        channel == 1,
        pltpu.roll(totals, 1, 0),
        jnp.where(channel == 2, pltpu.roll(totals, 2, 0), pltpu.roll(totals, 3, 0)),
    )
    velocity = totals / jnp.maximum(mass_of, mass_floor)
    velocity = jnp.where(channel == 3, velocity - time_step * gravity, velocity)
    velocity = jnp.where(channel == 0, 0.0, velocity)
    velocity = jnp.concatenate([velocity, velocity * lane_y, velocity * lane_z], axis=0)

    read_back(
        leave_ref, some, some[26:29], some[29:30], some_tables, some_high, some_low, velocity
    )
    m_send[...] = turned(leave_ref[...])[:leaving].reshape(FACES, cap, 128)
    m_steps = ((1, 0, 0), (-1, 0, 0), (0, 1, 0), (0, -1, 0), (0, 0, 1), (0, 0, -1))
    m_copies = [
        send(m_send.at[slot], come_ref.at[slot], m_sems, slot, step)
        for slot, step in enumerate(m_steps)
    ]
    read_back(new_ref, record, anchor, living, tables, high_ref, low_ref, velocity)
    for copy in xy_copies + z_copies + m_copies:
        copy.wait_send()
    for copy in m_copies:
        copy.wait_recv()
    placed = pick(dot_nn, turned(come_ref[...].reshape(leaving, 128))[:32])
    out_ref[...] = jnp.where(taken > 0.0, placed, new_ref[...])[0:26]


def body(sizes, particles, block_ids, node_offsets, live_count, migrations):
    count = particles.shape[1]
    vmem = pl.BlockSpec(memory_space=pltpu.VMEM)
    return pl.pallas_call(
        functools.partial(kernel, sizes),
        out_shape=pltpu.VMEM(particles.shape, f32),
        in_specs=[pl.BlockSpec(memory_space=pltpu.HBM)] * 5,
        out_specs=vmem,
        scratch_shapes=[
            pltpu.SMEM((1,), jnp.int32),
            pltpu.VMEM(particles.shape, f32),
            pltpu.VMEM((1, count), jnp.int32),
            pltpu.VMEM((1, count), jnp.int32),
            pltpu.VMEM(migrations.shape, jnp.int32),
            pltpu.SemaphoreType.DMA((5,)),
            pltpu.VMEM((LANES, count), bf16),
            pltpu.VMEM((LANES, count), bf16),
            pltpu.VMEM((128, LANES), bf16),
            pltpu.VMEM((128, LANES), bf16),
            pltpu.VMEM((128, 128), bf16),
            pltpu.VMEM((LANES, 128), bf16),
            pltpu.VMEM((LANES, 128), bf16),
            pltpu.VMEM((ROWS, LANES), f32),
            pltpu.VMEM((FACE_ROWS, 128), f32),
            pltpu.VMEM((2, FACE_ROWS, 128), f32),
            pltpu.VMEM((4, 8, 128), f32),
            pltpu.VMEM((2, 4, 8, 128), f32),
            pltpu.VMEM((2, 8, LANES), f32),
            pltpu.VMEM((2, THIRD, 128), f32),
            pltpu.VMEM((2, THIRD, 128), f32),
            pltpu.VMEM((4, 4, 128), f32),
            pltpu.VMEM((4, 4, 128), f32),
            pltpu.VMEM((4, 1, 128), f32),
            pltpu.VMEM((2, 4, 1, 128), f32),
            pltpu.VMEM((32, 128), f32),
            pltpu.VMEM((FACES, migrations.shape[1], 128), f32),
            pltpu.VMEM((FACES, migrations.shape[1], 128), f32),
            pltpu.VMEM((32, count), f32),
            pltpu.SemaphoreType.DMA((2, 18)),
            pltpu.SemaphoreType.DMA((2, 8)),
            pltpu.SemaphoreType.DMA((2, 6)),
        ],
        compiler_params=pltpu.CompilerParams(
            collective_id=0, has_side_effects=True, vmem_limit_bytes=60 * 1024 * 1024
        ),
        name="substep",
    )(
        live_count,
        particles,
        block_ids.reshape(1, count),
        node_offsets.reshape(1, count),
        migrations,
    )


def solution(mesh):
    sizes = tuple(mesh.shape[name] for name in AXES)
    return jax.shard_map(
        functools.partial(body, sizes),
        mesh=mesh,
        in_specs=(
            P(None, AXES),
            P(AXES),
            P(AXES),
            P(AXES),
            P(None, AXES),
        ),
        out_specs=P(None, AXES),
        check_vma=False,
    )
```

```python
import functools

import jax
import jax.numpy as jnp
from jax import lax
from jax.experimental import pallas as pl
from jax.experimental.pallas import tpu as pltpu
from jax.sharding import PartitionSpec as P

BLK = 2
AXES = ("gx", "gy", "gz")
SPAN = 8 * BLK + 2
STRIDE = 24
ROWS = 4 * SPAN
LANES = 512
USED = STRIDE * SPAN
EDGE = 2 * STRIDE
SIDE = STRIDE + SPAN
THIRD = ROWS // 3
HEAD = 40
FACE_ROWS = HEAD + 8
CENTRE = 0.5 * (SPAN - 1)
FACES = 6

time_step = 0.05
stress_gain = 0.2
shear_zero = 5.0
bulk_zero = 5.0
harden_rate = 10.0
mass_floor = 0.1
gravity = 9.8

f32 = jnp.float32
bf16 = jnp.bfloat16
MESH = pl.DeviceIdType.MESH


def iota(shape, dim):
    return lax.broadcasted_iota(jnp.int32, shape, dim)


def split(value):
    high = value.astype(bf16)
    return high, (value - high.astype(f32)).astype(bf16)


def stacked(value):
    high = value.astype(bf16).astype(f32)
    return jnp.concatenate([high, value - high], axis=0).astype(bf16)


def dot_nt(left, right):
    return lax.dot_general(left, right, (((1,), (1,)), ((), ())), preferred_element_type=f32)


def dot_nn(left, right):
    return lax.dot_general(left, right, (((1,), (0,)), ((), ())), preferred_element_type=f32)


def contract(dot, left, right_high, right_low):
    rows = left.shape[0]
    both = dot(stacked(left), right_high)
    return both[:rows] + both[rows:] + dot(left.astype(bf16), right_low)


def spline(place, anchor, fraction):
    apart = (place - anchor) - fraction
    size = jnp.abs(apart)
    outer = jnp.maximum(1.5 - size, 0.0)
    inner = jnp.maximum(0.5 - size, 0.0)
    weight = 0.5 * outer * outer - 1.5 * inner * inner
    return weight, weight * apart


def axis_tables(anchor, fraction):
    count = fraction.shape[1]
    line = iota((STRIDE, count), 0).astype(f32)
    line_x = jnp.right_shift(iota((ROWS, count), 0), 2).astype(f32)
    return (
        spline(line_x, anchor[0:1], fraction[0:1]),
        spline(line, anchor[1:2], fraction[1:2]),
        spline(line, anchor[2:3], fraction[2:3]),
    )


def store_pair(high_ref, low_ref, row, outer_line, inner_line, picks):
    pair = jnp.concatenate([outer_line[p : p + 1] * inner_line for p in picks], axis=0)
    high, low = split(pair)
    high_ref[row : row + EDGE, :] = high
    low_ref[row : row + EDGE, :] = low


def fill_tables(high_ref, low_ref, tables):
    _, (weight_y, _), (weight_z, _) = tables
    count = weight_y.shape[1]
    for pair in range(SPAN // 2):
        store_pair(high_ref, low_ref, EDGE * pair, weight_y, weight_z, (2 * pair, 2 * pair + 1))
    for ref in (high_ref, low_ref):
        ref[USED:LANES, :] = jnp.zeros((LANES - USED, count), bf16)


def fill_masks(gather_ref, spread_ref, corner_ref):
    lane = iota((128, LANES), 1)
    row = iota((128, LANES), 0)
    line = jnp.right_shift(lane * 2731, 16)
    place = lane - STRIDE * line
    k = row & 3
    same = (jnp.right_shift(row, 2) == line) & (line < SPAN)
    near = jnp.where(k < 2, k, k + (SPAN - 4))
    far = jnp.where(k < 2, k + (SPAN - 2), k - 2)
    gather_ref[...] = jnp.where(same & (place == near), 1.0, 0.0).astype(bf16)
    corner_ref[...] = jnp.where(
        jnp.where(line < 2, line, line + (SPAN - 4)) == jnp.right_shift(row, 2),
        jnp.where((place == near) & (line < 4), 1.0, 0.0),
        0.0,
    )[:, :128].astype(bf16)
    spread_ref[...] = jnp.where(same & (place == far), 1.0, 0.0).astype(bf16)


def pack_edges(face):
    group = jnp.right_shift(iota((8, 128), 1), 3)
    tiles = []
    for start in (4 * (SPAN - 2), 0):
        tile = jnp.zeros((8, 128), f32)
        for g in range(ROWS // 8):
            rolled = pltpu.roll(face[8 * g : 8 * g + 8], (8 * g - start) % 128, 1)
            tile = jnp.where(group == g, rolled, tile)
        tiles.append(tile)
    return tiles


def lane_places(lanes):
    lane = iota((1, lanes), 1)
    line = jnp.right_shift(lane * 2731, 16)
    return line.astype(f32) - CENTRE, (lane - STRIDE * line).astype(f32) - CENTRE


def combine(parts, place_y, place_z):
    return parts[:ROWS] + place_y * parts[ROWS : 2 * ROWS] + place_z * parts[2 * ROWS :]


def product(left, right):
    return [
        [
            left[i][0] * right[0][j] + left[i][1] * right[1][j] + left[i][2] * right[2][j]
            for j in range(3)
        ]
        for i in range(3)
    ]


def transposed(matrix):
    return [[matrix[j][i] for j in range(3)] for i in range(3)]


def pack(row):
    count = row.shape[1]
    return jnp.concatenate([row[:, s : s + 128] for s in range(0, count, 128)], axis=0)


def unpack(block):
    return jnp.concatenate([block[s : s + 1] for s in range(block.shape[0])], axis=1)


def stress(deform, plastic):
    rotation = deform
    for _ in range(5):
        inner = product(transposed(rotation), rotation)
        inner = [[(3.0 - inner[i][j]) if i == j else -inner[i][j] for j in range(3)] for i in range(3)]
        rotation = product(rotation, inner)
        rotation = [[0.5 * entry for entry in line] for line in rotation]
    f = deform
    volume = (
        f[0][0] * (f[1][1] * f[2][2] - f[1][2] * f[2][1])
        - f[0][1] * (f[1][0] * f[2][2] - f[1][2] * f[2][0])
        + f[0][2] * (f[1][0] * f[2][1] - f[1][1] * f[2][0])
    )
    harden = jnp.exp(harden_rate * (1.0 - plastic))
    shear = 2.0 * shear_zero * harden
    bulk = bulk_zero * harden * (volume - 1.0) * volume
    apart = [[f[i][j] - rotation[i][j] for j in range(3)] for i in range(3)]
    tau = product(apart, transposed(f))
    return [
        [shear * tau[i][j] + bulk if i == j else shear * tau[i][j] for j in range(3)]
        for i in range(3)
    ]


def read_back(out_ref, record, anchor, living, tables, high_ref, low_ref, velocity):
    count = record.shape[1]
    (weight_x, shift_x), _, _ = tables
    reads = contract(dot_nn, velocity, high_ref[...], low_ref[...])

    def fold(value):
        total = value[0:8]
        for row in range(8, ROWS, 8):
            total = total + value[row : row + 8]
        return total[0:4] + total[4:8]

    first = reads[:ROWS]
    speed = fold(weight_x * first) * living
    place = anchor + record[21:24] - CENTRE
    along = [
        4.0 * living * fold(shift_x * first),
        4.0 * (living * fold(weight_x * reads[ROWS : 2 * ROWS]) - place[1:2] * speed),
        4.0 * (living * fold(weight_x * reads[2 * ROWS :]) - place[2:3] * speed),
    ]
    out_ref[0:3, :] = speed[1:4]
    deform = [record[12 + 3 * k : 15 + 3 * k] for k in range(3)]
    for i in range(3):
        push = jnp.zeros((3, count), f32)
        for j in range(3):
            entry = along[j][1 + i : 2 + i]
            out_ref[3 + 3 * i + j : 4 + 3 * i + j, :] = entry
            push = push + entry * deform[j]
        out_ref[12 + 3 * i : 15 + 3 * i, :] = deform[i] * living + time_step * push
    out_ref[21:24, :] = record[21:24] * living + time_step * speed[1:4]
    out_ref[24:26, :] = record[24:26] * living
    out_ref[26:32, :] = jnp.zeros((6, count), f32)


def pack_side(tile):
    lane = iota((THIRD, 128), 1)
    middle = pltpu.roll(tile[THIRD : 2 * THIRD], SIDE, 1)
    last = pltpu.roll(tile[2 * THIRD :], 2 * SIDE, 1)
    return jnp.where(lane < SIDE, tile[:THIRD], jnp.where(lane < 2 * SIDE, middle, last))


def open_side(packed):
    rolled = [packed] + [pltpu.roll(packed, 128 - g * SIDE, 1) for g in (1, 2)]
    return jnp.where(iota((ROWS, 128), 1) < SIDE, jnp.concatenate(rolled, axis=0), 0.0)


def pack_corner(tile):
    return jnp.where(iota((4, 128), 1) < 64, tile[0:4], pltpu.roll(tile[4:8], 64, 1))


def open_corner(packed):
    full = jnp.concatenate([packed, pltpu.roll(packed, 64, 1)], axis=0)
    return jnp.where(iota((8, 128), 1) < SIDE, full, 0.0)


def pack_face(face):
    rest = jnp.concatenate([face[HEAD:], jnp.zeros((2 * HEAD - ROWS, 128), f32)], axis=0)
    head = jnp.where(iota((HEAD, 128), 1) < 72, face[:HEAD], pltpu.roll(rest, 72, 1))
    group = jnp.right_shift(iota((8, 128), 1), 4)
    tail = jnp.zeros((8, 128), f32)
    for g in range((ROWS - HEAD) // 8):
        rolled = pltpu.roll(rest[8 * g : 8 * g + 8], (16 * g - 56) % 128, 1)
        tail = jnp.where(group == g, rolled, tail)
    return jnp.concatenate([head, tail], axis=0)


def open_face(packed):
    tiles = [packed[r : r + 8] for r in range(0, HEAD, 8)]
    tail = packed[HEAD:]
    lane = iota((8, 128), 1)
    for g in range((ROWS - HEAD) // 8):
        body_part = pltpu.roll(packed[8 * g : 8 * g + 8], 56, 1)
        tiles.append(jnp.where(lane < 56, body_part, pltpu.roll(tail, (56 - 16 * g) % 128, 1)))
    return tiles


def pack_line(tile, start):
    group = jnp.right_shift(iota((8, 128), 1), 3)
    row = iota((8, 128), 0)
    total = jnp.zeros((8, 128), f32)
    for r in range(8):
        rolled = pltpu.roll(tile, (8 * r - start) % 128, 1)
        total = jnp.where((group == r) & (row == r), rolled, total)
    return jnp.sum(total, axis=0, keepdims=True)


def open_line(packed, start):
    wide = jnp.broadcast_to(packed, (8, 128))
    row = iota((8, 128), 0)
    total = pltpu.roll(wide, start, 1) if start else wide
    for r in range(1, 8):
        total = jnp.where(row == r, pltpu.roll(wide, (start - 8 * r) % 128, 1), total)
    return total


def turned(value):
    rows = jnp.zeros((128 - value.shape[0], 128), f32)
    return jnp.concatenate([value, rows], axis=0).T


def kernel(
    sizes,
    live_hbm,
    record_hbm,
    block_hbm,
    offset_hbm,
    plan_hbm,
    out_ref,
    live_ref,
    record_ref,
    block_ref,
    offset_ref,
    plan_ref,
    in_sems,
    high_ref,
    low_ref,
    gather_ref,
    spread_ref,
    corner_ref,
    some_high,
    some_low,
    grid_ref,
    z_send,
    z_recv,
    e_send,
    e_recv,
    x_recv,
    y_send,
    y_recv,
    c_send,
    c_recv,
    l_send,
    l_recv,
    leave_ref,
    m_send,
    come_ref,
    new_ref,
    z_sems,
    xy_sems,
    m_sems,
):
    operands = (
        (record_hbm, record_ref),
        (block_hbm, block_ref),
        (offset_hbm, offset_ref),
        (live_hbm, live_ref),
        (plan_hbm, plan_ref),
    )
    in_copies = [
        pltpu.make_async_copy(source, target, in_sems.at[slot])
        for slot, (source, target) in enumerate(operands)
    ]
    for copy in in_copies:
        copy.start()
    me = [lax.axis_index(name) for name in AXES]

    def at(*step):
        return tuple(
            lax.rem(me[a] + step[a] + sizes[a], sizes[a]) if step[a] else me[a] for a in range(3)
        )

    pair_z = sizes[2] == 2
    z_steps = ((0, 0, 1),) if pair_z else ((0, 0, 1), (0, 0, -1))
    xy_steps = tuple((i, j, 0) for i in (0, 1, -1) for j in (1, -1, 0) if i or j)
    barrier = pltpu.get_barrier_semaphore()
    around = xy_steps + tuple((i, j, k) for _, _, k in z_steps for i, j, _ in ((0, 0, 0),) + xy_steps)
    for step in around:
        pl.semaphore_signal(barrier, inc=1, device_id=at(*step), device_id_type=MESH)

    fill_masks(gather_ref, spread_ref, corner_ref)
    for copy in in_copies:
        copy.wait()
    count = record_ref.shape[1]
    record = record_ref[...]
    fraction = record[21:24]
    blocks = block_ref[...]
    offsets = offset_ref[...]
    anchor = (
        jnp.concatenate(
            [
                8 * jnp.right_shift(blocks, 2) + jnp.right_shift(offsets, 6),
                8 * (jnp.right_shift(blocks, 1) & 1) + (jnp.right_shift(offsets, 3) & 7),
                8 * (blocks & 1) + (offsets & 7),
            ],
            axis=0,
        )
        + 1
    ).astype(f32)
    living = jnp.where(iota((1, count), 1) < live_ref[0], 1.0, 0.0).astype(f32)

    tables = axis_tables(anchor, fraction)
    fill_tables(high_ref, low_ref, tables)

    plastic = pack(record[25:26])
    deform = [[pack(record[12 + 3 * i + j : 13 + 3 * i + j]) for j in range(3)] for i in range(3)]
    tau = stress(deform, plastic)
    mass = record[24:25]
    held = mass * living
    coupling = [
        [
            (mass * record[3 + 3 * i + j : 4 + 3 * i + j] - stress_gain * unpack(tau[i][j])) * living
            for j in range(3)
        ]
        for i in range(3)
    ]
    none = jnp.zeros((1, count), f32)
    places = anchor + fraction - CENTRE
    momentum = [
        held * record[i : i + 1] - coupling[i][1] * places[1:2] - coupling[i][2] * places[2:3]
        for i in range(3)
    ]
    base = jnp.concatenate([held] + momentum + [held] + momentum, axis=0)
    pushes = [
        jnp.concatenate([none, coupling[0][j], coupling[1][j], coupling[2][j]] * 2, axis=0)
        for j in range(3)
    ]
    weight_x, shift_x = tables[0]
    tiles = range(0, ROWS, 8)
    left = jnp.concatenate(
        [base * weight_x[r : r + 8] + pushes[0] * shift_x[r : r + 8] for r in tiles]
        + [pushes[1] * weight_x[r : r + 8] for r in tiles]
        + [pushes[2] * weight_x[r : r + 8] for r in tiles],
        axis=0,
    )

    def send(source, target, sems, slot, step):
        copy = pltpu.make_async_remote_copy(
            src_ref=source,
            dst_ref=target,
            send_sem=sems.at[0, slot],
            recv_sem=sems.at[1, slot],
            device_id=at(*step),
            device_id_type=MESH,
        )
        copy.start()
        return copy

    corners = ((1, 1), (1, -1), (-1, 1), (-1, -1))
    sides = ((0, 1), (0, -1), (1, 0), (-1, 0))
    last = {1: ROWS - 8, -1: 0}
    last_face = {1: 4 * (SPAN - 2), -1: 0}

    lane_y, lane_z = lane_places(LANES)
    cut = LANES - 128

    def outside(value, axis):
        low, high = lax.slice_in_dim(value, 0, 128, axis=axis), lax.slice_in_dim(value, cut, LANES, axis=axis)
        return jnp.concatenate([low, high], axis=axis)

    ends = combine(
        contract(
            dot_nt,
            left,
            *[jnp.concatenate([ref[0:128, :], ref[cut:, :]], axis=0) for ref in (high_ref, low_ref)],
        ),
        outside(lane_y, 1),
        outside(lane_z, 1),
    )
    ends = {-1: ends[:, :128], 1: ends[:, 128:]}
    y_send[0] = pack_side(ends[1])
    y_send[1] = pack_side(ends[-1])
    for number, (i, j) in enumerate(corners):
        c_send[number] = pack_corner(ends[j][last[i] : last[i] + 8])
    pl.semaphore_wait(barrier, len(around))
    xy_copies = []
    for number, j in enumerate((1, -1)):
        xy_copies.append(send(y_send.at[number], y_recv.at[number], xy_sems, number, (0, j, 0)))
    for number, (i, j) in enumerate(corners):
        xy_copies.append(send(c_send.at[number], c_recv.at[number], xy_sems, 2 + number, (i, j, 0)))

    both = jnp.where(iota((ROWS, 128), 1) < EDGE, ends[-1], pltpu.roll(ends[1], EDGE, 1))
    face = dot_nt(stacked(both), corner_ref[...])
    face = face[:ROWS] + face[ROWS:]
    e_send[0], e_send[1] = pack_edges(face)
    for number, (i, j) in enumerate(corners):
        l_send[number] = pack_line(face[last[i] : last[i] + 8], last_face[j])
    z_copies = []

    def send_edges(numbers):
        for slot, (_, _, k) in enumerate(z_steps):
            for number in numbers:
                i, j = sides[number]
                target = e_recv.at[slot, number]
                z_copies.append(
                    send(e_send.at[number], target, z_sems, 9 * slot + 1 + number, (i, j, k))
                )

    send_edges((0, 1))
    for slot, (_, _, k) in enumerate(z_steps):
        for number, (i, j) in enumerate(corners):
            target = l_recv.at[slot, number]
            z_copies.append(
                send(l_send.at[number], target, z_sems, 9 * slot + 5 + number, (i, j, k))
            )

    inside = combine(
        contract(dot_nt, left, high_ref[128:cut, :], low_ref[128:cut, :]),
        lane_y[:, 128:cut],
        lane_z[:, 128:cut],
    )
    partial = jnp.concatenate([ends[-1], inside, ends[1]], axis=1)
    grid_ref[...] = partial
    for number, i in enumerate((1, -1)):
        source = grid_ref.at[pl.ds(last[i], 8), :]
        xy_copies.append(send(source, x_recv.at[number], xy_sems, 6 + number, (i, 0, 0)))
    face = dot_nt(stacked(partial), gather_ref[...])
    face = face[:ROWS] + face[ROWS:]
    z_send[...] = pack_face(face)
    for slot, (_, _, k) in enumerate(z_steps):
        z_copies.append(send(z_send, z_recv.at[slot], z_sems, 9 * slot, (0, 0, k)))
    e_send[2] = face[last[1] : last[1] + 8]
    e_send[3] = face[last[-1] : last[-1] + 8]
    send_edges((2, 3))

    plan = plan_ref[...].astype(f32)
    cap = plan.shape[1]
    leaving = FACES * cap
    wide = jnp.concatenate(
        [jnp.broadcast_to(plan[q : q + 1], (cap, cap)) for q in range(FACES)], axis=0
    )
    diagonal = (iota((leaving, cap), 0) & (cap - 1)) == iota((leaving, cap), 1)
    chosen = jnp.sum(jnp.where(diagonal, wide, 0.0), axis=1, keepdims=True)
    picked = jnp.where(iota((leaving, count), 1).astype(f32) == chosen, 1.0, 0.0).astype(f32)
    taken = jnp.sum(picked, axis=0, keepdims=True)
    picker = jnp.concatenate([picked, jnp.zeros((128 - leaving, count), f32)], axis=0).astype(bf16)
    full = jnp.concatenate([record, anchor, living, jnp.zeros((2, count), f32)], axis=0)

    def thirds(value):
        high = value.astype(bf16).astype(f32)
        rest = value - high
        middle = rest.astype(bf16).astype(f32)
        return jnp.concatenate([high, middle, rest - middle], axis=0).astype(bf16)

    def pick(dot, value):
        got = dot(thirds(value), picker)
        return got[0:32] + got[32:64] + got[64:96]

    some = pick(dot_nt, full)
    some_tables = axis_tables(some[26:29], some[21:24])
    fill_tables(some_high, some_low, some_tables)

    for copy in xy_copies:
        copy.wait_recv()
    partial = grid_ref[...]
    low_side = open_side(y_recv[0])
    high_side = open_side(y_recv[1])
    middle = jnp.zeros((8, LANES - 256), f32)
    corner = [open_corner(c_recv[number]) for number in range(4)]
    low_rows = x_recv[0] + jnp.concatenate([corner[0], middle, corner[1]], axis=1)
    high_rows = x_recv[1] + jnp.concatenate([corner[2], middle, corner[3]], axis=1)
    totals = jnp.concatenate(
        [
            partial[:, 0:128] + low_side,
            partial[:, 128 : LANES - 128],
            partial[:, LANES - 128 :] + high_side,
        ],
        axis=1,
    )
    totals = jnp.concatenate(
        [totals[0:8] + low_rows, totals[8 : ROWS - 8], totals[ROWS - 8 :] + high_rows], axis=0
    )
    for copy in z_copies:
        copy.wait_recv()

    def from_z(ref, *index):
        if pair_z:
            return ref[(0,) + index]
        value = ref[(1,) + index]
        return jnp.where((iota(value.shape, 1) & 3) < 2, value, ref[(0,) + index])

    face_lane = iota((8, 128), 1)
    face_side = {1: face_lane < 8, -1: (face_lane >= 4 * (SPAN - 2)) & (face_lane < 4 * SPAN)}
    face_start = {1: 0, -1: 4 * (SPAN - 2)}
    edge = {step: from_z(e_recv, number) for number, step in enumerate(sides)}
    shared = open_face(from_z(z_recv))
    for g in range(ROWS // 8):
        for j in (1, -1):
            rolled = pltpu.roll(edge[0, j], (face_start[j] - 8 * g) % 128, 1)
            shared[g] = jnp.where(face_side[j], shared[g] + rolled, shared[g])
    for i in (1, -1):
        g = 0 if i > 0 else ROWS // 8 - 1
        shared[g] = shared[g] + edge[i, 0]
        for j in (1, -1):
            line = open_line(from_z(l_recv, corners.index((i, j))), face_start[j])
            shared[g] = jnp.where(face_side[j], shared[g] + line, shared[g])
    spread_sum = dot_nn(stacked(jnp.concatenate(shared, axis=0)), spread_ref[...])
    totals = totals + spread_sum[:ROWS] + spread_sum[ROWS:]

    channel = iota((ROWS, LANES), 0) & 3
    mass_of = jnp.where(
        channel == 1,
        pltpu.roll(totals, 1, 0),
        jnp.where(channel == 2, pltpu.roll(totals, 2, 0), pltpu.roll(totals, 3, 0)),
    )
    velocity = totals / jnp.maximum(mass_of, mass_floor)
    velocity = jnp.where(channel == 3, velocity - time_step * gravity, velocity)
    velocity = jnp.where(channel == 0, 0.0, velocity)
    velocity = jnp.concatenate([velocity, velocity * lane_y, velocity * lane_z], axis=0)

    read_back(
        leave_ref, some, some[26:29], some[29:30], some_tables, some_high, some_low, velocity
    )
    m_send[...] = turned(leave_ref[...])[:leaving].reshape(FACES, cap, 128)
    m_steps = ((1, 0, 0), (-1, 0, 0), (0, 1, 0), (0, -1, 0), (0, 0, 1), (0, 0, -1))
    m_copies = [
        send(m_send.at[slot], come_ref.at[slot], m_sems, slot, step)
        for slot, step in enumerate(m_steps)
    ]
    read_back(new_ref, record, anchor, living, tables, high_ref, low_ref, velocity)
    for copy in xy_copies + z_copies + m_copies:
        copy.wait_send()
    for copy in m_copies:
        copy.wait_recv()
    placed = pick(dot_nn, turned(come_ref[...].reshape(leaving, 128))[:32])
    out_ref[...] = jnp.where(taken > 0.0, placed, new_ref[...])[0:26]


def body(sizes, particles, block_ids, node_offsets, live_count, migrations):
    count = particles.shape[1]
    vmem = pl.BlockSpec(memory_space=pltpu.VMEM)
    return pl.pallas_call(
        functools.partial(kernel, sizes),
        out_shape=pltpu.VMEM(particles.shape, f32),
        in_specs=[pl.BlockSpec(memory_space=pltpu.HBM)] * 5,
        out_specs=vmem,
        scratch_shapes=[
            pltpu.SMEM((1,), jnp.int32),
            pltpu.VMEM(particles.shape, f32),
            pltpu.VMEM((1, count), jnp.int32),
            pltpu.VMEM((1, count), jnp.int32),
            pltpu.VMEM(migrations.shape, jnp.int32),
            pltpu.SemaphoreType.DMA((5,)),
            pltpu.VMEM((LANES, count), bf16),
            pltpu.VMEM((LANES, count), bf16),
            pltpu.VMEM((128, LANES), bf16),
            pltpu.VMEM((128, LANES), bf16),
            pltpu.VMEM((128, 128), bf16),
            pltpu.VMEM((LANES, 128), bf16),
            pltpu.VMEM((LANES, 128), bf16),
            pltpu.VMEM((ROWS, LANES), f32),
            pltpu.VMEM((FACE_ROWS, 128), f32),
            pltpu.VMEM((2, FACE_ROWS, 128), f32),
            pltpu.VMEM((4, 8, 128), f32),
            pltpu.VMEM((2, 4, 8, 128), f32),
            pltpu.VMEM((2, 8, LANES), f32),
            pltpu.VMEM((2, THIRD, 128), f32),
            pltpu.VMEM((2, THIRD, 128), f32),
            pltpu.VMEM((4, 4, 128), f32),
            pltpu.VMEM((4, 4, 128), f32),
            pltpu.VMEM((4, 1, 128), f32),
            pltpu.VMEM((2, 4, 1, 128), f32),
            pltpu.VMEM((32, 128), f32),
            pltpu.VMEM((FACES, migrations.shape[1], 128), f32),
            pltpu.VMEM((FACES, migrations.shape[1], 128), f32),
            pltpu.VMEM((32, count), f32),
            pltpu.SemaphoreType.DMA((2, 18)),
            pltpu.SemaphoreType.DMA((2, 8)),
            pltpu.SemaphoreType.DMA((2, 6)),
        ],
        compiler_params=pltpu.CompilerParams(
            collective_id=0, has_side_effects=True, vmem_limit_bytes=60 * 1024 * 1024
        ),
        name="substep",
    )(
        live_count,
        particles,
        block_ids.reshape(1, count),
        node_offsets.reshape(1, count),
        migrations,
    )


def solution(mesh):
    sizes = tuple(mesh.shape[name] for name in AXES)
    return jax.shard_map(
        functools.partial(body, sizes),
        mesh=mesh,
        in_specs=(
            P(None, AXES),
            P(AXES),
            P(AXES),
            P(AXES),
            P(None, AXES),
        ),
        out_specs=P(None, AXES),
        check_vma=False,
    )
```

```python
import functools

import jax
import jax.numpy as jnp
from jax import lax
from jax.experimental import pallas as pl
from jax.experimental.pallas import tpu as pltpu
from jax.sharding import PartitionSpec as P

BLK = 2
AXES = ("gx", "gy", "gz")
SPAN = 8 * BLK + 2
STRIDE = 24
ROWS = 4 * SPAN
LANES = 512
USED = STRIDE * SPAN
EDGE = 2 * STRIDE
SIDE = STRIDE + SPAN
THIRD = ROWS // 3
HEAD = 40
FACE_ROWS = HEAD + 8
CENTRE = 0.5 * (SPAN - 1)
FACES = 6

time_step = 0.05
stress_gain = 0.2
shear_zero = 5.0
bulk_zero = 5.0
harden_rate = 10.0
mass_floor = 0.1
gravity = 9.8

f32 = jnp.float32
bf16 = jnp.bfloat16
MESH = pl.DeviceIdType.MESH


def iota(shape, dim):
    return lax.broadcasted_iota(jnp.int32, shape, dim)


def split(value):
    high = value.astype(bf16)
    return high, (value - high.astype(f32)).astype(bf16)


def stacked(value):
    high = value.astype(bf16).astype(f32)
    return jnp.concatenate([high, value - high], axis=0).astype(bf16)


def dot_nt(left, right):
    return lax.dot_general(left, right, (((1,), (1,)), ((), ())), preferred_element_type=f32)


def dot_nn(left, right):
    return lax.dot_general(left, right, (((1,), (0,)), ((), ())), preferred_element_type=f32)


def contract(dot, left, right_high, right_low):
    rows = left.shape[0]
    both = dot(stacked(left), right_high)
    return both[:rows] + both[rows:] + dot(left.astype(bf16), right_low)


def spline(place, anchor, fraction):
    apart = (place - anchor) - fraction
    size = jnp.abs(apart)
    outer = jnp.maximum(1.5 - size, 0.0)
    inner = jnp.maximum(0.5 - size, 0.0)
    weight = 0.5 * outer * outer - 1.5 * inner * inner
    return weight, weight * apart


def axis_tables(anchor, fraction):
    count = fraction.shape[1]
    line = iota((STRIDE, count), 0).astype(f32)
    line_x = jnp.right_shift(iota((ROWS, count), 0), 2).astype(f32)
    return (
        spline(line_x, anchor[0:1], fraction[0:1]),
        spline(line, anchor[1:2], fraction[1:2]),
        spline(line, anchor[2:3], fraction[2:3]),
    )


def store_pair(high_ref, low_ref, row, outer_line, inner_line, picks):
    pair = jnp.concatenate([outer_line[p : p + 1] * inner_line for p in picks], axis=0)
    high, low = split(pair)
    high_ref[row : row + EDGE, :] = high
    low_ref[row : row + EDGE, :] = low


def fill_tables(high_ref, low_ref, tables):
    _, (weight_y, _), (weight_z, _) = tables
    count = weight_y.shape[1]
    for pair in range(SPAN // 2):
        store_pair(high_ref, low_ref, EDGE * pair, weight_y, weight_z, (2 * pair, 2 * pair + 1))
    for ref in (high_ref, low_ref):
        ref[USED:LANES, :] = jnp.zeros((LANES - USED, count), bf16)


def fill_masks(gather_ref, spread_ref, corner_ref):
    lane = iota((128, LANES), 1)
    row = iota((128, LANES), 0)
    line = jnp.right_shift(lane * 2731, 16)
    place = lane - STRIDE * line
    k = row & 3
    same = (jnp.right_shift(row, 2) == line) & (line < SPAN)
    near = jnp.where(k < 2, k, k + (SPAN - 4))
    far = jnp.where(k < 2, k + (SPAN - 2), k - 2)
    gather_ref[...] = jnp.where(same & (place == near), 1.0, 0.0).astype(bf16)
    corner_ref[...] = jnp.where(
        jnp.where(line < 2, line, line + (SPAN - 4)) == jnp.right_shift(row, 2),
        jnp.where((place == near) & (line < 4), 1.0, 0.0),
        0.0,
    )[:, :128].astype(bf16)
    spread_ref[...] = jnp.where(same & (place == far), 1.0, 0.0).astype(bf16)


def pack_edges(face):
    group = jnp.right_shift(iota((8, 128), 1), 3)
    tiles = []
    for start in (4 * (SPAN - 2), 0):
        tile = jnp.zeros((8, 128), f32)
        for g in range(ROWS // 8):
            rolled = pltpu.roll(face[8 * g : 8 * g + 8], (8 * g - start) % 128, 1)
            tile = jnp.where(group == g, rolled, tile)
        tiles.append(tile)
    return tiles


def lane_places(lanes):
    lane = iota((1, lanes), 1)
    line = jnp.right_shift(lane * 2731, 16)
    return line.astype(f32) - CENTRE, (lane - STRIDE * line).astype(f32) - CENTRE


def combine(parts, place_y, place_z):
    return parts[:ROWS] + place_y * parts[ROWS : 2 * ROWS] + place_z * parts[2 * ROWS :]


def product(left, right):
    return [
        [
            left[i][0] * right[0][j] + left[i][1] * right[1][j] + left[i][2] * right[2][j]
            for j in range(3)
        ]
        for i in range(3)
    ]


def transposed(matrix):
    return [[matrix[j][i] for j in range(3)] for i in range(3)]


def pack(row):
    count = row.shape[1]
    return jnp.concatenate([row[:, s : s + 128] for s in range(0, count, 128)], axis=0)


def unpack(block):
    return jnp.concatenate([block[s : s + 1] for s in range(block.shape[0])], axis=1)


def stress(deform, plastic):
    rotation = deform
    for _ in range(5):
        inner = product(transposed(rotation), rotation)
        inner = [[(3.0 - inner[i][j]) if i == j else -inner[i][j] for j in range(3)] for i in range(3)]
        rotation = product(rotation, inner)
        rotation = [[0.5 * entry for entry in line] for line in rotation]
    f = deform
    volume = (
        f[0][0] * (f[1][1] * f[2][2] - f[1][2] * f[2][1])
        - f[0][1] * (f[1][0] * f[2][2] - f[1][2] * f[2][0])
        + f[0][2] * (f[1][0] * f[2][1] - f[1][1] * f[2][0])
    )
    harden = jnp.exp(harden_rate * (1.0 - plastic))
    shear = 2.0 * shear_zero * harden
    bulk = bulk_zero * harden * (volume - 1.0) * volume
    apart = [[f[i][j] - rotation[i][j] for j in range(3)] for i in range(3)]
    tau = product(apart, transposed(f))
    return [
        [shear * tau[i][j] + bulk if i == j else shear * tau[i][j] for j in range(3)]
        for i in range(3)
    ]


def read_back(out_ref, record, anchor, living, tables, high_ref, low_ref, velocity):
    count = record.shape[1]
    (weight_x, shift_x), _, _ = tables
    reads = contract(dot_nn, velocity, high_ref[...], low_ref[...])

    def fold(value):
        total = value[0:8]
        for row in range(8, ROWS, 8):
            total = total + value[row : row + 8]
        return total[0:4] + total[4:8]

    first = reads[:ROWS]
    speed = fold(weight_x * first) * living
    place = anchor + record[21:24] - CENTRE
    along = [
        4.0 * living * fold(shift_x * first),
        4.0 * (living * fold(weight_x * reads[ROWS : 2 * ROWS]) - place[1:2] * speed),
        4.0 * (living * fold(weight_x * reads[2 * ROWS :]) - place[2:3] * speed),
    ]
    out_ref[0:3, :] = speed[1:4]
    deform = [record[12 + 3 * k : 15 + 3 * k] for k in range(3)]
    for i in range(3):
        push = jnp.zeros((3, count), f32)
        for j in range(3):
            entry = along[j][1 + i : 2 + i]
            out_ref[3 + 3 * i + j : 4 + 3 * i + j, :] = entry
            push = push + entry * deform[j]
        out_ref[12 + 3 * i : 15 + 3 * i, :] = deform[i] * living + time_step * push
    out_ref[21:24, :] = record[21:24] * living + time_step * speed[1:4]
    out_ref[24:26, :] = record[24:26] * living
    out_ref[26:32, :] = jnp.zeros((6, count), f32)


def pack_side(tile):
    lane = iota((THIRD, 128), 1)
    middle = pltpu.roll(tile[THIRD : 2 * THIRD], SIDE, 1)
    last = pltpu.roll(tile[2 * THIRD :], 2 * SIDE, 1)
    return jnp.where(lane < SIDE, tile[:THIRD], jnp.where(lane < 2 * SIDE, middle, last))


def open_side(packed):
    rolled = [packed] + [pltpu.roll(packed, 128 - g * SIDE, 1) for g in (1, 2)]
    return jnp.where(iota((ROWS, 128), 1) < SIDE, jnp.concatenate(rolled, axis=0), 0.0)


def pack_corner(tile):
    return jnp.where(iota((4, 128), 1) < 64, tile[0:4], pltpu.roll(tile[4:8], 64, 1))


def open_corner(packed):
    full = jnp.concatenate([packed, pltpu.roll(packed, 64, 1)], axis=0)
    return jnp.where(iota((8, 128), 1) < SIDE, full, 0.0)


def pack_face(face):
    rest = jnp.concatenate([face[HEAD:], jnp.zeros((2 * HEAD - ROWS, 128), f32)], axis=0)
    head = jnp.where(iota((HEAD, 128), 1) < 72, face[:HEAD], pltpu.roll(rest, 72, 1))
    group = jnp.right_shift(iota((8, 128), 1), 4)
    tail = jnp.zeros((8, 128), f32)
    for g in range((ROWS - HEAD) // 8):
        rolled = pltpu.roll(rest[8 * g : 8 * g + 8], (16 * g - 56) % 128, 1)
        tail = jnp.where(group == g, rolled, tail)
    return jnp.concatenate([head, tail], axis=0)


def open_face(packed):
    tiles = [packed[r : r + 8] for r in range(0, HEAD, 8)]
    tail = packed[HEAD:]
    lane = iota((8, 128), 1)
    for g in range((ROWS - HEAD) // 8):
        body_part = pltpu.roll(packed[8 * g : 8 * g + 8], 56, 1)
        tiles.append(jnp.where(lane < 56, body_part, pltpu.roll(tail, (56 - 16 * g) % 128, 1)))
    return tiles


def pack_line(tile, start):
    group = jnp.right_shift(iota((8, 128), 1), 3)
    row = iota((8, 128), 0)
    total = jnp.zeros((8, 128), f32)
    for r in range(8):
        rolled = pltpu.roll(tile, (8 * r - start) % 128, 1)
        total = jnp.where((group == r) & (row == r), rolled, total)
    return jnp.sum(total, axis=0, keepdims=True)


def open_line(packed, start):
    wide = jnp.broadcast_to(packed, (8, 128))
    row = iota((8, 128), 0)
    total = pltpu.roll(wide, start, 1) if start else wide
    for r in range(1, 8):
        total = jnp.where(row == r, pltpu.roll(wide, (start - 8 * r) % 128, 1), total)
    return total


def turned(value):
    rows = jnp.zeros((128 - value.shape[0], 128), f32)
    return jnp.concatenate([value, rows], axis=0).T


def kernel(
    sizes,
    live_hbm,
    record_hbm,
    block_hbm,
    offset_hbm,
    plan_hbm,
    out_ref,
    live_ref,
    record_ref,
    block_ref,
    offset_ref,
    plan_ref,
    in_sems,
    high_ref,
    low_ref,
    gather_ref,
    spread_ref,
    corner_ref,
    some_high,
    some_low,
    grid_ref,
    z_send,
    z_recv,
    e_send,
    e_recv,
    x_recv,
    y_send,
    y_recv,
    c_send,
    c_recv,
    l_send,
    l_recv,
    leave_ref,
    m_send,
    come_ref,
    new_ref,
    z_sems,
    xy_sems,
    m_sems,
):
    operands = (
        (record_hbm, record_ref),
        (block_hbm, block_ref),
        (offset_hbm, offset_ref),
        (live_hbm, live_ref),
        (plan_hbm, plan_ref),
    )
    in_copies = [
        pltpu.make_async_copy(source, target, in_sems.at[slot])
        for slot, (source, target) in enumerate(operands)
    ]
    for copy in in_copies:
        copy.start()
    me = [lax.axis_index(name) for name in AXES]

    def at(*step):
        return tuple(
            lax.rem(me[a] + step[a] + sizes[a], sizes[a]) if step[a] else me[a] for a in range(3)
        )

    pair_z = sizes[2] == 2
    z_steps = ((0, 0, 1),) if pair_z else ((0, 0, 1), (0, 0, -1))
    xy_steps = tuple((i, j, 0) for i in (0, 1, -1) for j in (1, -1, 0) if i or j)
    barrier = pltpu.get_barrier_semaphore()
    around = xy_steps + tuple((i, j, k) for _, _, k in z_steps for i, j, _ in ((0, 0, 0),) + xy_steps)
    for step in around:
        pl.semaphore_signal(barrier, inc=1, device_id=at(*step), device_id_type=MESH)

    fill_masks(gather_ref, spread_ref, corner_ref)
    for copy in in_copies:
        copy.wait()
    count = record_ref.shape[1]
    record = record_ref[...]
    fraction = record[21:24]
    blocks = block_ref[...]
    offsets = offset_ref[...]
    anchor = (
        jnp.concatenate(
            [
                8 * jnp.right_shift(blocks, 2) + jnp.right_shift(offsets, 6),
                8 * (jnp.right_shift(blocks, 1) & 1) + (jnp.right_shift(offsets, 3) & 7),
                8 * (blocks & 1) + (offsets & 7),
            ],
            axis=0,
        )
        + 1
    ).astype(f32)
    living = jnp.where(iota((1, count), 1) < live_ref[0], 1.0, 0.0).astype(f32)

    tables = axis_tables(anchor, fraction)
    fill_tables(high_ref, low_ref, tables)

    plastic = pack(record[25:26])
    deform = [[pack(record[12 + 3 * i + j : 13 + 3 * i + j]) for j in range(3)] for i in range(3)]
    tau = stress(deform, plastic)
    mass = record[24:25]
    held = mass * living
    coupling = [
        [
            (mass * record[3 + 3 * i + j : 4 + 3 * i + j] - stress_gain * unpack(tau[i][j])) * living
            for j in range(3)
        ]
        for i in range(3)
    ]
    none = jnp.zeros((1, count), f32)
    places = anchor + fraction - CENTRE
    momentum = [
        held * record[i : i + 1] - coupling[i][1] * places[1:2] - coupling[i][2] * places[2:3]
        for i in range(3)
    ]
    base = jnp.concatenate([held] + momentum + [held] + momentum, axis=0)
    pushes = [
        jnp.concatenate([none, coupling[0][j], coupling[1][j], coupling[2][j]] * 2, axis=0)
        for j in range(3)
    ]
    weight_x, shift_x = tables[0]
    tiles = range(0, ROWS, 8)
    left = jnp.concatenate(
        [base * weight_x[r : r + 8] + pushes[0] * shift_x[r : r + 8] for r in tiles]
        + [pushes[1] * weight_x[r : r + 8] for r in tiles]
        + [pushes[2] * weight_x[r : r + 8] for r in tiles],
        axis=0,
    )

    def send(source, target, sems, slot, step):
        copy = pltpu.make_async_remote_copy(
            src_ref=source,
            dst_ref=target,
            send_sem=sems.at[0, slot],
            recv_sem=sems.at[1, slot],
            device_id=at(*step),
            device_id_type=MESH,
        )
        copy.start()
        return copy

    corners = ((1, 1), (1, -1), (-1, 1), (-1, -1))
    sides = ((0, 1), (0, -1), (1, 0), (-1, 0))
    last = {1: ROWS - 8, -1: 0}
    last_face = {1: 4 * (SPAN - 2), -1: 0}

    lane_y, lane_z = lane_places(LANES)
    cut = LANES - 128

    def outside(value, axis):
        low, high = lax.slice_in_dim(value, 0, 128, axis=axis), lax.slice_in_dim(value, cut, LANES, axis=axis)
        return jnp.concatenate([low, high], axis=axis)

    ends = combine(
        contract(
            dot_nt,
            left,
            *[jnp.concatenate([ref[0:128, :], ref[cut:, :]], axis=0) for ref in (high_ref, low_ref)],
        ),
        outside(lane_y, 1),
        outside(lane_z, 1),
    )
    ends = {-1: ends[:, :128], 1: ends[:, 128:]}
    y_send[0] = pack_side(ends[1])
    y_send[1] = pack_side(ends[-1])
    for number, (i, j) in enumerate(corners):
        c_send[number] = pack_corner(ends[j][last[i] : last[i] + 8])
    pl.semaphore_wait(barrier, len(around))
    xy_copies = []
    for number, j in enumerate((1, -1)):
        xy_copies.append(send(y_send.at[number], y_recv.at[number], xy_sems, number, (0, j, 0)))
    for number, (i, j) in enumerate(corners):
        xy_copies.append(send(c_send.at[number], c_recv.at[number], xy_sems, 2 + number, (i, j, 0)))

    both = jnp.where(iota((ROWS, 128), 1) < EDGE, ends[-1], pltpu.roll(ends[1], EDGE, 1))
    face = dot_nt(stacked(both), corner_ref[...])
    face = face[:ROWS] + face[ROWS:]
    e_send[0], e_send[1] = pack_edges(face)
    for number, (i, j) in enumerate(corners):
        l_send[number] = pack_line(face[last[i] : last[i] + 8], last_face[j])
    z_copies = []

    def send_edges(numbers):
        for slot, (_, _, k) in enumerate(z_steps):
            for number in numbers:
                i, j = sides[number]
                target = e_recv.at[slot, number]
                z_copies.append(
                    send(e_send.at[number], target, z_sems, 9 * slot + 1 + number, (i, j, k))
                )

    send_edges((0, 1))
    for slot, (_, _, k) in enumerate(z_steps):
        for number, (i, j) in enumerate(corners):
            target = l_recv.at[slot, number]
            z_copies.append(
                send(l_send.at[number], target, z_sems, 9 * slot + 5 + number, (i, j, k))
            )

    inside = combine(
        contract(dot_nt, left, high_ref[128:cut, :], low_ref[128:cut, :]),
        lane_y[:, 128:cut],
        lane_z[:, 128:cut],
    )
    partial = jnp.concatenate([ends[-1], inside, ends[1]], axis=1)
    grid_ref[...] = partial
    for number, i in enumerate((1, -1)):
        source = grid_ref.at[pl.ds(last[i], 8), :]
        xy_copies.append(send(source, x_recv.at[number], xy_sems, 6 + number, (i, 0, 0)))
    face = dot_nt(stacked(partial), gather_ref[...])
    face = face[:ROWS] + face[ROWS:]
    z_send[...] = pack_face(face)
    for slot, (_, _, k) in enumerate(z_steps):
        z_copies.append(send(z_send, z_recv.at[slot], z_sems, 9 * slot, (0, 0, k)))
    e_send[2] = face[last[1] : last[1] + 8]
    e_send[3] = face[last[-1] : last[-1] + 8]
    send_edges((2, 3))

    plan = plan_ref[...].astype(f32)
    cap = plan.shape[1]
    leaving = FACES * cap
    wide = jnp.concatenate(
        [jnp.broadcast_to(plan[q : q + 1], (cap, cap)) for q in range(FACES)], axis=0
    )
    diagonal = (iota((leaving, cap), 0) & (cap - 1)) == iota((leaving, cap), 1)
    chosen = jnp.sum(jnp.where(diagonal, wide, 0.0), axis=1, keepdims=True)
    picked = jnp.where(iota((leaving, count), 1).astype(f32) == chosen, 1.0, 0.0).astype(f32)
    taken = jnp.sum(picked, axis=0, keepdims=True)
    picker = jnp.concatenate([picked, jnp.zeros((128 - leaving, count), f32)], axis=0).astype(bf16)
    full = jnp.concatenate([record, anchor, living, jnp.zeros((2, count), f32)], axis=0)

    def pick(dot, value):
        got = dot(stacked(value), picker)
        return got[0:32] + got[32:64]

    some = pick(dot_nt, full)
    some_tables = axis_tables(some[26:29], some[21:24])
    fill_tables(some_high, some_low, some_tables)

    for copy in xy_copies:
        copy.wait_recv()
    partial = grid_ref[...]
    low_side = open_side(y_recv[0])
    high_side = open_side(y_recv[1])
    middle = jnp.zeros((8, LANES - 256), f32)
    corner = [open_corner(c_recv[number]) for number in range(4)]
    low_rows = x_recv[0] + jnp.concatenate([corner[0], middle, corner[1]], axis=1)
    high_rows = x_recv[1] + jnp.concatenate([corner[2], middle, corner[3]], axis=1)
    totals = jnp.concatenate(
        [
            partial[:, 0:128] + low_side,
            partial[:, 128 : LANES - 128],
            partial[:, LANES - 128 :] + high_side,
        ],
        axis=1,
    )
    totals = jnp.concatenate(
        [totals[0:8] + low_rows, totals[8 : ROWS - 8], totals[ROWS - 8 :] + high_rows], axis=0
    )
    for copy in z_copies:
        copy.wait_recv()

    def from_z(ref, *index):
        if pair_z:
            return ref[(0,) + index]
        value = ref[(1,) + index]
        return jnp.where((iota(value.shape, 1) & 3) < 2, value, ref[(0,) + index])

    face_lane = iota((8, 128), 1)
    face_side = {1: face_lane < 8, -1: (face_lane >= 4 * (SPAN - 2)) & (face_lane < 4 * SPAN)}
    face_start = {1: 0, -1: 4 * (SPAN - 2)}
    edge = {step: from_z(e_recv, number) for number, step in enumerate(sides)}
    shared = open_face(from_z(z_recv))
    for g in range(ROWS // 8):
        for j in (1, -1):
            rolled = pltpu.roll(edge[0, j], (face_start[j] - 8 * g) % 128, 1)
            shared[g] = jnp.where(face_side[j], shared[g] + rolled, shared[g])
    for i in (1, -1):
        g = 0 if i > 0 else ROWS // 8 - 1
        shared[g] = shared[g] + edge[i, 0]
        for j in (1, -1):
            line = open_line(from_z(l_recv, corners.index((i, j))), face_start[j])
            shared[g] = jnp.where(face_side[j], shared[g] + line, shared[g])
    spread_sum = dot_nn(stacked(jnp.concatenate(shared, axis=0)), spread_ref[...])
    totals = totals + spread_sum[:ROWS] + spread_sum[ROWS:]

    channel = iota((ROWS, LANES), 0) & 3
    mass_of = jnp.where(
        channel == 1,
        pltpu.roll(totals, 1, 0),
        jnp.where(channel == 2, pltpu.roll(totals, 2, 0), pltpu.roll(totals, 3, 0)),
    )
    velocity = totals / jnp.maximum(mass_of, mass_floor)
    velocity = jnp.where(channel == 3, velocity - time_step * gravity, velocity)
    velocity = jnp.where(channel == 0, 0.0, velocity)
    velocity = jnp.concatenate([velocity, velocity * lane_y, velocity * lane_z], axis=0)

    read_back(
        leave_ref, some, some[26:29], some[29:30], some_tables, some_high, some_low, velocity
    )
    m_send[...] = turned(leave_ref[...])[:leaving].reshape(FACES, cap, 128)
    m_steps = ((1, 0, 0), (-1, 0, 0), (0, 1, 0), (0, -1, 0), (0, 0, 1), (0, 0, -1))
    m_copies = [
        send(m_send.at[slot], come_ref.at[slot], m_sems, slot, step)
        for slot, step in sorted(enumerate(m_steps), key=lambda pair: pair[1][1] == 0)
    ]
    read_back(new_ref, record, anchor, living, tables, high_ref, low_ref, velocity)
    for copy in xy_copies + z_copies + m_copies:
        copy.wait_send()
    for copy in m_copies:
        copy.wait_recv()
    placed = pick(dot_nn, turned(come_ref[...].reshape(leaving, 128))[:32])
    out_ref[...] = jnp.where(taken > 0.0, placed, new_ref[...])[0:26]


def body(sizes, particles, block_ids, node_offsets, live_count, migrations):
    count = particles.shape[1]
    vmem = pl.BlockSpec(memory_space=pltpu.VMEM)
    return pl.pallas_call(
        functools.partial(kernel, sizes),
        out_shape=pltpu.VMEM(particles.shape, f32),
        in_specs=[pl.BlockSpec(memory_space=pltpu.HBM)] * 5,
        out_specs=vmem,
        scratch_shapes=[
            pltpu.SMEM((1,), jnp.int32),
            pltpu.VMEM(particles.shape, f32),
            pltpu.VMEM((1, count), jnp.int32),
            pltpu.VMEM((1, count), jnp.int32),
            pltpu.VMEM(migrations.shape, jnp.int32),
            pltpu.SemaphoreType.DMA((5,)),
            pltpu.VMEM((LANES, count), bf16),
            pltpu.VMEM((LANES, count), bf16),
            pltpu.VMEM((128, LANES), bf16),
            pltpu.VMEM((128, LANES), bf16),
            pltpu.VMEM((128, 128), bf16),
            pltpu.VMEM((LANES, 128), bf16),
            pltpu.VMEM((LANES, 128), bf16),
            pltpu.VMEM((ROWS, LANES), f32),
            pltpu.VMEM((FACE_ROWS, 128), f32),
            pltpu.VMEM((2, FACE_ROWS, 128), f32),
            pltpu.VMEM((4, 8, 128), f32),
            pltpu.VMEM((2, 4, 8, 128), f32),
            pltpu.VMEM((2, 8, LANES), f32),
            pltpu.VMEM((2, THIRD, 128), f32),
            pltpu.VMEM((2, THIRD, 128), f32),
            pltpu.VMEM((4, 4, 128), f32),
            pltpu.VMEM((4, 4, 128), f32),
            pltpu.VMEM((4, 1, 128), f32),
            pltpu.VMEM((2, 4, 1, 128), f32),
            pltpu.VMEM((32, 128), f32),
            pltpu.VMEM((FACES, migrations.shape[1], 128), f32),
            pltpu.VMEM((FACES, migrations.shape[1], 128), f32),
            pltpu.VMEM((32, count), f32),
            pltpu.SemaphoreType.DMA((2, 18)),
            pltpu.SemaphoreType.DMA((2, 8)),
            pltpu.SemaphoreType.DMA((2, 6)),
        ],
        compiler_params=pltpu.CompilerParams(
            collective_id=0, has_side_effects=True, vmem_limit_bytes=60 * 1024 * 1024
        ),
        name="substep",
    )(
        live_count,
        particles,
        block_ids.reshape(1, count),
        node_offsets.reshape(1, count),
        migrations,
    )


def solution(mesh):
    sizes = tuple(mesh.shape[name] for name in AXES)
    return jax.shard_map(
        functools.partial(body, sizes),
        mesh=mesh,
        in_specs=(
            P(None, AXES),
            P(AXES),
            P(AXES),
            P(AXES),
            P(None, AXES),
        ),
        out_specs=P(None, AXES),
        check_vma=False,
    )
```
